512 devices in a mesh: ctx: 32 (over x_lo, z, core), tp: 16 (over x_hi, y).
Axes of the slice: x: 4 (x_hi: 2, x_lo: 2; x = x_hi * 2 + x_lo), y: 8, z: 8, core: 2. Of those that a mesh axis runs over, the one named last changes fastest.
Arguments:
- signal: bfloat16 [256, 32768], P('tp', 'ctx'), may hold values from -6 to 6
- filter_taps: float32 [16, 32768], P(None, 'ctx'), may hold values from -6 to 6
- skip_gain: float32 [256], P('tp'), may hold values from 0.5 to 1.5
- grad_out: bfloat16 [256, 32768], P('tp', 'ctx'), may hold values from -6 to 6
Outputs:
- output: bfloat16 [256, 32768], P('tp', 'ctx')
- grad_signal: bfloat16 [256, 32768], P('tp', 'ctx')
- grad_filter: float32 [16, 32768], P(None, 'ctx')
The draws below stay inside these ranges and needn't reach their ends.
All inputs are finite; a program needn't handle non-finite values.
Results may differ from the reference program's by a relative error of at most 0.0012.
Values sent between devices are 32-bit elements; how exact they have to be, the bound alone decides.
No kernel may reach another device: no remote copies, remote signals or barrier semaphores. Data moves between devices by JAX's collectives and lax.ppermute only.
A program may use at most 64 MiB of HBM per device.

```python
import math
import jax
import jax.numpy as jnp

CH_DEV = 16
LENGTH = 32768
CHANNELS = 256
N_TP = 16


def shard_levels(stream_key, dims, split, least, high):
    loudness, own = 1.0, jax.random.fold_in(stream_key, 6)
    for axis_at, parts in split:
        steps = jnp.exp(jax.random.uniform(jax.random.fold_in(own, axis_at), (parts,), jnp.float32, least / len(split), high / len(split)))
        loudness = loudness * jnp.repeat(steps, dims[axis_at] // parts).reshape([-1 if axis == axis_at else 1 for axis in range(len(dims))])
    return loudness


def bell_draw(stream_key, shape, deviation, limit, shards=(), kind=jnp.bfloat16):
    array = jax.random.normal(stream_key, shape, jnp.float32) * deviation
    if len(shards) > 0:
        array = shard_levels(stream_key, shape, shards, -0.22, 0.18) * array
    return jnp.clip(array, min=-limit, max=limit).astype(kind)


def setup_inputs(seed: int = 0) -> dict:
    seeds = jax.random.split(jax.random.key(seed), 5)
    signal = bell_draw(seeds[0], (CHANNELS, LENGTH), 1.0, 6.0, ((0, 16), (1, 32)))
    filter_taps = bell_draw(seeds[1], (CH_DEV, LENGTH), 1.0, 6.0, ((1, 32),), jnp.float32)
    skip_gain = jnp.clip(0.5 + 1.0 * jax.random.uniform(seeds[2], (CHANNELS,), jnp.float32) ** shard_levels(seeds[2], (CHANNELS,), ((0, 16),), -0.2, 0.2), 0.5, 1.5)
    grad_out = bell_draw(seeds[3], (CHANNELS, LENGTH), 1.0, 6.0, ((0, 16), (1, 32)))
    return {"signal": signal, "filter_taps": filter_taps, "skip_gain": skip_gain, "grad_out": grad_out}


def reference(signal, filter_taps, skip_gain, grad_out):
    padded = 2 * LENGTH
    filter_scale = 1.0 / math.sqrt(LENGTH)
    values = signal.astype(jnp.float32)
    cotangent = grad_out.astype(jnp.float32)
    response = jnp.tile(filter_taps * filter_scale, (N_TP, 1))
    signal_spec = jnp.fft.rfft(values, n=padded, axis=1)
    grad_spec = jnp.fft.rfft(cotangent, n=padded, axis=1)
    filter_spec = jnp.fft.rfft(response, n=padded, axis=1)
    conv_out = jnp.fft.irfft(signal_spec * filter_spec, n=padded, axis=1)[:, :LENGTH]
    conv_back = jnp.fft.irfft(grad_spec * jnp.conj(filter_spec), n=padded, axis=1)[:, :LENGTH]
    conv_corr = jnp.fft.irfft(grad_spec * jnp.conj(signal_spec), n=padded, axis=1)[:, :LENGTH]
    output = (conv_out + skip_gain[:, None] * values).astype(jnp.bfloat16)
    grad_signal = (conv_back + skip_gain[:, None] * cotangent).astype(jnp.bfloat16)
    grad_filter = conv_corr.reshape(N_TP, CH_DEV, LENGTH).sum(axis=0) * filter_scale
    return (output, grad_signal, grad_filter)
```

```python
import functools
import math

import jax
import jax.numpy as jnp
import ml_dtypes
import numpy as np
from jax import lax
from jax.experimental import pallas as pl
from jax.experimental.pallas import tpu as pltpu
from jax.sharding import PartitionSpec as P

LANES = 128
SUBLANES = 8
VMEM_BYTES = 24 * 1024 * 1024


def split_table(table):
    high = table.astype(np.float32).astype(ml_dtypes.bfloat16)
    low = (table - high.astype(np.float64)).astype(ml_dtypes.bfloat16)
    return high, low


def make_tables(rows, scale):
    period = 2 * rows
    padded = period * LANES
    a = np.arange(rows)
    f1 = np.arange(rows)
    turn = 2.0 * np.pi * (np.outer(f1, a) % period) / period
    alternating = np.where(a % 2 == 0, 1.0, -1.0)
    cosines = np.cos(turn)
    sines = -np.sin(turn)
    sines[0] = alternating
    outer = np.concatenate([cosines, sines], axis=0)
    weights = np.full((rows,), 2.0)
    weights[0] = 1.0
    weights = np.concatenate([weights, weights])
    outer_back = (outer * weights[:, None]).T * (scale / padded)
    b = np.arange(LANES)
    kept = np.arange(rows + 1)
    angle = 2.0 * np.pi * (np.outer(kept, b) % padded) / padded
    twist = np.zeros((rows + 16, 2 * LANES))
    twist[: rows + 1, :LANES] = np.cos(angle)
    twist[: rows + 1, LANES:] = -np.sin(angle)
    inner = 2.0 * np.pi * (np.outer(b, b) % LANES) / LANES
    c, s = np.cos(inner), np.sin(inner)
    inner_there = np.block([[c, -s], [s, c]])
    inner_back = np.block([[c, s], [-s, c]])
    return (
        *split_table(outer),
        twist.astype(np.float32),
        *split_table(inner_there),
        *split_table(inner_back),
        *split_table(outer_back),
    )


def split(x):
    high = x.astype(jnp.bfloat16)
    low = (x - high.astype(jnp.float32)).astype(jnp.bfloat16)
    return high, low


def dot(x, y):
    return jnp.dot(x, y, preferred_element_type=jnp.float32)


def pack_kernel(signal_ref, grad_ref, filter_ref, out_ref):
    channels = signal_ref.shape[0]
    values = signal_ref[...].astype(jnp.float32)
    cotangent = grad_ref[...].astype(jnp.float32)
    taps = filter_ref[...]
    for core, order in enumerate(((values, cotangent, taps), (cotangent, values, taps))):
        for part, array in enumerate(order):
            for chunk in range(SUBLANES):
                start = core * 24 + part * 8 + chunk
                out_ref[pl.ds(start, channels, stride=48), :] = array[:, chunk * LANES : (chunk + 1) * LANES]


def convolve_kernel(
    sign_ref, in_ref, outer_h, outer_l, twist, there_h, there_l, back_h, back_l, outer_back_h, outer_back_l,
    out_ref, a_ref, u_h, u_l,
):
    blocks = in_ref.shape[0]
    rows = blocks * SUBLANES
    sign = sign_ref[0]

    def sequence(part):
        return in_ref[:, part * 8 : part * 8 + 8, :].reshape(rows, LANES)

    both = jnp.concatenate([sequence(0), sequence(1)], axis=1).astype(jnp.bfloat16)
    taps_h, taps_l = split(sequence(2))
    a_ref[:, : 2 * LANES] = dot(outer_h[...], both) + dot(outer_l[...], both)
    taps = dot(outer_h[...], jnp.concatenate([taps_h, taps_l], axis=1))
    a_ref[:, 2 * LANES :] = taps[:, :LANES] + taps[:, LANES:] + dot(outer_l[...], taps_h)

    last = a_ref[rows : rows + 1, :]
    first_row = lax.broadcasted_iota(jnp.int32, (16, 1), 0) == 0

    for start, count in ((0, rows // 2), (rows // 2, rows // 2), (rows, 16)):
        tr = twist[start : start + count, :LANES]
        ti = twist[start : start + count, LANES:]
        pieces = []
        for part in range(3):
            lanes = slice(part * LANES, (part + 1) * LANES)
            if start == rows:
                ar = jnp.where(first_row, last[:, lanes], 0.0)
                pieces.append(jnp.concatenate([ar * tr, ar * ti], axis=1))
                continue
            ar = a_ref[start : start + count, lanes]
            ai = a_ref[rows + start : rows + start + count, lanes]
            if start == 0:
                row = lax.broadcasted_iota(jnp.int32, (count, 1), 0)
                ai = jnp.where(row == 0, 0.0, ai)
            pieces.append(jnp.concatenate([ar * tr - ai * ti, ar * ti + ai * tr], axis=1))
        z_h, z_l = split(jnp.concatenate(pieces, axis=0))
        spec = dot(z_h, there_h[...]) + dot(z_l, there_h[...]) + dot(z_h, there_l[...])
        mr, mi = spec[:count, :LANES], spec[:count, LANES:]
        qr, qi = spec[count : 2 * count, :LANES], spec[count : 2 * count, LANES:]
        hr, hi = spec[2 * count :, :LANES], spec[2 * count :, LANES:] * sign
        conv = jnp.concatenate([mr * hr - mi * hi, mr * hi + mi * hr], axis=1)
        corr = jnp.concatenate([qr * mr + qi * mi, (qi * mr - qr * mi) * sign], axis=1)
        p_h, p_l = split(jnp.concatenate([conv, corr], axis=0))
        v = dot(p_h, back_h[...]) + dot(p_l, back_h[...]) + dot(p_h, back_l[...])
        for part in range(2):
            vr = v[part * count : (part + 1) * count, :LANES]
            vi = v[part * count : (part + 1) * count, LANES:]
            lanes = slice(part * LANES, (part + 1) * LANES)
            real_h, real_l = split(vr * tr + vi * ti)
            if start == rows:
                u_h[rows : rows + 16, lanes] = jnp.where(first_row, real_h, u_h[rows : rows + 16, lanes])
                u_l[rows : rows + 16, lanes] = jnp.where(first_row, real_l, u_l[rows : rows + 16, lanes])
                continue
            imag_h, imag_l = split(vi * tr - vr * ti)
            u_h[start : start + count, lanes] = real_h
            u_l[start : start + count, lanes] = real_l
            u_h[rows + start : rows + start + count, lanes] = imag_h
            u_l[rows + start : rows + start + count, lanes] = imag_l

    y = dot(outer_back_h[...], u_h[...]) + dot(outer_back_h[...], u_l[...]) + dot(outer_back_l[...], u_h[...])
    out_ref[:, :8, :] = y[:, :LANES].reshape(blocks, SUBLANES, LANES)
    out_ref[:, 8:, :] = y[:, LANES:].reshape(blocks, SUBLANES, LANES)


def collect_kernel(in_ref, corr_ref):
    channels = corr_ref.shape[0]
    for chunk in range(SUBLANES):
        corr_ref[:, chunk * LANES : (chunk + 1) * LANES] = in_ref[pl.ds(8 + chunk, channels, stride=32), :]


def finish_kernel(in_ref, gain_ref, signal_ref, grad_ref, out_ref, back_ref):
    channels = signal_ref.shape[0]
    gains = gain_ref[...]
    for chunk in range(SUBLANES):
        lanes = slice(chunk * LANES, (chunk + 1) * LANES)
        for core, (own, result) in enumerate(((signal_ref, out_ref), (grad_ref, back_ref))):
            conv = in_ref[pl.ds(core * 16 + chunk, channels, stride=32), :]
            result[:, lanes] = (conv + gains * own[:, lanes].astype(jnp.float32)).astype(jnp.bfloat16)


def call(kernel, out_shape, operands, scratch=(), smem=0):
    in_specs = [pl.BlockSpec(memory_space=pltpu.SMEM)] * smem
    in_specs += [pl.BlockSpec(memory_space=pltpu.VMEM)] * (len(operands) - smem)
    return pl.pallas_call(
        kernel,
        out_shape=out_shape,
        in_specs=in_specs,
        out_specs=jax.tree.map(lambda _: pl.BlockSpec(memory_space=pltpu.VMEM), out_shape),
        scratch_shapes=list(scratch),
        compiler_params=pltpu.CompilerParams(vmem_limit_bytes=VMEM_BYTES),
    )(*operands)


def on_device(signal, filter_taps, skip_gain, grad_out):
    channels, tokens = signal.shape
    ctx = lax.axis_size("ctx")
    tp = lax.axis_size("tp")
    length = tokens * ctx
    rows = length // LANES
    tables = make_tables(rows, 1.0 / math.sqrt(length))
    sign = (1 - 2 * (lax.axis_index("ctx") % 2)).astype(jnp.float32).reshape(1)

    packed = call(
        pack_kernel, jax.ShapeDtypeStruct((ctx * 24, LANES), jnp.float32), (signal, grad_out, filter_taps)
    )
    sequences = lax.all_to_all(packed.reshape(ctx, 24, LANES), "ctx", 0, 0, tiled=True)
    results = call(
        convolve_kernel,
        jax.ShapeDtypeStruct((ctx, 16, LANES), jnp.float32),
        (sign, sequences, *tables),
        scratch=(
            pltpu.VMEM((2 * rows, 3 * LANES), jnp.float32),
            pltpu.VMEM((2 * rows, 2 * LANES), jnp.bfloat16),
            pltpu.VMEM((2 * rows, 2 * LANES), jnp.bfloat16),
        ),
        smem=1,
    )
    returned = lax.all_to_all(results, "ctx", 0, 0, tiled=True).reshape(ctx * 16, LANES)
    corr = call(collect_kernel, jax.ShapeDtypeStruct((channels, tokens), jnp.float32), (returned,))
    everyone = jnp.broadcast_to(corr[None], (tp, channels, tokens))
    shares = lax.all_to_all(everyone, "tp", 0, 0, tiled=True)
    grad_filter = jnp.sum(shares, axis=0)
    output, grad_signal = call(
        finish_kernel,
        (
            jax.ShapeDtypeStruct((channels, tokens), jnp.bfloat16),
            jax.ShapeDtypeStruct((channels, tokens), jnp.bfloat16),
        ),
        (returned, skip_gain[:, None], signal, grad_out),
    )
    return (output, grad_signal, grad_filter)


def solution(mesh):
    in_specs = (P("tp", "ctx"), P(None, "ctx"), P("tp"), P("tp", "ctx"))
    out_specs = (P("tp", "ctx"), P("tp", "ctx"), P(None, "ctx"))
    return jax.shard_map(
        on_device, mesh=mesh, in_specs=in_specs, out_specs=out_specs, check_vma=False
    )
```

```python
import math

import jax
import jax.numpy as jnp
import ml_dtypes
import numpy as np
from jax import lax
from jax.experimental import pallas as pl
from jax.experimental.pallas import tpu as pltpu
from jax.sharding import Mesh
from jax.sharding import PartitionSpec as P

LANES = 128
SUBLANES = 8
CTX = ("chip", "core")
TP = ("tp_far", "tp_near")
VMEM_BYTES = 24 * 1024 * 1024


def split_table(table):
    high = table.astype(np.float32).astype(ml_dtypes.bfloat16)
    low = (table - high.astype(np.float64)).astype(ml_dtypes.bfloat16)
    return high, low


def make_tables(rows, blocks, scale):
    period = 2 * rows
    padded = period * LANES
    place = np.arange(rows)
    a = place % blocks * SUBLANES + place // blocks
    f1 = np.arange(rows)
    turn = 2.0 * np.pi * (np.outer(f1, a) % period) / period
    cosines = np.cos(turn)
    sines = -np.sin(turn)
    sines[0] = np.where(a % 2 == 0, 1.0, -1.0)
    outer = np.concatenate([cosines, sines], axis=0)
    weights = np.full((rows,), 2.0)
    weights[0] = 1.0
    outer_back = (outer * np.concatenate([weights, weights])[:, None]).T * (scale / padded)
    b = np.arange(LANES)
    kept = np.arange(rows + 1)
    angle = 2.0 * np.pi * (np.outer(kept, b) % padded) / padded
    twist = np.zeros((rows + 16, 2 * LANES))
    twist[: rows + 1, :LANES] = np.cos(angle)
    twist[: rows + 1, LANES:] = -np.sin(angle)
    inner = 2.0 * np.pi * (np.outer(b, b) % LANES) / LANES
    c, s = np.cos(inner), np.sin(inner)
    inner_there = np.block([[c, -s], [s, c]])
    inner_back = np.block([[c, s], [-s, c]])
    back_columns = np.concatenate(np.split(outer_back, 2 * rows // (2 * LANES), axis=1), axis=0)
    stacked = np.concatenate([outer, inner_there, inner_back, back_columns], axis=0)
    high, low = split_table(stacked)
    return np.stack([high, low]), twist.astype(np.float32)


def split(x):
    high = x.astype(jnp.bfloat16)
    low = (x - high.astype(jnp.float32)).astype(jnp.bfloat16)
    return high, low


def dot(x, y):
    return jnp.dot(x, y, preferred_element_type=jnp.float32)


def pack_kernel(
    signal_hbm, grad_hbm, filter_hbm, table_hbm, twist_hbm, out_ref, table_ref, twist_ref, signal_ref, grad_ref, filter_ref, sems
):
    pairs = (
        (signal_hbm, signal_ref),
        (grad_hbm, grad_ref),
        (filter_hbm, filter_ref),
        (table_hbm, table_ref),
        (twist_hbm, twist_ref),
    )
    copies = [pltpu.make_async_copy(source, target, sems.at[k]) for k, (source, target) in enumerate(pairs)]
    for copy in copies:
        copy.start()
    channels = signal_ref.shape[0]

    def put(core, w, chunk, array):
        out_ref[pl.ds(core * 12 + w, channels, stride=24), :] = array[:, chunk * LANES : (chunk + 1) * LANES]

    for core, ref in enumerate((signal_ref, grad_ref)):
        copies[core].wait()
        array = ref[...].astype(jnp.float32)
        for chunk in range(SUBLANES):
            put(core, chunk, chunk, array)
    copies[2].wait()
    taps = filter_ref[...]
    for chunk in range(SUBLANES):
        put(chunk // 4, 8 + chunk % 4, chunk, taps)
    for copy in copies[3:]:
        copy.wait()


def convolve_kernel(core_ref, in_ref, table, twist, out_ref, a_ref, u_h, u_l):
    blocks = in_ref.shape[0] // 24
    rows = blocks * SUBLANES
    on_second = core_ref[0] == 1
    sign = jnp.where(on_second, -1.0, 1.0)

    def part(number, start, count):
        return table[number, start : start + count, :]

    def chunk(core, w):
        return in_ref[pl.ds(core * blocks * 12 + w, blocks, stride=12), :]

    signal = jnp.concatenate([chunk(0, w) for w in range(8)], axis=0)
    grad = jnp.concatenate([chunk(1, w) for w in range(8)], axis=0)
    taps = jnp.concatenate([chunk(core, 8 + w) for core in range(2) for w in range(4)], axis=0)
    both = jnp.concatenate([signal, grad], axis=1).astype(jnp.bfloat16)
    taps_h, taps_l = split(taps)
    outer_h, outer_l = part(0, 0, 2 * rows), part(1, 0, 2 * rows)
    a_ref[:, : 2 * LANES] = dot(outer_h, both) + dot(outer_l, both)
    turned = dot(outer_h, jnp.concatenate([taps_h, taps_l], axis=1))
    a_ref[:, 2 * LANES :] = turned[:, :LANES] + turned[:, LANES:] + dot(outer_l, taps_h)
    at = 2 * rows
    there_h, there_l = part(0, at, 2 * LANES), part(1, at, 2 * LANES)
    at += 2 * LANES
    back_h, back_l = part(0, at, 2 * LANES), part(1, at, 2 * LANES)
    at += 2 * LANES

    last = a_ref[rows : rows + 1, :]
    first_row = lax.broadcasted_iota(jnp.int32, (16, 1), 0) == 0

    for start, count in ((0, rows // 2), (rows // 2, rows // 2), (rows, 16)):
        tr = twist[start : start + count, :LANES]
        ti = twist[start : start + count, LANES:]
        pieces = []
        for number in range(3):
            lanes = slice(number * LANES, (number + 1) * LANES)
            if start == rows:
                ar = jnp.where(first_row, last[:, lanes], 0.0)
                pieces.append(jnp.concatenate([ar * tr, ar * ti], axis=1))
                continue
            ar = a_ref[start : start + count, lanes]
            ai = a_ref[rows + start : rows + start + count, lanes]
            if start == 0:
                row = lax.broadcasted_iota(jnp.int32, (count, 1), 0)
                ai = jnp.where(row == 0, 0.0, ai)
            pieces.append(jnp.concatenate([ar * tr - ai * ti, ar * ti + ai * tr], axis=1))
        z_h, z_l = split(jnp.concatenate(pieces, axis=0))
        spec = dot(z_h, there_h) + dot(z_l, there_h) + dot(z_h, there_l)
        sr, si = spec[:count, :LANES], spec[:count, LANES:]
        gr, gi = spec[count : 2 * count, :LANES], spec[count : 2 * count, LANES:]
        hr, hi = spec[2 * count :, :LANES], spec[2 * count :, LANES:] * sign
        mr, mi = jnp.where(on_second, gr, sr), jnp.where(on_second, gi, si)
        conv = jnp.concatenate([mr * hr - mi * hi, mr * hi + mi * hr], axis=1)
        corr = jnp.concatenate([gr * sr + gi * si, gi * sr - gr * si], axis=1)
        p_h, p_l = split(jnp.concatenate([conv, corr], axis=0))
        v = dot(p_h, back_h) + dot(p_l, back_h) + dot(p_h, back_l)
        for number in range(2):
            vr = v[number * count : (number + 1) * count, :LANES]
            vi = v[number * count : (number + 1) * count, LANES:]
            lanes = slice(number * LANES, (number + 1) * LANES)
            real_h, real_l = split(vr * tr + vi * ti)
            if start == rows:
                u_h[rows : rows + 16, lanes] = jnp.where(first_row, real_h, u_h[rows : rows + 16, lanes])
                u_l[rows : rows + 16, lanes] = jnp.where(first_row, real_l, u_l[rows : rows + 16, lanes])
                continue
            imag_h, imag_l = split(vi * tr - vr * ti)
            u_h[start : start + count, lanes] = real_h
            u_l[start : start + count, lanes] = real_l
            u_h[rows + start : rows + start + count, lanes] = imag_h
            u_l[rows + start : rows + start + count, lanes] = imag_l

    y = jnp.zeros((rows, 2 * LANES), jnp.float32)
    for inner in range(0, 2 * rows, 2 * LANES):
        here = slice(inner, inner + 2 * LANES)
        columns_h, columns_l = part(0, at, rows), part(1, at, rows)
        y += dot(columns_h, u_h[here, :]) + dot(columns_h, u_l[here, :]) + dot(columns_l, u_h[here, :])
        at += rows
    half = rows // 2
    corr = jnp.where(on_second, y[half:, LANES:], y[:half, LANES:])
    for w in range(8):
        out_ref[pl.ds(w, blocks, stride=12), :] = y[w * blocks : (w + 1) * blocks, :LANES]
    for w in range(4):
        out_ref[pl.ds(8 + w, blocks, stride=12), :] = corr[w * blocks : (w + 1) * blocks]


def collect_kernel(in_ref, corr_ref):
    channels = corr_ref.shape[0]
    for chunk in range(SUBLANES):
        start = chunk // 4 * 12 + 8 + chunk % 4
        corr_ref[:, chunk * LANES : (chunk + 1) * LANES] = in_ref[pl.ds(start, channels, stride=24), :]


def add_kernel(in_ref, out_ref):
    total = in_ref[0] + in_ref[1]
    for place in range(out_ref.shape[0]):
        out_ref[place] = total


def finish_kernel(in_ref, gain_ref, signal_ref, grad_ref, out_ref, back_ref):
    channels = signal_ref.shape[0]
    gains = gain_ref[...]
    for chunk in range(SUBLANES):
        lanes = slice(chunk * LANES, (chunk + 1) * LANES)
        for core, (own, result) in enumerate(((signal_ref, out_ref), (grad_ref, back_ref))):
            conv = in_ref[pl.ds(core * 12 + chunk, channels, stride=24), :]
            result[:, lanes] = (conv + gains * own[:, lanes].astype(jnp.float32)).astype(jnp.bfloat16)


def call(kernel, out_shape, operands, scratch=(), spaces=None):
    if spaces is None:
        spaces = [pltpu.VMEM] * len(operands)
    return pl.pallas_call(
        kernel,
        out_shape=out_shape,
        in_specs=[pl.BlockSpec(memory_space=space) for space in spaces],
        out_specs=jax.tree.map(lambda _: pl.BlockSpec(memory_space=pltpu.VMEM), out_shape),
        scratch_shapes=list(scratch),
        compiler_params=pltpu.CompilerParams(vmem_limit_bytes=VMEM_BYTES),
    )(*operands)


def on_device(signal, filter_taps, skip_gain, grad_out):
    channels, tokens = signal.shape
    ctx = lax.axis_size(CTX)
    length = tokens * ctx
    rows = length // LANES
    table, twist = make_tables(rows, ctx, 1.0 / math.sqrt(length))
    core = lax.axis_index("core").astype(jnp.int32).reshape(1)

    in_hbm = [pltpu.with_memory_space_constraint(x, pltpu.HBM) for x in (signal, grad_out, filter_taps, table, twist)]
    packed, table, twist = call(
        pack_kernel,
        (
            pltpu.VMEM((ctx * 12, LANES), jnp.float32),
            pltpu.VMEM(table.shape, table.dtype),
            pltpu.VMEM(twist.shape, twist.dtype),
        ),
        in_hbm,
        scratch=(
            pltpu.VMEM(signal.shape, signal.dtype),
            pltpu.VMEM(grad_out.shape, grad_out.dtype),
            pltpu.VMEM(filter_taps.shape, filter_taps.dtype),
            pltpu.SemaphoreType.DMA((5,)),
        ),
        spaces=[pltpu.HBM] * 5,
    )
    spread = lax.all_to_all(packed.reshape(ctx * 3, 4, LANES), CTX, 0, 0, tiled=True)
    sequences = lax.all_gather(spread, "core", tiled=True).reshape(ctx * 24, LANES)
    results = call(
        convolve_kernel,
        jax.ShapeDtypeStruct((ctx * 12, LANES), jnp.float32),
        (core, sequences, table, twist),
        scratch=(
            pltpu.VMEM((2 * rows, 3 * LANES), jnp.float32),
            pltpu.VMEM((2 * rows, 2 * LANES), jnp.bfloat16),
            pltpu.VMEM((2 * rows, 2 * LANES), jnp.bfloat16),
        ),
        spaces=[pltpu.SMEM] + [pltpu.VMEM] * 3,
    )
    returned = lax.all_to_all(results.reshape(ctx * 3, 4, LANES), CTX, 0, 0, tiled=True)
    returned = returned.reshape(ctx * 12, LANES)
    corr = call(collect_kernel, jax.ShapeDtypeStruct((channels, tokens), jnp.float32), (returned,))
    pair = lax.all_gather(corr, "tp_far")
    near = lax.axis_size("tp_near")
    everyone = call(add_kernel, jax.ShapeDtypeStruct((near, channels, tokens), jnp.float32), (pair,))
    shares = lax.all_to_all(everyone, "tp_near", 0, 0, tiled=True)
    grad_filter = jnp.sum(shares, axis=0)
    output, grad_signal = call(
        finish_kernel,
        (
            jax.ShapeDtypeStruct((channels, tokens), jnp.bfloat16),
            jax.ShapeDtypeStruct((channels, tokens), jnp.bfloat16),
        ),
        (returned, skip_gain[:, None], signal, grad_out),
    )
    return (output, grad_signal, grad_filter)


def solution(mesh):
    ctx, tp = mesh.shape["ctx"], mesh.shape["tp"]
    far = 2 if tp % 2 == 0 else 1
    parted = Mesh(mesh.devices.reshape(ctx // 2, 2, far, tp // far), ("chip", "core", "tp_far", "tp_near"))
    in_specs = (P(TP, CTX), P(None, CTX), P(TP), P(TP, CTX))
    out_specs = (P(TP, CTX), P(TP, CTX), P(None, CTX))
    return jax.shard_map(
        on_device, mesh=parted, in_specs=in_specs, out_specs=out_specs, check_vma=False
    )
```

```python
import math

import jax
import jax.numpy as jnp
import ml_dtypes
import numpy as np
from jax import lax
from jax.experimental import pallas as pl
from jax.experimental.pallas import tpu as pltpu
from jax.sharding import Mesh
from jax.sharding import PartitionSpec as P

LANES = 128
SUBLANES = 8
CTX = ("chip", "core")
TP = ("tp_far", "tp_near")
VMEM_BYTES = 24 * 1024 * 1024


def split_table(table):
    high = table.astype(np.float32).astype(ml_dtypes.bfloat16)
    low = (table - high.astype(np.float64)).astype(ml_dtypes.bfloat16)
    return high, low


def make_tables(rows, blocks, scale):
    period = 2 * rows
    padded = period * LANES
    place = np.arange(rows)
    a = place % blocks * SUBLANES + place // blocks
    f1 = np.arange(rows)
    turn = 2.0 * np.pi * (np.outer(f1, a) % period) / period
    cosines = np.cos(turn)
    sines = -np.sin(turn)
    sines[0] = np.where(a % 2 == 0, 1.0, -1.0)
    outer = np.concatenate([cosines, sines], axis=0)
    weights = np.full((rows,), 2.0)
    weights[0] = 1.0
    outer_back = (outer * np.concatenate([weights, weights])[:, None]).T * (scale / padded)
    b = np.arange(LANES)
    kept = np.arange(rows + 1)
    angle = 2.0 * np.pi * (np.outer(kept, b) % padded) / padded
    twist = np.zeros((rows + 16, 2 * LANES))
    twist[: rows + 1, :LANES] = np.cos(angle)
    twist[: rows + 1, LANES:] = -np.sin(angle)
    inner = 2.0 * np.pi * (np.outer(b, b) % LANES) / LANES
    c, s = np.cos(inner), np.sin(inner)
    inner_there = np.block([[c, -s], [s, c]])
    inner_back = np.block([[c, s], [-s, c]])
    back_columns = np.concatenate(np.split(outer_back, 2 * rows // (2 * LANES), axis=1), axis=0)
    stacked = np.concatenate([outer, inner_there, inner_back, back_columns], axis=0)
    high, low = split_table(stacked)
    return np.stack([high, low]), twist.astype(np.float32)


def split(x):
    high = x.astype(jnp.bfloat16)
    low = (x - high.astype(jnp.float32)).astype(jnp.bfloat16)
    return high, low


def dot(x, y):
    return jnp.dot(x, y, preferred_element_type=jnp.float32)


def pack_kernel(
    signal_hbm, grad_hbm, filter_hbm, table_hbm, twist_hbm, out_ref, table_ref, twist_ref, signal_ref, grad_ref, filter_ref, sems
):
    pairs = (
        (signal_hbm, signal_ref),
        (grad_hbm, grad_ref),
        (filter_hbm, filter_ref),
        (table_hbm, table_ref),
        (twist_hbm, twist_ref),
    )
    copies = [pltpu.make_async_copy(source, target, sems.at[k]) for k, (source, target) in enumerate(pairs)]
    for copy in copies:
        copy.start()
    channels = signal_ref.shape[0]

    def put(core, w, chunk, array):
        out_ref[pl.ds(core * 12 + w, channels, stride=24), :] = array[:, chunk * LANES : (chunk + 1) * LANES]

    for core, ref in enumerate((signal_ref, grad_ref)):
        copies[core].wait()
        array = ref[...].astype(jnp.float32)
        for chunk in range(SUBLANES):
            put(core, chunk, chunk, array)
    copies[2].wait()
    taps = filter_ref[...]
    for chunk in range(SUBLANES):
        put(chunk // 4, 8 + chunk % 4, chunk, taps)
    for copy in copies[3:]:
        copy.wait()


def convolve_kernel(core_ref, in_ref, table, twist, out_ref, a_ref, u_h, u_l):
    blocks = in_ref.shape[0] // 24
    rows = blocks * SUBLANES
    on_second = core_ref[0] == 1
    sign = jnp.where(on_second, -1.0, 1.0)

    def part(number, start, count):
        return table[number, start : start + count, :]

    def chunk(core, w):
        return in_ref[pl.ds(core * blocks * 12 + w, blocks, stride=12), :]

    signal = jnp.concatenate([chunk(0, w) for w in range(8)], axis=0)
    grad = jnp.concatenate([chunk(1, w) for w in range(8)], axis=0)
    taps = jnp.concatenate([chunk(core, 8 + w) for core in range(2) for w in range(4)], axis=0)
    both = jnp.concatenate([signal, grad], axis=1).astype(jnp.bfloat16)
    taps_h, taps_l = split(taps)
    outer_h, outer_l = part(0, 0, 2 * rows), part(1, 0, 2 * rows)
    a_ref[:, : 2 * LANES] = dot(outer_h, both) + dot(outer_l, both)
    turned = dot(outer_h, jnp.concatenate([taps_h, taps_l], axis=1))
    a_ref[:, 2 * LANES :] = turned[:, :LANES] + turned[:, LANES:] + dot(outer_l, taps_h)
    at = 2 * rows
    there_h, there_l = part(0, at, 2 * LANES), part(1, at, 2 * LANES)
    at += 2 * LANES
    back_h, back_l = part(0, at, 2 * LANES), part(1, at, 2 * LANES)
    at += 2 * LANES

    last = a_ref[rows : rows + 1, :]
    first_row = lax.broadcasted_iota(jnp.int32, (16, 1), 0) == 0

    for start, count in ((0, rows // 2), (rows // 2, rows // 2), (rows, 16)):
        tr = twist[start : start + count, :LANES]
        ti = twist[start : start + count, LANES:]
        pieces = []
        for number in range(3):
            lanes = slice(number * LANES, (number + 1) * LANES)
            if start == rows:
                ar = jnp.where(first_row, last[:, lanes], 0.0)
                pieces.append(jnp.concatenate([ar * tr, ar * ti], axis=1))
                continue
            ar = a_ref[start : start + count, lanes]
            ai = a_ref[rows + start : rows + start + count, lanes]
            if start == 0:
                row = lax.broadcasted_iota(jnp.int32, (count, 1), 0)
                ai = jnp.where(row == 0, 0.0, ai)
            pieces.append(jnp.concatenate([ar * tr - ai * ti, ar * ti + ai * tr], axis=1))
        z_h, z_l = split(jnp.concatenate(pieces, axis=0))
        spec = dot(z_h, there_h) + dot(z_l, there_h) + dot(z_h, there_l)
        sr, si = spec[:count, :LANES], spec[:count, LANES:]
        gr, gi = spec[count : 2 * count, :LANES], spec[count : 2 * count, LANES:]
        hr, hi = spec[2 * count :, :LANES], spec[2 * count :, LANES:] * sign
        mr, mi = jnp.where(on_second, gr, sr), jnp.where(on_second, gi, si)
        conv = jnp.concatenate([mr * hr - mi * hi, mr * hi + mi * hr], axis=1)
        corr = jnp.concatenate([gr * sr + gi * si, gi * sr - gr * si], axis=1)
        p_h, p_l = split(jnp.concatenate([conv, corr], axis=0))
        v = dot(p_h, back_h) + dot(p_l, back_h) + dot(p_h, back_l)
        for number in range(2):
            vr = v[number * count : (number + 1) * count, :LANES]
            vi = v[number * count : (number + 1) * count, LANES:]
            lanes = slice(number * LANES, (number + 1) * LANES)
            real_h, real_l = split(vr * tr + vi * ti)
            if start == rows:
                u_h[rows : rows + 16, lanes] = jnp.where(first_row, real_h, u_h[rows : rows + 16, lanes])
                u_l[rows : rows + 16, lanes] = jnp.where(first_row, real_l, u_l[rows : rows + 16, lanes])
                continue
            imag_h, imag_l = split(vi * tr - vr * ti)
            u_h[start : start + count, lanes] = real_h
            u_l[start : start + count, lanes] = real_l
            u_h[rows + start : rows + start + count, lanes] = imag_h
            u_l[rows + start : rows + start + count, lanes] = imag_l

    y = jnp.zeros((rows, 2 * LANES), jnp.float32)
    for inner in range(0, 2 * rows, 2 * LANES):
        here = slice(inner, inner + 2 * LANES)
        columns_h, columns_l = part(0, at, rows), part(1, at, rows)
        y += dot(columns_h, u_h[here, :]) + dot(columns_h, u_l[here, :]) + dot(columns_l, u_h[here, :])
        at += rows
    half = rows // 2
    corr = jnp.where(on_second, y[half:, LANES:], y[:half, LANES:])
    for w in range(8):
        out_ref[pl.ds(w, blocks, stride=12), :] = y[w * blocks : (w + 1) * blocks, :LANES]
    for w in range(4):
        out_ref[pl.ds(8 + w, blocks, stride=12), :] = corr[w * blocks : (w + 1) * blocks]


def collect_kernel(in_ref, corr_ref):
    channels = corr_ref.shape[0]
    for chunk in range(SUBLANES):
        start = chunk // 4 * 12 + 8 + chunk % 4
        corr_ref[:, chunk * LANES : (chunk + 1) * LANES] = in_ref[pl.ds(start, channels, stride=24), :]


def finish_kernel(pair_ref, in_ref, gain_ref, signal_ref, grad_ref, everyone_ref, out_ref, back_ref):
    total = pair_ref[0]
    for place in range(1, pair_ref.shape[0]):
        total += pair_ref[place]
    for place in range(everyone_ref.shape[0]):
        everyone_ref[place] = total
    channels = signal_ref.shape[0]
    gains = gain_ref[...]
    for chunk in range(SUBLANES):
        lanes = slice(chunk * LANES, (chunk + 1) * LANES)
        for core, (own, result) in enumerate(((signal_ref, out_ref), (grad_ref, back_ref))):
            conv = in_ref[pl.ds(core * 12 + chunk, channels, stride=24), :]
            result[:, lanes] = (conv + gains * own[:, lanes].astype(jnp.float32)).astype(jnp.bfloat16)


def call(kernel, out_shape, operands, scratch=(), spaces=None):
    if spaces is None:
        spaces = [pltpu.VMEM] * len(operands)
    return pl.pallas_call(
        kernel,
        out_shape=out_shape,
        in_specs=[pl.BlockSpec(memory_space=space) for space in spaces],
        out_specs=jax.tree.map(lambda _: pl.BlockSpec(memory_space=pltpu.VMEM), out_shape),
        scratch_shapes=list(scratch),
        compiler_params=pltpu.CompilerParams(vmem_limit_bytes=VMEM_BYTES),
    )(*operands)


def on_device(signal, filter_taps, skip_gain, grad_out):
    channels, tokens = signal.shape
    ctx = lax.axis_size(CTX)
    length = tokens * ctx
    rows = length // LANES
    table, twist = make_tables(rows, ctx, 1.0 / math.sqrt(length))
    core = lax.axis_index("core").astype(jnp.int32).reshape(1)

    in_hbm = [pltpu.with_memory_space_constraint(x, pltpu.HBM) for x in (signal, grad_out, filter_taps, table, twist)]
    packed, table, twist = call(
        pack_kernel,
        (
            pltpu.VMEM((ctx * 12, LANES), jnp.float32),
            pltpu.VMEM(table.shape, table.dtype),
            pltpu.VMEM(twist.shape, twist.dtype),
        ),
        in_hbm,
        scratch=(
            pltpu.VMEM(signal.shape, signal.dtype),
            pltpu.VMEM(grad_out.shape, grad_out.dtype),
            pltpu.VMEM(filter_taps.shape, filter_taps.dtype),
            pltpu.SemaphoreType.DMA((5,)),
        ),
        spaces=[pltpu.HBM] * 5,
    )
    spread = lax.all_to_all(packed.reshape(ctx * 3, 4, LANES), CTX, 0, 0, tiled=True)
    sequences = lax.all_gather(spread, "core", tiled=True).reshape(ctx * 24, LANES)
    results = call(
        convolve_kernel,
        jax.ShapeDtypeStruct((ctx * 12, LANES), jnp.float32),
        (core, sequences, table, twist),
        scratch=(
            pltpu.VMEM((2 * rows, 3 * LANES), jnp.float32),
            pltpu.VMEM((2 * rows, 2 * LANES), jnp.bfloat16),
            pltpu.VMEM((2 * rows, 2 * LANES), jnp.bfloat16),
        ),
        spaces=[pltpu.SMEM] + [pltpu.VMEM] * 3,
    )
    returned = lax.all_to_all(results.reshape(ctx * 3, 4, LANES), CTX, 0, 0, tiled=True)
    returned = returned.reshape(ctx * 12, LANES)
    corr = call(collect_kernel, jax.ShapeDtypeStruct((channels, tokens), jnp.float32), (returned,))
    pair = lax.all_gather(corr, "tp_far")
    near = lax.axis_size("tp_near")
    everyone, output, grad_signal = call(
        finish_kernel,
        (
            jax.ShapeDtypeStruct((near, channels, tokens), jnp.float32),
            jax.ShapeDtypeStruct((channels, tokens), jnp.bfloat16),
            jax.ShapeDtypeStruct((channels, tokens), jnp.bfloat16),
        ),
        (pair, returned, skip_gain[:, None], signal, grad_out),
    )
    shares = lax.all_to_all(everyone, "tp_near", 0, 0, tiled=True)
    grad_filter = jnp.sum(shares, axis=0)
    return (output, grad_signal, grad_filter)


def solution(mesh):
    ctx, tp = mesh.shape["ctx"], mesh.shape["tp"]
    far = 2 if tp % 2 == 0 else 1
    parted = Mesh(mesh.devices.reshape(ctx // 2, 2, far, tp // far), ("chip", "core", "tp_far", "tp_near"))
    in_specs = (P(TP, CTX), P(None, CTX), P(TP), P(TP, CTX))
    out_specs = (P(TP, CTX), P(TP, CTX), P(None, CTX))
    return jax.shard_map(
        on_device, mesh=parted, in_specs=in_specs, out_specs=out_specs, check_vma=False
    )
```

```python
import math

import jax
import jax.numpy as jnp
import ml_dtypes
import numpy as np
from jax import lax
from jax.experimental import pallas as pl
from jax.experimental.pallas import tpu as pltpu
from jax.sharding import Mesh
from jax.sharding import PartitionSpec as P

LANES = 128
SUBLANES = 8
CTX = ("chip", "core")
TP = ("tp_far", "tp_near")
VMEM_BYTES = 24 * 1024 * 1024


def split_table(table):
    high = table.astype(np.float32).astype(ml_dtypes.bfloat16)
    low = (table - high.astype(np.float64)).astype(ml_dtypes.bfloat16)
    return high, low


def make_tables(rows, blocks, scale):
    period = 2 * rows
    padded = period * LANES
    place = np.arange(rows)
    block = place // SUBLANES % (blocks // 2) * 2 + place // (rows // 2)
    a = block * SUBLANES + place % SUBLANES
    f1 = np.arange(rows)
    turn = 2.0 * np.pi * (np.outer(f1, a) % period) / period
    cosines = np.cos(turn)
    sines = -np.sin(turn)
    sines[0] = np.where(a % 2 == 0, 1.0, -1.0)
    outer = np.concatenate([cosines, sines], axis=0)
    weights = np.full((rows,), 2.0)
    weights[0] = 1.0
    outer_back = (outer * np.concatenate([weights, weights])[:, None]).T * (scale / padded)
    b = np.arange(LANES)
    kept = np.arange(rows + 1)
    angle = 2.0 * np.pi * (np.outer(kept, b) % padded) / padded
    twist = np.zeros((rows + 16, 2 * LANES))
    twist[: rows + 1, :LANES] = np.cos(angle)
    twist[: rows + 1, LANES:] = -np.sin(angle)
    inner = 2.0 * np.pi * (np.outer(b, b) % LANES) / LANES
    c, s = np.cos(inner), np.sin(inner)
    inner_there = np.block([[c, -s], [s, c]])
    inner_back = np.block([[c, s], [-s, c]])
    back_columns = np.concatenate(np.split(outer_back, 2 * rows // (2 * LANES), axis=1), axis=0)
    stacked = np.concatenate([outer, inner_there, inner_back, back_columns], axis=0)
    high, low = split_table(stacked)
    return np.stack([high, low]), twist.astype(np.float32)


def split(x):
    high = x.astype(jnp.bfloat16)
    low = (x - high.astype(jnp.float32)).astype(jnp.bfloat16)
    return high, low


def dot(x, y):
    return jnp.dot(x, y, preferred_element_type=jnp.float32)


def pack_kernel(
    signal_hbm, grad_hbm, filter_hbm, table_hbm, twist_hbm, out_ref, table_ref, twist_ref, signal_ref, grad_ref, filter_ref, sems
):
    pairs = (
        (signal_hbm, signal_ref),
        (grad_hbm, grad_ref),
        (filter_hbm, filter_ref),
        (table_hbm, table_ref),
        (twist_hbm, twist_ref),
    )
    copies = [pltpu.make_async_copy(source, target, sems.at[k]) for k, (source, target) in enumerate(pairs)]
    for copy in copies:
        copy.start()
    channels = signal_ref.shape[0]
    for number, ref in enumerate((signal_ref, grad_ref, filter_ref)):
        copies[number].wait()
        array = ref[...].astype(jnp.float32)
        for chunk in range(SUBLANES):
            out_ref[pl.ds(number * 8 + chunk, channels, stride=24), :] = array[:, chunk * LANES : (chunk + 1) * LANES]
    for copy in copies[3:]:
        copy.wait()


def convolve_kernel(core_ref, in_ref, table, twist, out_ref, a_ref, u_h, u_l):
    chips = out_ref.shape[0]
    half = chips * SUBLANES
    rows = 2 * half
    core = core_ref[0]

    def part(number, start, count):
        return table[number, start : start + count, :]

    def sequence(number):
        return in_ref[:, number * 8 : number * 8 + 8, :].reshape(rows, LANES)

    both = jnp.concatenate([sequence(0), sequence(1)], axis=1).astype(jnp.bfloat16)
    taps_h, taps_l = split(sequence(2))
    outer_h, outer_l = part(0, 0, 2 * rows), part(1, 0, 2 * rows)
    a_ref[:, : 2 * LANES] = dot(outer_h, both) + dot(outer_l, both)
    turned = dot(outer_h, jnp.concatenate([taps_h, taps_l], axis=1))
    a_ref[:, 2 * LANES :] = turned[:, :LANES] + turned[:, LANES:] + dot(outer_l, taps_h)
    at = 2 * rows
    there_h, there_l = part(0, at, 2 * LANES), part(1, at, 2 * LANES)
    at += 2 * LANES
    back_h, back_l = part(0, at, 2 * LANES), part(1, at, 2 * LANES)
    at += 2 * LANES

    last = a_ref[rows : rows + 1, :]
    first_row = lax.broadcasted_iota(jnp.int32, (16, 1), 0) == 0

    for start, count in ((0, rows // 2), (rows // 2, rows // 2), (rows, 16)):
        tr = twist[start : start + count, :LANES]
        ti = twist[start : start + count, LANES:]
        pieces = []
        for number in range(3):
            lanes = slice(number * LANES, (number + 1) * LANES)
            if start == rows:
                ar = jnp.where(first_row, last[:, lanes], 0.0)
                pieces.append(jnp.concatenate([ar * tr, ar * ti], axis=1))
                continue
            ar = a_ref[start : start + count, lanes]
            ai = a_ref[rows + start : rows + start + count, lanes]
            if start == 0:
                row = lax.broadcasted_iota(jnp.int32, (count, 1), 0)
                ai = jnp.where(row == 0, 0.0, ai)
            pieces.append(jnp.concatenate([ar * tr - ai * ti, ar * ti + ai * tr], axis=1))
        z_h, z_l = split(jnp.concatenate(pieces, axis=0))
        spec = dot(z_h, there_h) + dot(z_l, there_h) + dot(z_h, there_l)
        sr, si = spec[:count, :LANES], spec[:count, LANES:]
        gr, gi = spec[count : 2 * count, :LANES], spec[count : 2 * count, LANES:]
        hr, hi = spec[2 * count :, :LANES], spec[2 * count :, LANES:]
        conv = jnp.concatenate([sr * hr - si * hi, sr * hi + si * hr], axis=1)
        back = jnp.concatenate([gr * hr + gi * hi, gi * hr - gr * hi], axis=1)
        corr = jnp.concatenate([gr * sr + gi * si, gi * sr - gr * si], axis=1)
        p_h, p_l = split(jnp.concatenate([conv, back, corr], axis=0))
        v = dot(p_h, back_h) + dot(p_l, back_h) + dot(p_h, back_l)
        for number in range(3):
            vr = v[number * count : (number + 1) * count, :LANES]
            vi = v[number * count : (number + 1) * count, LANES:]
            lanes = slice(number * LANES, (number + 1) * LANES)
            real_h, real_l = split(vr * tr + vi * ti)
            if start == rows:
                u_h[rows : rows + 16, lanes] = jnp.where(first_row, real_h, u_h[rows : rows + 16, lanes])
                u_l[rows : rows + 16, lanes] = jnp.where(first_row, real_l, u_l[rows : rows + 16, lanes])
                continue
            imag_h, imag_l = split(vi * tr - vr * ti)
            u_h[start : start + count, lanes] = real_h
            u_l[start : start + count, lanes] = real_l
            u_h[rows + start : rows + start + count, lanes] = imag_h
            u_l[rows + start : rows + start + count, lanes] = imag_l

    y = jnp.zeros((half, 3 * LANES), jnp.float32)
    for inner in range(0, 2 * rows, 2 * LANES):
        here = slice(inner, inner + 2 * LANES)
        mine = pl.ds(pl.multiple_of(at + core * half, half), half)
        columns_h, columns_l = table[0, mine, :], table[1, mine, :]
        y += dot(columns_h, u_h[here, :]) + dot(columns_h, u_l[here, :]) + dot(columns_l, u_h[here, :])
        at += rows
    for number in range(3):
        out_ref[:, number * 8 : number * 8 + 8, :] = y[:, number * LANES : (number + 1) * LANES].reshape(chips, SUBLANES, LANES)


def collect_kernel(in_ref, corr_ref):
    channels = corr_ref.shape[0]
    for chunk in range(SUBLANES):
        corr_ref[:, chunk * LANES : (chunk + 1) * LANES] = in_ref[pl.ds(16 + chunk, channels, stride=24), :]


def add_kernel(in_ref, out_ref):
    total = in_ref[0] + in_ref[1]
    for place in range(out_ref.shape[0]):
        out_ref[place] = total


def finish_kernel(in_ref, gain_ref, signal_ref, grad_ref, out_ref, back_ref):
    channels = signal_ref.shape[0]
    gains = gain_ref[...]
    for chunk in range(SUBLANES):
        lanes = slice(chunk * LANES, (chunk + 1) * LANES)
        for number, (own, result) in enumerate(((signal_ref, out_ref), (grad_ref, back_ref))):
            conv = in_ref[pl.ds(number * 8 + chunk, channels, stride=24), :]
            result[:, lanes] = (conv + gains * own[:, lanes].astype(jnp.float32)).astype(jnp.bfloat16)


def call(kernel, out_shape, operands, scratch=(), spaces=None):
    if spaces is None:
        spaces = [pltpu.VMEM] * len(operands)
    return pl.pallas_call(
        kernel,
        out_shape=out_shape,
        in_specs=[pl.BlockSpec(memory_space=space) for space in spaces],
        out_specs=jax.tree.map(lambda _: pl.BlockSpec(memory_space=pltpu.VMEM), out_shape),
        scratch_shapes=list(scratch),
        compiler_params=pltpu.CompilerParams(vmem_limit_bytes=VMEM_BYTES),
    )(*operands)


def on_device(signal, filter_taps, skip_gain, grad_out):
    channels, tokens = signal.shape
    chips = lax.axis_size("chip")
    ctx = 2 * chips
    assert channels == chips and tokens == SUBLANES * LANES
    length = tokens * ctx
    rows = length // LANES
    table, twist = make_tables(rows, ctx, 1.0 / math.sqrt(length))
    core = lax.axis_index("core").astype(jnp.int32).reshape(1)

    in_hbm = [pltpu.with_memory_space_constraint(x, pltpu.HBM) for x in (signal, grad_out, filter_taps, table, twist)]
    packed, table, twist = call(
        pack_kernel,
        (
            pltpu.VMEM((chips * 24, LANES), jnp.float32),
            pltpu.VMEM(table.shape, table.dtype),
            pltpu.VMEM(twist.shape, twist.dtype),
        ),
        in_hbm,
        scratch=(
            pltpu.VMEM(signal.shape, signal.dtype),
            pltpu.VMEM(grad_out.shape, grad_out.dtype),
            pltpu.VMEM(filter_taps.shape, filter_taps.dtype),
            pltpu.SemaphoreType.DMA((5,)),
        ),
        spaces=[pltpu.HBM] * 5,
    )
    spread = lax.all_to_all(packed.reshape(chips, 24, LANES), "chip", 0, 0, tiled=True)
    sequences = lax.all_gather(spread, "core", tiled=True)
    results = call(
        convolve_kernel,
        jax.ShapeDtypeStruct((chips, 24, LANES), jnp.float32),
        (core, sequences, table, twist),
        scratch=(
            pltpu.VMEM((2 * rows, 3 * LANES), jnp.float32),
            pltpu.VMEM((2 * rows, 3 * LANES), jnp.bfloat16),
            pltpu.VMEM((2 * rows, 3 * LANES), jnp.bfloat16),
        ),
        spaces=[pltpu.SMEM] + [pltpu.VMEM] * 3,
    )
    returned = lax.all_to_all(results, "chip", 0, 0, tiled=True).reshape(chips * 24, LANES)
    corr = call(collect_kernel, jax.ShapeDtypeStruct((channels, tokens), jnp.float32), (returned,))
    pair = lax.all_gather(corr, "tp_far")
    near = lax.axis_size("tp_near")
    everyone = call(add_kernel, jax.ShapeDtypeStruct((near, channels, tokens), jnp.float32), (pair,))
    shares = lax.all_to_all(everyone, "tp_near", 0, 0, tiled=True)
    grad_filter = jnp.sum(shares, axis=0)
    output, grad_signal = call(
        finish_kernel,
        (
            jax.ShapeDtypeStruct((channels, tokens), jnp.bfloat16),
            jax.ShapeDtypeStruct((channels, tokens), jnp.bfloat16),
        ),
        (returned, skip_gain[:, None], signal, grad_out),
    )
    return (output, grad_signal, grad_filter)


def solution(mesh):
    ctx, tp = mesh.shape["ctx"], mesh.shape["tp"]
    far = 2 if tp % 2 == 0 else 1
    parted = Mesh(mesh.devices.reshape(ctx // 2, 2, far, tp // far), ("chip", "core", "tp_far", "tp_near"))
    in_specs = (P(TP, CTX), P(None, CTX), P(TP), P(TP, CTX))
    out_specs = (P(TP, CTX), P(TP, CTX), P(None, CTX))
    return jax.shard_map(
        on_device, mesh=parted, in_specs=in_specs, out_specs=out_specs, check_vma=False
    )
```

```python
import math

import jax
import jax.numpy as jnp
import ml_dtypes
import numpy as np
from jax import lax
from jax.experimental import pallas as pl
from jax.experimental.pallas import tpu as pltpu
from jax.sharding import Mesh
from jax.sharding import PartitionSpec as P

LANES = 128
SUBLANES = 8
CTX = ("chip", "core")
TP = ("tp_far", "tp_near")
VMEM_BYTES = 24 * 1024 * 1024


def split_table(table):
    high = table.astype(np.float32).astype(ml_dtypes.bfloat16)
    low = (table - high.astype(np.float64)).astype(ml_dtypes.bfloat16)
    return high, low


def make_tables(rows, blocks, scale):
    period = 2 * rows
    padded = period * LANES
    place = np.arange(rows)
    block = place // SUBLANES % (blocks // 2) * 2 + place // (rows // 2)
    a = block * SUBLANES + place % SUBLANES
    f1 = np.arange(rows)
    turn = 2.0 * np.pi * (np.outer(f1, a) % period) / period
    cosines = np.cos(turn)
    sines = -np.sin(turn)
    sines[0] = np.where(a % 2 == 0, 1.0, -1.0)
    outer = np.concatenate([cosines, sines], axis=0)
    weights = np.full((rows,), 2.0)
    weights[0] = 1.0
    outer_back = (outer * np.concatenate([weights, weights])[:, None]).T * (scale / padded)
    b = np.arange(LANES)
    kept = np.arange(rows + 1)
    angle = 2.0 * np.pi * (np.outer(kept, b) % padded) / padded
    twist = np.zeros((rows + 16, 2 * LANES))
    twist[: rows + 1, :LANES] = np.cos(angle)
    twist[: rows + 1, LANES:] = -np.sin(angle)
    inner = 2.0 * np.pi * (np.outer(b, b) % LANES) / LANES
    c, s = np.cos(inner), np.sin(inner)
    inner_there = np.block([[c, -s], [s, c]])
    inner_back = np.block([[c, s], [-s, c]])
    back_columns = np.concatenate(np.split(outer_back, 2 * rows // (2 * LANES), axis=1), axis=0)
    stacked = np.concatenate([outer, inner_there, inner_back, back_columns], axis=0)
    high, low = split_table(stacked)
    return np.stack([high, low]), twist.astype(np.float32)


def split(x):
    high = x.astype(jnp.bfloat16)
    low = (x - high.astype(jnp.float32)).astype(jnp.bfloat16)
    return high, low


def dot(x, y):
    return jnp.dot(x, y, preferred_element_type=jnp.float32)


def pack_kernel(
    signal_hbm, grad_hbm, filter_hbm, gain_hbm, table_hbm, twist_hbm,
    out_ref, skip_ref, table_ref, twist_ref,
    signal_ref, grad_ref, filter_ref, gain_ref, sems,
):
    pairs = (
        (signal_hbm, signal_ref),
        (grad_hbm, grad_ref),
        (filter_hbm, filter_ref),
        (gain_hbm, gain_ref),
        (table_hbm, table_ref),
        (twist_hbm, twist_ref),
    )
    copies = [pltpu.make_async_copy(source, target, sems.at[k]) for k, (source, target) in enumerate(pairs)]
    for copy in copies:
        copy.start()
    channels = signal_ref.shape[0]
    arrays = []
    for number, ref in enumerate((signal_ref, grad_ref, filter_ref)):
        copies[number].wait()
        arrays.append(ref[...].astype(jnp.float32))
        for chunk in range(SUBLANES):
            lanes = slice(chunk * LANES, (chunk + 1) * LANES)
            out_ref[pl.ds(number * 8 + chunk, channels, stride=24), :] = arrays[number][:, lanes]
    copies[3].wait()
    row = lax.broadcasted_iota(jnp.int32, (channels, 1), 0)
    gains = jnp.zeros((channels, 1), jnp.float32)
    for channel in range(channels):
        gains = jnp.where(row == channel, gain_ref[channel], gains)
    skip_ref[0] = gains * arrays[0]
    skip_ref[1] = gains * arrays[1]
    for copy in copies[4:]:
        copy.wait()


def convolve_kernel(in_ref, table, twist, out_ref, a_ref, u_h, u_l):
    chips = out_ref.shape[0]
    half = chips * SUBLANES
    rows = 2 * half
    core = lax.axis_index("core")

    def part(number, start, count):
        return table[number, start : start + count, :]

    def sequence(number):
        return in_ref[:, number * 8 : number * 8 + 8, :].reshape(rows, LANES)

    both = jnp.concatenate([sequence(0), sequence(1)], axis=1).astype(jnp.bfloat16)
    taps_h, taps_l = split(sequence(2))
    outer_h, outer_l = part(0, 0, 2 * rows), part(1, 0, 2 * rows)
    a_ref[:, : 2 * LANES] = dot(outer_h, both) + dot(outer_l, both)
    turned = dot(outer_h, jnp.concatenate([taps_h, taps_l], axis=1))
    a_ref[:, 2 * LANES :] = turned[:, :LANES] + turned[:, LANES:] + dot(outer_l, taps_h)
    at = 2 * rows
    there_h, there_l = part(0, at, 2 * LANES), part(1, at, 2 * LANES)
    at += 2 * LANES
    back_h, back_l = part(0, at, 2 * LANES), part(1, at, 2 * LANES)
    at += 2 * LANES

    last = a_ref[rows : rows + 1, :]
    first_row = lax.broadcasted_iota(jnp.int32, (16, 1), 0) == 0

    for start, count in ((0, rows // 2), (rows // 2, rows // 2), (rows, 16)):
        tr = twist[start : start + count, :LANES]
        ti = twist[start : start + count, LANES:]
        pieces = []
        for number in range(3):
            lanes = slice(number * LANES, (number + 1) * LANES)
            if start == rows:
                ar = jnp.where(first_row, last[:, lanes], 0.0)
                pieces.append(jnp.concatenate([ar * tr, ar * ti], axis=1))
                continue
            ar = a_ref[start : start + count, lanes]
            ai = a_ref[rows + start : rows + start + count, lanes]
            if start == 0:
                row = lax.broadcasted_iota(jnp.int32, (count, 1), 0)
                ai = jnp.where(row == 0, 0.0, ai)
            pieces.append(jnp.concatenate([ar * tr - ai * ti, ar * ti + ai * tr], axis=1))
        z_h, z_l = split(jnp.concatenate(pieces, axis=0))
        spec = dot(z_h, there_h) + dot(z_l, there_h) + dot(z_h, there_l)
        sr, si = spec[:count, :LANES], spec[:count, LANES:]
        gr, gi = spec[count : 2 * count, :LANES], spec[count : 2 * count, LANES:]
        hr, hi = spec[2 * count :, :LANES], spec[2 * count :, LANES:]
        conv = jnp.concatenate([sr * hr - si * hi, sr * hi + si * hr], axis=1)
        back = jnp.concatenate([gr * hr + gi * hi, gi * hr - gr * hi], axis=1)
        corr = jnp.concatenate([gr * sr + gi * si, gi * sr - gr * si], axis=1)
        p_h, p_l = split(jnp.concatenate([conv, back, corr], axis=0))
        v = dot(p_h, back_h) + dot(p_l, back_h) + dot(p_h, back_l)
        for number in range(3):
            vr = v[number * count : (number + 1) * count, :LANES]
            vi = v[number * count : (number + 1) * count, LANES:]
            lanes = slice(number * LANES, (number + 1) * LANES)
            real_h, real_l = split(vr * tr + vi * ti)
            if start == rows:
                u_h[rows : rows + 16, lanes] = jnp.where(first_row, real_h, u_h[rows : rows + 16, lanes])
                u_l[rows : rows + 16, lanes] = jnp.where(first_row, real_l, u_l[rows : rows + 16, lanes])
                continue
            imag_h, imag_l = split(vi * tr - vr * ti)
            u_h[start : start + count, lanes] = real_h
            u_l[start : start + count, lanes] = real_l
            u_h[rows + start : rows + start + count, lanes] = imag_h
            u_l[rows + start : rows + start + count, lanes] = imag_l

    y = jnp.zeros((half, 3 * LANES), jnp.float32)
    for inner in range(0, 2 * rows, 2 * LANES):
        here = slice(inner, inner + 2 * LANES)
        mine = pl.ds(pl.multiple_of(at + core * half, half), half)
        columns_h, columns_l = table[0, mine, :], table[1, mine, :]
        y += dot(columns_h, u_h[here, :]) + dot(columns_h, u_l[here, :]) + dot(columns_l, u_h[here, :])
        at += rows
    for number in range(3):
        out_ref[:, number * 8 : number * 8 + 8, :] = y[:, number * LANES : (number + 1) * LANES].reshape(chips, SUBLANES, LANES)


def collect_kernel(in_ref, corr_ref):
    channels = corr_ref.shape[0]
    for chunk in range(SUBLANES):
        corr_ref[:, chunk * LANES : (chunk + 1) * LANES] = in_ref[pl.ds(16 + chunk, channels, stride=24), :]


def add_kernel(in_ref, out_ref):
    total = in_ref[0]
    for place in range(1, in_ref.shape[0]):
        total += in_ref[place]
    for place in range(out_ref.shape[0]):
        out_ref[place] = total


def finish_kernel(in_ref, skip_ref, shares_ref, out_ref, back_ref, corr_ref):
    channels = corr_ref.shape[0]
    for chunk in range(SUBLANES):
        lanes = slice(chunk * LANES, (chunk + 1) * LANES)
        for number, result in enumerate((out_ref, back_ref)):
            conv = in_ref[pl.ds(number * 8 + chunk, channels, stride=24), :]
            result[:, lanes] = (conv + skip_ref[number, :, lanes]).astype(jnp.bfloat16)
    total = shares_ref[0]
    for place in range(1, shares_ref.shape[0]):
        total += shares_ref[place]
    corr_ref[...] = total


def call(kernel, out_shape, operands, scratch=(), spaces=None):
    if spaces is None:
        spaces = [pltpu.VMEM] * len(operands)
    return pl.pallas_call(
        kernel,
        out_shape=out_shape,
        in_specs=[pl.BlockSpec(memory_space=space) for space in spaces],
        out_specs=jax.tree.map(lambda _: pl.BlockSpec(memory_space=pltpu.VMEM), out_shape),
        scratch_shapes=list(scratch),
        compiler_params=pltpu.CompilerParams(vmem_limit_bytes=VMEM_BYTES),
    )(*operands)


def on_device(signal, filter_taps, skip_gain, grad_out):
    channels, tokens = signal.shape
    chips = lax.axis_size("chip")
    ctx = 2 * chips
    assert channels == chips and tokens == SUBLANES * LANES
    length = tokens * ctx
    rows = length // LANES
    table, twist = make_tables(rows, ctx, 1.0 / math.sqrt(length))

    in_hbm = [
        pltpu.with_memory_space_constraint(x, pltpu.HBM)
        for x in (signal, grad_out, filter_taps, skip_gain, table, twist)
    ]
    packed, skip, table, twist = call(
        pack_kernel,
        (
            pltpu.VMEM((chips * 24, LANES), jnp.float32),
            pltpu.VMEM((2, channels, tokens), jnp.float32),
            pltpu.VMEM(table.shape, table.dtype),
            pltpu.VMEM(twist.shape, twist.dtype),
        ),
        in_hbm,
        scratch=(
            pltpu.VMEM(signal.shape, signal.dtype),
            pltpu.VMEM(grad_out.shape, grad_out.dtype),
            pltpu.VMEM(filter_taps.shape, filter_taps.dtype),
            pltpu.SMEM(skip_gain.shape, skip_gain.dtype),
            pltpu.SemaphoreType.DMA((6,)),
        ),
        spaces=[pltpu.HBM] * 6,
    )
    spread = lax.all_to_all(packed.reshape(chips, 24, LANES), "chip", 0, 0, tiled=True)
    sequences = lax.all_gather(spread, "core", tiled=True)
    results = call(
        convolve_kernel,
        jax.ShapeDtypeStruct((chips, 24, LANES), jnp.float32),
        (sequences, table, twist),
        scratch=(
            pltpu.VMEM((2 * rows, 3 * LANES), jnp.float32),
            pltpu.VMEM((2 * rows, 3 * LANES), jnp.bfloat16),
            pltpu.VMEM((2 * rows, 3 * LANES), jnp.bfloat16),
        ),
    )
    returned = lax.all_to_all(results, "chip", 0, 0, tiled=True).reshape(chips * 24, LANES)
    corr = call(collect_kernel, jax.ShapeDtypeStruct((channels, tokens), jnp.float32), (returned,))
    pair = lax.all_gather(corr, "tp_far")
    near = lax.axis_size("tp_near")
    everyone = call(add_kernel, jax.ShapeDtypeStruct((near, channels, tokens), jnp.float32), (pair,))
    shares = lax.all_to_all(everyone, "tp_near", 0, 0, tiled=True)
    output, grad_signal, grad_filter = call(
        finish_kernel,
        (
            jax.ShapeDtypeStruct((channels, tokens), jnp.bfloat16),
            jax.ShapeDtypeStruct((channels, tokens), jnp.bfloat16),
            jax.ShapeDtypeStruct((channels, tokens), jnp.float32),
        ),
        (returned, skip, shares),
    )
    return (output, grad_signal, grad_filter)


def solution(mesh):
    ctx, tp = mesh.shape["ctx"], mesh.shape["tp"]
    far = 2 if tp % 2 == 0 else 1
    parted = Mesh(mesh.devices.reshape(ctx // 2, 2, far, tp // far), ("chip", "core", "tp_far", "tp_near"))
    in_specs = (P(TP, CTX), P(None, CTX), P(TP), P(TP, CTX))
    out_specs = (P(TP, CTX), P(TP, CTX), P(None, CTX))
    return jax.shard_map(
        on_device, mesh=parted, in_specs=in_specs, out_specs=out_specs, check_vma=False
    )
```

```python
import math

import jax
import jax.numpy as jnp
import ml_dtypes
import numpy as np
from jax import lax
from jax.experimental import pallas as pl
from jax.experimental.pallas import tpu as pltpu
from jax.sharding import Mesh
from jax.sharding import PartitionSpec as P

LANES = 128
SUBLANES = 8
CTX = ("chip", "core")
TP = ("tp_far", "tp_near")
VMEM_BYTES = 24 * 1024 * 1024


def split_table(table):
    high = table.astype(np.float32).astype(ml_dtypes.bfloat16)
    low = (table - high.astype(np.float64)).astype(ml_dtypes.bfloat16)
    return high, low


def make_tables(rows, blocks, scale):
    period = 2 * rows
    padded = period * LANES
    place = np.arange(rows)
    block = place // SUBLANES % (blocks // 2) * 2 + place // (rows // 2)
    a = block * SUBLANES + place % SUBLANES
    f1 = np.arange(rows)
    turn = 2.0 * np.pi * (np.outer(f1, a) % period) / period
    cosines = np.cos(turn)
    sines = -np.sin(turn)
    sines[0] = np.where(a % 2 == 0, 1.0, -1.0)
    outer = np.concatenate([cosines, sines], axis=0)
    weights = np.full((rows,), 2.0)
    weights[0] = 1.0
    outer_back = (outer * np.concatenate([weights, weights])[:, None]).T * (scale / padded)
    b = np.arange(LANES)
    kept = np.arange(rows + 1)
    angle = 2.0 * np.pi * (np.outer(kept, b) % padded) / padded
    twist = np.zeros((rows + 16, 2 * LANES))
    twist[: rows + 1, :LANES] = np.cos(angle)
    twist[: rows + 1, LANES:] = -np.sin(angle)
    inner = 2.0 * np.pi * (np.outer(b, b) % LANES) / LANES
    c, s = np.cos(inner), np.sin(inner)
    inner_there = np.block([[c, -s], [s, c]])
    inner_back = np.block([[c, s], [-s, c]])
    back_columns = np.concatenate(np.split(outer_back, 2 * rows // (2 * LANES), axis=1), axis=0)
    stacked = np.concatenate([outer, inner_there, inner_back, back_columns], axis=0)
    high, low = split_table(stacked)
    return np.stack([high, low]), twist.astype(np.float32)


def split(x):
    high = x.astype(jnp.bfloat16)
    low = (x - high.astype(jnp.float32)).astype(jnp.bfloat16)
    return high, low


def dot(x, y):
    return jnp.dot(x, y, preferred_element_type=jnp.float32)


def pack_kernel(
    signal_hbm, grad_hbm, filter_hbm, gain_hbm, table_hbm, twist_hbm,
    out_ref, skip_ref, table_ref, twist_ref,
    signal_ref, grad_ref, filter_ref, gain_ref, sems,
):
    pairs = (
        (signal_hbm, signal_ref),
        (grad_hbm, grad_ref),
        (filter_hbm, filter_ref),
        (gain_hbm, gain_ref),
        (table_hbm, table_ref),
        (twist_hbm, twist_ref),
    )
    copies = [pltpu.make_async_copy(source, target, sems.at[k]) for k, (source, target) in enumerate(pairs)]
    for copy in copies:
        copy.start()
    channels = signal_ref.shape[0]
    arrays = []
    for number, ref in enumerate((signal_ref, grad_ref, filter_ref)):
        copies[number].wait()
        arrays.append(ref[...].astype(jnp.float32))
        for chunk in range(SUBLANES):
            lanes = slice(chunk * LANES, (chunk + 1) * LANES)
            out_ref[pl.ds(number * 8 + chunk, channels, stride=24), :] = arrays[number][:, lanes]
    copies[3].wait()
    row = lax.broadcasted_iota(jnp.int32, (channels, 1), 0)
    gains = jnp.zeros((channels, 1), jnp.float32)
    for channel in range(channels):
        gains = jnp.where(row == channel, gain_ref[channel], gains)
    skip_ref[0] = gains * arrays[0]
    skip_ref[1] = gains * arrays[1]
    for copy in copies[4:]:
        copy.wait()


def convolve_kernel(in_ref, table, twist, out_ref, a_ref, u_h, u_l):
    chips = out_ref.shape[0]
    half = chips * SUBLANES
    rows = 2 * half
    core = lax.axis_index("core")

    def part(number, start, count):
        return table[number, start : start + count, :]

    def sequence(number):
        return in_ref[:, number * 8 : number * 8 + 8, :].reshape(rows, LANES)

    both = jnp.concatenate([sequence(0), sequence(1)], axis=1).astype(jnp.bfloat16)
    taps_h, taps_l = split(sequence(2))
    outer_h, outer_l = part(0, 0, 2 * rows), part(1, 0, 2 * rows)
    a_ref[:, : 2 * LANES] = dot(outer_h, both) + dot(outer_l, both)
    turned = dot(outer_h, jnp.concatenate([taps_h, taps_l], axis=1))
    a_ref[:, 2 * LANES :] = turned[:, :LANES] + turned[:, LANES:] + dot(outer_l, taps_h)
    at = 2 * rows
    there_h, there_l = part(0, at, 2 * LANES), part(1, at, 2 * LANES)
    at += 2 * LANES
    back_h, back_l = part(0, at, 2 * LANES), part(1, at, 2 * LANES)
    at += 2 * LANES

    last = a_ref[rows : rows + 1, :]
    first_row = lax.broadcasted_iota(jnp.int32, (16, 1), 0) == 0

    for start, count in ((0, rows // 2), (rows // 2, rows // 2), (rows, 16)):
        tr = twist[start : start + count, :LANES]
        ti = twist[start : start + count, LANES:]
        pieces = []
        for number in range(3):
            lanes = slice(number * LANES, (number + 1) * LANES)
            if start == rows:
                ar = jnp.where(first_row, last[:, lanes], 0.0)
                pieces.append(jnp.concatenate([ar * tr, ar * ti], axis=1))
                continue
            ar = a_ref[start : start + count, lanes]
            ai = a_ref[rows + start : rows + start + count, lanes]
            if start == 0:
                row = lax.broadcasted_iota(jnp.int32, (count, 1), 0)
                ai = jnp.where(row == 0, 0.0, ai)
            pieces.append(jnp.concatenate([ar * tr - ai * ti, ar * ti + ai * tr], axis=1))
        z_h, z_l = split(jnp.concatenate(pieces, axis=0))
        spec = dot(z_h, there_h) + dot(z_l, there_h) + dot(z_h, there_l)
        sr, si = spec[:count, :LANES], spec[:count, LANES:]
        gr, gi = spec[count : 2 * count, :LANES], spec[count : 2 * count, LANES:]
        hr, hi = spec[2 * count :, :LANES], spec[2 * count :, LANES:]
        conv = jnp.concatenate([sr * hr - si * hi, sr * hi + si * hr], axis=1)
        back = jnp.concatenate([gr * hr + gi * hi, gi * hr - gr * hi], axis=1)
        corr = jnp.concatenate([gr * sr + gi * si, gi * sr - gr * si], axis=1)
        p_h, p_l = split(jnp.concatenate([conv, back, corr], axis=0))
        v = dot(p_h, back_h) + dot(p_l, back_h) + dot(p_h, back_l)
        for number in range(3):
            vr = v[number * count : (number + 1) * count, :LANES]
            vi = v[number * count : (number + 1) * count, LANES:]
            lanes = slice(number * LANES, (number + 1) * LANES)
            real_h, real_l = split(vr * tr + vi * ti)
            if start == rows:
                u_h[rows : rows + 16, lanes] = jnp.where(first_row, real_h, u_h[rows : rows + 16, lanes])
                u_l[rows : rows + 16, lanes] = jnp.where(first_row, real_l, u_l[rows : rows + 16, lanes])
                continue
            imag_h, imag_l = split(vi * tr - vr * ti)
            u_h[start : start + count, lanes] = real_h
            u_l[start : start + count, lanes] = real_l
            u_h[rows + start : rows + start + count, lanes] = imag_h
            u_l[rows + start : rows + start + count, lanes] = imag_l

    y = jnp.zeros((half, 3 * LANES), jnp.float32)
    for inner in range(0, 2 * rows, 2 * LANES):
        here = slice(inner, inner + 2 * LANES)
        mine = pl.ds(pl.multiple_of(at + core * half, half), half)
        columns_h, columns_l = table[0, mine, :], table[1, mine, :]
        y += dot(columns_h, u_h[here, :]) + dot(columns_h, u_l[here, :]) + dot(columns_l, u_h[here, :])
        at += rows
    for number in range(3):
        out_ref[:, number * 8 : number * 8 + 8, :] = y[:, number * LANES : (number + 1) * LANES].reshape(chips, SUBLANES, LANES)


def collect_kernel(in_ref, corr_ref):
    corr_ref[...] = in_ref[:, 16:, :]


def add_kernel(in_ref, out_ref):
    total = in_ref[0]
    for place in range(1, in_ref.shape[0]):
        total += in_ref[place]
    for place in range(out_ref.shape[0]):
        out_ref[place] = total


def finish_kernel(in_ref, skip_ref, shares_ref, out_ref, back_ref, corr_ref, total_ref):
    channels = corr_ref.shape[0]
    total = shares_ref[0]
    for place in range(1, shares_ref.shape[0]):
        total += shares_ref[place]
    total_ref[...] = total
    for chunk in range(SUBLANES):
        lanes = slice(chunk * LANES, (chunk + 1) * LANES)
        corr_ref[:, lanes] = total_ref[pl.ds(chunk, channels, stride=SUBLANES), :]
        for number, result in enumerate((out_ref, back_ref)):
            conv = in_ref[pl.ds(number * 8 + chunk, channels, stride=24), :]
            result[:, lanes] = (conv + skip_ref[number, :, lanes]).astype(jnp.bfloat16)


def call(kernel, out_shape, operands, scratch=(), spaces=None):
    if spaces is None:
        spaces = [pltpu.VMEM] * len(operands)
    return pl.pallas_call(
        kernel,
        out_shape=out_shape,
        in_specs=[pl.BlockSpec(memory_space=space) for space in spaces],
        out_specs=jax.tree.map(lambda _: pl.BlockSpec(memory_space=pltpu.VMEM), out_shape),
        scratch_shapes=list(scratch),
        compiler_params=pltpu.CompilerParams(vmem_limit_bytes=VMEM_BYTES),
    )(*operands)


def on_device(signal, filter_taps, skip_gain, grad_out):
    channels, tokens = signal.shape
    chips = lax.axis_size("chip")
    ctx = 2 * chips
    assert channels == chips and tokens == SUBLANES * LANES
    length = tokens * ctx
    rows = length // LANES
    table, twist = make_tables(rows, ctx, 1.0 / math.sqrt(length))

    in_hbm = [
        pltpu.with_memory_space_constraint(x, pltpu.HBM)
        for x in (signal, grad_out, filter_taps, skip_gain, table, twist)
    ]
    packed, skip, table, twist = call(
        pack_kernel,
        (
            pltpu.VMEM((chips * 24, LANES), jnp.float32),
            pltpu.VMEM((2, channels, tokens), jnp.float32),
            pltpu.VMEM(table.shape, table.dtype),
            pltpu.VMEM(twist.shape, twist.dtype),
        ),
        in_hbm,
        scratch=(
            pltpu.VMEM(signal.shape, signal.dtype),
            pltpu.VMEM(grad_out.shape, grad_out.dtype),
            pltpu.VMEM(filter_taps.shape, filter_taps.dtype),
            pltpu.SMEM(skip_gain.shape, skip_gain.dtype),
            pltpu.SemaphoreType.DMA((6,)),
        ),
        spaces=[pltpu.HBM] * 6,
    )
    spread = lax.all_to_all(packed.reshape(chips, 24, LANES), "chip", 0, 0, tiled=True)
    sequences = lax.all_gather(spread, "core", tiled=True)
    results = call(
        convolve_kernel,
        jax.ShapeDtypeStruct((chips, 24, LANES), jnp.float32),
        (sequences, table, twist),
        scratch=(
            pltpu.VMEM((2 * rows, 3 * LANES), jnp.float32),
            pltpu.VMEM((2 * rows, 3 * LANES), jnp.bfloat16),
            pltpu.VMEM((2 * rows, 3 * LANES), jnp.bfloat16),
        ),
    )
    returned = lax.all_to_all(results, "chip", 0, 0, tiled=True)
    corr = call(collect_kernel, jax.ShapeDtypeStruct((channels, SUBLANES, LANES), jnp.float32), (returned,))
    corr = corr.reshape(channels * SUBLANES, LANES)
    pair = lax.all_gather(corr, "tp_far")
    near = lax.axis_size("tp_near")
    everyone = call(add_kernel, jax.ShapeDtypeStruct((near, *corr.shape), jnp.float32), (pair,))
    shares = lax.all_to_all(everyone, "tp_near", 0, 0, tiled=True)
    output, grad_signal, grad_filter = call(
        finish_kernel,
        (
            jax.ShapeDtypeStruct((channels, tokens), jnp.bfloat16),
            jax.ShapeDtypeStruct((channels, tokens), jnp.bfloat16),
            jax.ShapeDtypeStruct((channels, tokens), jnp.float32),
        ),
        (returned.reshape(chips * 24, LANES), skip, shares),
        scratch=(pltpu.VMEM(corr.shape, corr.dtype),),
    )
    return (output, grad_signal, grad_filter)


def solution(mesh):
    ctx, tp = mesh.shape["ctx"], mesh.shape["tp"]
    far = 2 if tp % 2 == 0 else 1
    parted = Mesh(mesh.devices.reshape(ctx // 2, 2, far, tp // far), ("chip", "core", "tp_far", "tp_near"))
    in_specs = (P(TP, CTX), P(None, CTX), P(TP), P(TP, CTX))
    out_specs = (P(TP, CTX), P(TP, CTX), P(None, CTX))
    return jax.shard_map(
        on_device, mesh=parted, in_specs=in_specs, out_specs=out_specs, check_vma=False
    )
```

```python
import math

import jax
import jax.numpy as jnp
import ml_dtypes
import numpy as np
from jax import lax
from jax.experimental import pallas as pl
from jax.experimental.pallas import tpu as pltpu
from jax.sharding import Mesh
from jax.sharding import PartitionSpec as P

LANES = 128
SUBLANES = 8
CTX = ("chip", "core")
TP = ("tp_far", "tp_near")
VMEM_BYTES = 24 * 1024 * 1024


def split_table(table):
    high = table.astype(np.float32).astype(ml_dtypes.bfloat16)
    low = (table - high.astype(np.float64)).astype(ml_dtypes.bfloat16)
    return high, low


def make_tables(rows, blocks, scale):
    period = 2 * rows
    padded = period * LANES
    place = np.arange(rows)
    block = place // SUBLANES % (blocks // 2) * 2 + place // (rows // 2)
    a = block * SUBLANES + place % SUBLANES
    f1 = np.arange(rows)
    turn = 2.0 * np.pi * (np.outer(f1, a) % period) / period
    cosines = np.cos(turn)
    sines = -np.sin(turn)
    sines[0] = np.where(a % 2 == 0, 1.0, -1.0)
    outer = np.concatenate([cosines, sines], axis=0)
    weights = np.full((rows,), 2.0)
    weights[0] = 1.0
    outer_back = (outer * np.concatenate([weights, weights])[:, None]).T * (scale / padded)
    b = np.arange(LANES)
    kept = np.arange(rows + 1)
    angle = 2.0 * np.pi * (np.outer(kept, b) % padded) / padded
    twist = np.zeros((rows + 16, 2 * LANES))
    twist[: rows + 1, :LANES] = np.cos(angle)
    twist[: rows + 1, LANES:] = -np.sin(angle)
    inner = 2.0 * np.pi * (np.outer(b, b) % LANES) / LANES
    c, s = np.cos(inner), np.sin(inner)
    inner_there = np.block([[c, -s], [s, c]])
    inner_back = np.block([[c, s], [-s, c]])
    back_columns = np.concatenate(np.split(outer_back, 2 * rows // (2 * LANES), axis=1), axis=0)
    stacked = np.concatenate([outer, inner_there, inner_back, back_columns], axis=0)
    high, low = split_table(stacked)
    return np.stack([high, low]), twist.astype(np.float32)


def split(x):
    high = x.astype(jnp.bfloat16)
    low = (x - high.astype(jnp.float32)).astype(jnp.bfloat16)
    return high, low


def dot(x, y):
    return jnp.dot(x, y, preferred_element_type=jnp.float32)


def pack_kernel(
    signal_hbm, grad_hbm, filter_hbm, gain_hbm, table_hbm, twist_hbm,
    out_ref, skip_ref, table_ref, twist_ref,
    signal_ref, grad_ref, filter_ref, gain_ref, sems,
):
    pairs = (
        (signal_hbm, signal_ref),
        (grad_hbm, grad_ref),
        (filter_hbm, filter_ref),
        (gain_hbm, gain_ref),
        (table_hbm, table_ref),
        (twist_hbm, twist_ref),
    )
    copies = [pltpu.make_async_copy(source, target, sems.at[k]) for k, (source, target) in enumerate(pairs)]
    for copy in copies:
        copy.start()
    channels = signal_ref.shape[0]
    arrays = []
    for number, ref in enumerate((signal_ref, grad_ref, filter_ref)):
        copies[number].wait()
        arrays.append(ref[...].astype(jnp.float32))
        for chunk in range(SUBLANES):
            lanes = slice(chunk * LANES, (chunk + 1) * LANES)
            out_ref[pl.ds(number * 8 + chunk, channels, stride=24), :] = arrays[number][:, lanes]
    copies[3].wait()
    row = lax.broadcasted_iota(jnp.int32, (channels, 1), 0)
    gains = jnp.zeros((channels, 1), jnp.float32)
    for channel in range(channels):
        gains = jnp.where(row == channel, gain_ref[channel], gains)
    skip_ref[0] = gains * arrays[0]
    skip_ref[1] = gains * arrays[1]
    for copy in copies[4:]:
        copy.wait()


def convolve_kernel(in_ref, table, twist, out_ref, a_ref, u_h, u_l):
    chips = out_ref.shape[0]
    half = chips * SUBLANES
    rows = 2 * half
    core = lax.axis_index("core")

    def part(number, start, count):
        return table[number, start : start + count, :]

    def sequence(number):
        return in_ref[:, number * 8 : number * 8 + 8, :].reshape(rows, LANES)

    both = jnp.concatenate([sequence(0), sequence(1)], axis=1).astype(jnp.bfloat16)
    taps_h, taps_l = split(sequence(2))
    outer_h, outer_l = part(0, 0, 2 * rows), part(1, 0, 2 * rows)
    a_ref[:, : 2 * LANES] = dot(outer_h, both) + dot(outer_l, both)
    turned = dot(outer_h, jnp.concatenate([taps_h, taps_l], axis=1))
    a_ref[:, 2 * LANES :] = turned[:, :LANES] + turned[:, LANES:] + dot(outer_l, taps_h)
    at = 2 * rows
    there_h, there_l = part(0, at, 2 * LANES), part(1, at, 2 * LANES)
    at += 2 * LANES
    back_h, back_l = part(0, at, 2 * LANES), part(1, at, 2 * LANES)
    at += 2 * LANES

    last = a_ref[rows : rows + 1, :]
    first_row = lax.broadcasted_iota(jnp.int32, (16, 1), 0) == 0

    for start, count in ((0, rows // 2), (rows // 2, rows // 2), (rows, 16)):
        tr = twist[start : start + count, :LANES]
        ti = twist[start : start + count, LANES:]
        pieces = []
        for number in range(3):
            lanes = slice(number * LANES, (number + 1) * LANES)
            if start == rows:
                ar = jnp.where(first_row, last[:, lanes], 0.0)
                pieces.append(jnp.concatenate([ar * tr, ar * ti], axis=1))
                continue
            ar = a_ref[start : start + count, lanes]
            ai = a_ref[rows + start : rows + start + count, lanes]
            if start == 0:
                row = lax.broadcasted_iota(jnp.int32, (count, 1), 0)
                ai = jnp.where(row == 0, 0.0, ai)
            pieces.append(jnp.concatenate([ar * tr - ai * ti, ar * ti + ai * tr], axis=1))
        z_h, z_l = split(jnp.concatenate(pieces, axis=0))
        spec = dot(z_h, there_h) + dot(z_l, there_h) + dot(z_h, there_l)
        sr, si = spec[:count, :LANES], spec[:count, LANES:]
        gr, gi = spec[count : 2 * count, :LANES], spec[count : 2 * count, LANES:]
        hr, hi = spec[2 * count :, :LANES], spec[2 * count :, LANES:]
        conv = jnp.concatenate([sr * hr - si * hi, sr * hi + si * hr], axis=1)
        back = jnp.concatenate([gr * hr + gi * hi, gi * hr - gr * hi], axis=1)
        corr = jnp.concatenate([gr * sr + gi * si, gi * sr - gr * si], axis=1)
        p_h, p_l = split(jnp.concatenate([conv, back, corr], axis=0))
        v = dot(p_h, back_h) + dot(p_l, back_h) + dot(p_h, back_l)
        for number in range(3):
            vr = v[number * count : (number + 1) * count, :LANES]
            vi = v[number * count : (number + 1) * count, LANES:]
            lanes = slice(number * LANES, (number + 1) * LANES)
            real_h, real_l = split(vr * tr + vi * ti)
            if start == rows:
                u_h[rows : rows + 16, lanes] = jnp.where(first_row, real_h, u_h[rows : rows + 16, lanes])
                u_l[rows : rows + 16, lanes] = jnp.where(first_row, real_l, u_l[rows : rows + 16, lanes])
                continue
            imag_h, imag_l = split(vi * tr - vr * ti)
            u_h[start : start + count, lanes] = real_h
            u_l[start : start + count, lanes] = real_l
            u_h[rows + start : rows + start + count, lanes] = imag_h
            u_l[rows + start : rows + start + count, lanes] = imag_l

    y = jnp.zeros((half, 3 * LANES), jnp.float32)
    for inner in range(0, 2 * rows, 2 * LANES):
        here = slice(inner, inner + 2 * LANES)
        mine = pl.ds(pl.multiple_of(at + core * half, half), half)
        columns_h, columns_l = table[0, mine, :], table[1, mine, :]
        y += dot(columns_h, u_h[here, :]) + dot(columns_h, u_l[here, :]) + dot(columns_l, u_h[here, :])
        at += rows
    for number in range(3):
        piece = y[:, number * LANES : (number + 1) * LANES].reshape(chips, SUBLANES, LANES)
        for far in range(out_ref.shape[1]):
            out_ref[:, far, number * 8 : number * 8 + 8, :] = piece


def collect_kernel(in_ref, everyone_ref):
    channels, chunks, lanes = in_ref.shape[0], SUBLANES, in_ref.shape[3]
    total = in_ref[:, 0, 16:, :]
    for far in range(1, in_ref.shape[1]):
        total += in_ref[:, far, 16:, :]
    total = total.reshape(channels * chunks, lanes)
    for place in range(everyone_ref.shape[0]):
        everyone_ref[place] = total


def finish_kernel(in_ref, skip_ref, shares_ref, out_ref, back_ref, corr_ref, own_ref, total_ref):
    channels = corr_ref.shape[0]
    total = shares_ref[0]
    for place in range(1, shares_ref.shape[0]):
        total += shares_ref[place]
    total_ref[...] = total
    own = in_ref[:, pl.ds(lax.axis_index("tp_far"), 1), :16, :]
    own_ref[...] = own.reshape(own_ref.shape)
    for chunk in range(SUBLANES):
        lanes = slice(chunk * LANES, (chunk + 1) * LANES)
        corr_ref[:, lanes] = total_ref[pl.ds(chunk, channels, stride=SUBLANES), :]
        for number, result in enumerate((out_ref, back_ref)):
            conv = own_ref[pl.ds(number * 8 + chunk, channels, stride=16), :]
            result[:, lanes] = (conv + skip_ref[number, :, lanes]).astype(jnp.bfloat16)


def call(kernel, out_shape, operands, scratch=(), spaces=None):
    if spaces is None:
        spaces = [pltpu.VMEM] * len(operands)
    return pl.pallas_call(
        kernel,
        out_shape=out_shape,
        in_specs=[pl.BlockSpec(memory_space=space) for space in spaces],
        out_specs=jax.tree.map(lambda _: pl.BlockSpec(memory_space=pltpu.VMEM), out_shape),
        scratch_shapes=list(scratch),
        compiler_params=pltpu.CompilerParams(vmem_limit_bytes=VMEM_BYTES),
    )(*operands)


def on_device(signal, filter_taps, skip_gain, grad_out):
    channels, tokens = signal.shape
    chips = lax.axis_size("chip")
    far = lax.axis_size("tp_far")
    ctx = 2 * chips
    assert channels == chips and tokens == SUBLANES * LANES
    length = tokens * ctx
    rows = length // LANES
    table, twist = make_tables(rows, ctx, 1.0 / math.sqrt(length))

    in_hbm = [
        pltpu.with_memory_space_constraint(x, pltpu.HBM)
        for x in (signal, grad_out, filter_taps, skip_gain, table, twist)
    ]
    packed, skip, table, twist = call(
        pack_kernel,
        (
            pltpu.VMEM((chips * 24, LANES), jnp.float32),
            pltpu.VMEM((2, channels, tokens), jnp.float32),
            pltpu.VMEM(table.shape, table.dtype),
            pltpu.VMEM(twist.shape, twist.dtype),
        ),
        in_hbm,
        scratch=(
            pltpu.VMEM(signal.shape, signal.dtype),
            pltpu.VMEM(grad_out.shape, grad_out.dtype),
            pltpu.VMEM(filter_taps.shape, filter_taps.dtype),
            pltpu.SMEM(skip_gain.shape, skip_gain.dtype),
            pltpu.SemaphoreType.DMA((6,)),
        ),
        spaces=[pltpu.HBM] * 6,
    )
    spread = lax.all_to_all(packed.reshape(chips, 24, LANES), "chip", 0, 0, tiled=True)
    sequences = lax.all_gather(spread, "core", tiled=True)
    results = call(
        convolve_kernel,
        jax.ShapeDtypeStruct((chips, far, 24, LANES), jnp.float32),
        (sequences, table, twist),
        scratch=(
            pltpu.VMEM((2 * rows, 3 * LANES), jnp.float32),
            pltpu.VMEM((2 * rows, 3 * LANES), jnp.bfloat16),
            pltpu.VMEM((2 * rows, 3 * LANES), jnp.bfloat16),
        ),
    )
    results = results.reshape(chips * far, 24, LANES)
    returned = lax.all_to_all(results, ("chip", "tp_far"), 0, 0, tiled=True).reshape(chips, far, 24, LANES)
    near = lax.axis_size("tp_near")
    everyone = call(
        collect_kernel, jax.ShapeDtypeStruct((near, channels * SUBLANES, LANES), jnp.float32), (returned,)
    )
    shares = lax.all_to_all(everyone, "tp_near", 0, 0, tiled=True)
    output, grad_signal, grad_filter = call(
        finish_kernel,
        (
            jax.ShapeDtypeStruct((channels, tokens), jnp.bfloat16),
            jax.ShapeDtypeStruct((channels, tokens), jnp.bfloat16),
            jax.ShapeDtypeStruct((channels, tokens), jnp.float32),
        ),
        (returned, skip, shares),
        scratch=(
            pltpu.VMEM((channels * 16, LANES), jnp.float32),
            pltpu.VMEM((channels * SUBLANES, LANES), jnp.float32),
        ),
    )
    return (output, grad_signal, grad_filter)


def solution(mesh):
    ctx, tp = mesh.shape["ctx"], mesh.shape["tp"]
    far = 2 if tp % 2 == 0 else 1
    parted = Mesh(mesh.devices.reshape(ctx // 2, 2, far, tp // far), ("chip", "core", "tp_far", "tp_near"))
    in_specs = (P(TP, CTX), P(None, CTX), P(TP), P(TP, CTX))
    out_specs = (P(TP, CTX), P(TP, CTX), P(None, CTX))
    return jax.shard_map(
        on_device, mesh=parted, in_specs=in_specs, out_specs=out_specs, check_vma=False
    )
```

```python
import math

import jax
import jax.numpy as jnp
import ml_dtypes
import numpy as np
from jax import lax
from jax.experimental import pallas as pl
from jax.experimental.pallas import tpu as pltpu
from jax.sharding import Mesh
from jax.sharding import PartitionSpec as P

LANES = 128
SUBLANES = 8
CTX = ("chip", "core")
TP = ("tp_far", "tp_even", "tp_next")
TP_FIRST = ("tp_far", "tp_next")
TP_SECOND = ("tp_even",)
VMEM_BYTES = 24 * 1024 * 1024


def split_table(table):
    high = table.astype(np.float32).astype(ml_dtypes.bfloat16)
    low = (table - high.astype(np.float64)).astype(ml_dtypes.bfloat16)
    return high, low


def make_tables(rows, blocks, scale):
    period = 2 * rows
    padded = period * LANES
    place = np.arange(rows)
    block = place // SUBLANES % (blocks // 2) * 2 + place // (rows // 2)
    a = block * SUBLANES + place % SUBLANES
    f1 = np.arange(rows)
    turn = 2.0 * np.pi * (np.outer(f1, a) % period) / period
    cosines = np.cos(turn)
    sines = -np.sin(turn)
    sines[0] = np.where(a % 2 == 0, 1.0, -1.0)
    outer = np.concatenate([cosines, sines], axis=0)
    weights = np.full((rows,), 2.0)
    weights[0] = 1.0
    outer_back = (outer * np.concatenate([weights, weights])[:, None]).T * (scale / padded)
    b = np.arange(LANES)
    kept = np.arange(rows + 1)
    angle = 2.0 * np.pi * (np.outer(kept, b) % padded) / padded
    twist = np.zeros((rows + 16, 2 * LANES))
    twist[: rows + 1, :LANES] = np.cos(angle)
    twist[: rows + 1, LANES:] = -np.sin(angle)
    inner = 2.0 * np.pi * (np.outer(b, b) % LANES) / LANES
    c, s = np.cos(inner), np.sin(inner)
    inner_there = np.block([[c, -s], [s, c]])
    inner_back = np.block([[c, s], [-s, c]])
    back_columns = np.concatenate(np.split(outer_back, 2 * rows // (2 * LANES), axis=1), axis=0)
    stacked = np.concatenate([outer, inner_there, inner_back, back_columns], axis=0)
    high, low = split_table(stacked)
    return np.stack([high, low]), twist.astype(np.float32)


def split(x):
    high = x.astype(jnp.bfloat16)
    low = (x - high.astype(jnp.float32)).astype(jnp.bfloat16)
    return high, low


def dot(x, y):
    return jnp.dot(x, y, preferred_element_type=jnp.float32)


def pack_kernel(
    signal_hbm, grad_hbm, filter_hbm, gain_hbm, table_hbm, twist_hbm,
    out_ref, skip_ref, table_ref, twist_ref,
    signal_ref, grad_ref, filter_ref, gain_ref, sems,
):
    pairs = (
        (signal_hbm, signal_ref),
        (grad_hbm, grad_ref),
        (filter_hbm, filter_ref),
        (gain_hbm, gain_ref),
        (table_hbm, table_ref),
        (twist_hbm, twist_ref),
    )
    copies = [pltpu.make_async_copy(source, target, sems.at[k]) for k, (source, target) in enumerate(pairs)]
    for copy in copies:
        copy.start()
    channels = signal_ref.shape[0]
    arrays = []
    for number, ref in enumerate((signal_ref, grad_ref, filter_ref)):
        copies[number].wait()
        arrays.append(ref[...].astype(jnp.float32))
        for chunk in range(SUBLANES):
            lanes = slice(chunk * LANES, (chunk + 1) * LANES)
            out_ref[pl.ds(number * 8 + chunk, channels, stride=24), :] = arrays[number][:, lanes]
    copies[3].wait()
    row = lax.broadcasted_iota(jnp.int32, (channels, 1), 0)
    gains = jnp.zeros((channels, 1), jnp.float32)
    for channel in range(channels):
        gains = jnp.where(row == channel, gain_ref[channel], gains)
    skip_ref[0] = gains * arrays[0]
    skip_ref[1] = gains * arrays[1]
    for copy in copies[4:]:
        copy.wait()


def convolve_kernel(in_ref, table, twist, out_ref, a_ref, u_h, u_l):
    chips = out_ref.shape[0]
    half = chips * SUBLANES
    rows = 2 * half
    core = lax.axis_index("core")

    def part(number, start, count):
        return table[number, start : start + count, :]

    def sequence(number):
        return in_ref[:, number * 8 : number * 8 + 8, :].reshape(rows, LANES)

    both = jnp.concatenate([sequence(0), sequence(1)], axis=1).astype(jnp.bfloat16)
    taps_h, taps_l = split(sequence(2))
    outer_h, outer_l = part(0, 0, 2 * rows), part(1, 0, 2 * rows)
    a_ref[:, : 2 * LANES] = dot(outer_h, both) + dot(outer_l, both)
    turned = dot(outer_h, jnp.concatenate([taps_h, taps_l], axis=1))
    a_ref[:, 2 * LANES :] = turned[:, :LANES] + turned[:, LANES:] + dot(outer_l, taps_h)
    at = 2 * rows
    there_h, there_l = part(0, at, 2 * LANES), part(1, at, 2 * LANES)
    at += 2 * LANES
    back_h, back_l = part(0, at, 2 * LANES), part(1, at, 2 * LANES)
    at += 2 * LANES

    last = a_ref[rows : rows + 1, :]
    first_row = lax.broadcasted_iota(jnp.int32, (16, 1), 0) == 0

    for start, count in ((0, rows // 2), (rows // 2, rows // 2), (rows, 16)):
        tr = twist[start : start + count, :LANES]
        ti = twist[start : start + count, LANES:]
        pieces = []
        for number in range(3):
            lanes = slice(number * LANES, (number + 1) * LANES)
            if start == rows:
                ar = jnp.where(first_row, last[:, lanes], 0.0)
                pieces.append(jnp.concatenate([ar * tr, ar * ti], axis=1))
                continue
            ar = a_ref[start : start + count, lanes]
            ai = a_ref[rows + start : rows + start + count, lanes]
            if start == 0:
                row = lax.broadcasted_iota(jnp.int32, (count, 1), 0)
                ai = jnp.where(row == 0, 0.0, ai)
            pieces.append(jnp.concatenate([ar * tr - ai * ti, ar * ti + ai * tr], axis=1))
        z_h, z_l = split(jnp.concatenate(pieces, axis=0))
        spec = dot(z_h, there_h) + dot(z_l, there_h) + dot(z_h, there_l)
        sr, si = spec[:count, :LANES], spec[:count, LANES:]
        gr, gi = spec[count : 2 * count, :LANES], spec[count : 2 * count, LANES:]
        hr, hi = spec[2 * count :, :LANES], spec[2 * count :, LANES:]
        conv = jnp.concatenate([sr * hr - si * hi, sr * hi + si * hr], axis=1)
        back = jnp.concatenate([gr * hr + gi * hi, gi * hr - gr * hi], axis=1)
        corr = jnp.concatenate([gr * sr + gi * si, gi * sr - gr * si], axis=1)
        p_h, p_l = split(jnp.concatenate([conv, back, corr], axis=0))
        v = dot(p_h, back_h) + dot(p_l, back_h) + dot(p_h, back_l)
        for number in range(3):
            vr = v[number * count : (number + 1) * count, :LANES]
            vi = v[number * count : (number + 1) * count, LANES:]
            lanes = slice(number * LANES, (number + 1) * LANES)
            real_h, real_l = split(vr * tr + vi * ti)
            if start == rows:
                u_h[rows : rows + 16, lanes] = jnp.where(first_row, real_h, u_h[rows : rows + 16, lanes])
                u_l[rows : rows + 16, lanes] = jnp.where(first_row, real_l, u_l[rows : rows + 16, lanes])
                continue
            imag_h, imag_l = split(vi * tr - vr * ti)
            u_h[start : start + count, lanes] = real_h
            u_l[start : start + count, lanes] = real_l
            u_h[rows + start : rows + start + count, lanes] = imag_h
            u_l[rows + start : rows + start + count, lanes] = imag_l

    y = jnp.zeros((half, 3 * LANES), jnp.float32)
    for inner in range(0, 2 * rows, 2 * LANES):
        here = slice(inner, inner + 2 * LANES)
        mine = pl.ds(pl.multiple_of(at + core * half, half), half)
        columns_h, columns_l = table[0, mine, :], table[1, mine, :]
        y += dot(columns_h, u_h[here, :]) + dot(columns_h, u_l[here, :]) + dot(columns_l, u_h[here, :])
        at += rows
    for number in range(3):
        out_ref[:, number * 8 : number * 8 + 8, :] = y[:, number * LANES : (number + 1) * LANES].reshape(chips, SUBLANES, LANES)


def collect_kernel(in_ref, out_ref):
    mine = in_ref[:, 16:, :].reshape(out_ref.shape[1:])
    for place in range(out_ref.shape[0]):
        out_ref[place] = mine


def add_kernel(in_ref, out_ref):
    total = in_ref[0]
    for place in range(1, in_ref.shape[0]):
        total += in_ref[place]
    for place in range(out_ref.shape[0]):
        out_ref[place] = total


def finish_kernel(in_ref, skip_ref, shares_ref, out_ref, back_ref, corr_ref, total_ref):
    channels = corr_ref.shape[0]
    total = shares_ref[0]
    for place in range(1, shares_ref.shape[0]):
        total += shares_ref[place]
    total_ref[...] = total
    for chunk in range(SUBLANES):
        lanes = slice(chunk * LANES, (chunk + 1) * LANES)
        corr_ref[:, lanes] = total_ref[pl.ds(chunk, channels, stride=SUBLANES), :]
        for number, result in enumerate((out_ref, back_ref)):
            conv = in_ref[pl.ds(number * 8 + chunk, channels, stride=24), :]
            result[:, lanes] = (conv + skip_ref[number, :, lanes]).astype(jnp.bfloat16)


def call(kernel, out_shape, operands, scratch=(), spaces=None):
    if spaces is None:
        spaces = [pltpu.VMEM] * len(operands)
    return pl.pallas_call(
        kernel,
        out_shape=out_shape,
        in_specs=[pl.BlockSpec(memory_space=space) for space in spaces],
        out_specs=jax.tree.map(lambda _: pl.BlockSpec(memory_space=pltpu.VMEM), out_shape),
        scratch_shapes=list(scratch),
        compiler_params=pltpu.CompilerParams(vmem_limit_bytes=VMEM_BYTES),
    )(*operands)


def on_device(signal, filter_taps, skip_gain, grad_out):
    channels, tokens = signal.shape
    chips = lax.axis_size("chip")
    ctx = 2 * chips
    assert channels == chips and tokens == SUBLANES * LANES
    length = tokens * ctx
    rows = length // LANES
    table, twist = make_tables(rows, ctx, 1.0 / math.sqrt(length))

    in_hbm = [
        pltpu.with_memory_space_constraint(x, pltpu.HBM)
        for x in (signal, grad_out, filter_taps, skip_gain, table, twist)
    ]
    packed, skip, table, twist = call(
        pack_kernel,
        (
            pltpu.VMEM((chips * 24, LANES), jnp.float32),
            pltpu.VMEM((2, channels, tokens), jnp.float32),
            pltpu.VMEM(table.shape, table.dtype),
            pltpu.VMEM(twist.shape, twist.dtype),
        ),
        in_hbm,
        scratch=(
            pltpu.VMEM(signal.shape, signal.dtype),
            pltpu.VMEM(grad_out.shape, grad_out.dtype),
            pltpu.VMEM(filter_taps.shape, filter_taps.dtype),
            pltpu.SMEM(skip_gain.shape, skip_gain.dtype),
            pltpu.SemaphoreType.DMA((6,)),
        ),
        spaces=[pltpu.HBM] * 6,
    )
    spread = lax.all_to_all(packed.reshape(chips, 24, LANES), "chip", 0, 0, tiled=True)
    sequences = lax.all_gather(spread, "core", tiled=True)
    results = call(
        convolve_kernel,
        jax.ShapeDtypeStruct((chips, 24, LANES), jnp.float32),
        (sequences, table, twist),
        scratch=(
            pltpu.VMEM((2 * rows, 3 * LANES), jnp.float32),
            pltpu.VMEM((2 * rows, 3 * LANES), jnp.bfloat16),
            pltpu.VMEM((2 * rows, 3 * LANES), jnp.bfloat16),
        ),
    )
    returned = lax.all_to_all(results, "chip", 0, 0, tiled=True)
    shape = (channels * SUBLANES, LANES)
    first, second = lax.axis_size(TP_FIRST), lax.axis_size(TP_SECOND)
    everyone = call(collect_kernel, jax.ShapeDtypeStruct((first, *shape), jnp.float32), (returned,))
    shares = lax.all_to_all(everyone, TP_FIRST, 0, 0, tiled=True)
    everyone = call(add_kernel, jax.ShapeDtypeStruct((second, *shape), jnp.float32), (shares,))
    shares = lax.all_to_all(everyone, TP_SECOND, 0, 0, tiled=True)
    output, grad_signal, grad_filter = call(
        finish_kernel,
        (
            jax.ShapeDtypeStruct((channels, tokens), jnp.bfloat16),
            jax.ShapeDtypeStruct((channels, tokens), jnp.bfloat16),
            jax.ShapeDtypeStruct((channels, tokens), jnp.float32),
        ),
        (returned.reshape(chips * 24, LANES), skip, shares),
        scratch=(pltpu.VMEM(shape, jnp.float32),),
    )
    return (output, grad_signal, grad_filter)


def solution(mesh):
    ctx, tp = mesh.shape["ctx"], mesh.shape["tp"]
    parted = Mesh(mesh.devices.reshape(ctx // 2, 2, 2, tp // 4, 2), (*CTX, *TP))
    in_specs = (P(TP, CTX), P(None, CTX), P(TP), P(TP, CTX))
    out_specs = (P(TP, CTX), P(TP, CTX), P(None, CTX))
    return jax.shard_map(
        on_device, mesh=parted, in_specs=in_specs, out_specs=out_specs, check_vma=False
    )
```

```python
import math

import jax
import jax.numpy as jnp
import ml_dtypes
import numpy as np
from jax import lax
from jax.experimental import pallas as pl
from jax.experimental.pallas import tpu as pltpu
from jax.sharding import Mesh
from jax.sharding import PartitionSpec as P

LANES = 128
SUBLANES = 8
CTX = ("chip", "core")
TP = ("tp_far", "tp_even", "tp_next")
TP_FIRST = ("tp_far", "tp_next")
TP_SECOND = ("tp_even",)
VMEM_BYTES = 24 * 1024 * 1024


def split_table(table):
    high = table.astype(np.float32).astype(ml_dtypes.bfloat16)
    low = (table - high.astype(np.float64)).astype(ml_dtypes.bfloat16)
    return high, low


def make_tables(rows, blocks, scale):
    period = 2 * rows
    padded = period * LANES
    place = np.arange(rows)
    block = place // SUBLANES % (blocks // 2) * 2 + place // (rows // 2)
    a = block * SUBLANES + place % SUBLANES
    f1 = np.arange(rows)
    turn = 2.0 * np.pi * (np.outer(f1, a) % period) / period
    cosines = np.cos(turn)
    sines = -np.sin(turn)
    sines[0] = np.where(a % 2 == 0, 1.0, -1.0)
    outer = np.concatenate([cosines, sines], axis=0)
    weights = np.full((rows,), 2.0)
    weights[0] = 1.0
    outer_back = (outer * np.concatenate([weights, weights])[:, None]).T * (scale / padded)
    b = np.arange(LANES)
    kept = np.arange(rows + 1)
    angle = 2.0 * np.pi * (np.outer(kept, b) % padded) / padded
    twist = np.zeros((rows + 16, 2 * LANES))
    twist[: rows + 1, :LANES] = np.cos(angle)
    twist[: rows + 1, LANES:] = -np.sin(angle)
    inner = 2.0 * np.pi * (np.outer(b, b) % LANES) / LANES
    c, s = np.cos(inner), np.sin(inner)
    inner_there = np.block([[c, -s], [s, c]])
    inner_back = np.block([[c, s], [-s, c]])
    back_columns = np.concatenate(np.split(outer_back, 2 * rows // (2 * LANES), axis=1), axis=0)
    parts = [np.stack(split_table(part)) for part in (outer, inner_there, inner_back, *np.split(back_columns, 2))]
    return (*parts, twist.astype(np.float32))


def split(x):
    high = x.astype(jnp.bfloat16)
    low = (x - high.astype(jnp.float32)).astype(jnp.bfloat16)
    return high, low


def dot(x, y):
    return jnp.dot(x, y, preferred_element_type=jnp.float32)


def pack_kernel(
    signal_hbm, grad_hbm, filter_hbm, gain_hbm, table_hbm,
    out_ref, skip_ref, table_ref,
    signal_ref, grad_ref, filter_ref, gain_ref, sems,
):
    pairs = (
        (signal_hbm, signal_ref),
        (grad_hbm, grad_ref),
        (filter_hbm, filter_ref),
        (gain_hbm, gain_ref),
        (table_hbm, table_ref),
    )
    copies = [pltpu.make_async_copy(source, target, sems.at[k]) for k, (source, target) in enumerate(pairs)]
    for copy in copies:
        copy.start()
    channels = signal_ref.shape[0]
    arrays = []
    for number, ref in enumerate((signal_ref, grad_ref, filter_ref)):
        copies[number].wait()
        arrays.append(ref[...].astype(jnp.float32))
        for chunk in range(SUBLANES):
            lanes = slice(chunk * LANES, (chunk + 1) * LANES)
            out_ref[pl.ds(number * 8 + chunk, channels, stride=24), :] = arrays[number][:, lanes]
    copies[3].wait()
    row = lax.broadcasted_iota(jnp.int32, (channels, 1), 0)
    gains = jnp.zeros((channels, 1), jnp.float32)
    for channel in range(channels):
        gains = jnp.where(row == channel, gain_ref[channel], gains)
    skip_ref[0] = gains * arrays[0]
    skip_ref[1] = gains * arrays[1]
    for copy in copies[4:]:
        copy.wait()


def convolve_kernel(in_ref, outer, there, back, first_back, second_back, twist, out_ref, a_ref, u_h, u_l):
    chips = out_ref.shape[0]
    half = chips * SUBLANES
    rows = 2 * half
    core = lax.axis_index("core")

    def sequence(number):
        return in_ref[:, number * 8 : number * 8 + 8, :].reshape(rows, LANES)

    both = jnp.concatenate([sequence(0), sequence(1)], axis=1).astype(jnp.bfloat16)
    taps_h, taps_l = split(sequence(2))
    outer_h, outer_l = outer[0], outer[1]
    a_ref[:, : 2 * LANES] = dot(outer_h, both) + dot(outer_l, both)
    turned = dot(outer_h, jnp.concatenate([taps_h, taps_l], axis=1))
    a_ref[:, 2 * LANES :] = turned[:, :LANES] + turned[:, LANES:] + dot(outer_l, taps_h)
    there_h, there_l = there[0], there[1]
    back_h, back_l = back[0], back[1]

    last = a_ref[rows : rows + 1, :]
    first_row = lax.broadcasted_iota(jnp.int32, (16, 1), 0) == 0

    for start, count in [(k, 64) for k in range(0, rows, 64)] + [(rows, 16)]:
        tr = twist[start : start + count, :LANES]
        ti = twist[start : start + count, LANES:]
        pieces = []
        for number in range(3):
            lanes = slice(number * LANES, (number + 1) * LANES)
            if start == rows:
                ar = jnp.where(first_row, last[:, lanes], 0.0)
                pieces.append(jnp.concatenate([ar * tr, ar * ti], axis=1))
                continue
            ar = a_ref[start : start + count, lanes]
            ai = a_ref[rows + start : rows + start + count, lanes]
            if start == 0:
                row = lax.broadcasted_iota(jnp.int32, (count, 1), 0)
                ai = jnp.where(row == 0, 0.0, ai)
            pieces.append(jnp.concatenate([ar * tr - ai * ti, ar * ti + ai * tr], axis=1))
        z_h, z_l = split(jnp.concatenate(pieces, axis=0))
        spec = dot(z_h, there_h) + dot(z_l, there_h) + dot(z_h, there_l)
        sr, si = spec[:count, :LANES], spec[:count, LANES:]
        gr, gi = spec[count : 2 * count, :LANES], spec[count : 2 * count, LANES:]
        hr, hi = spec[2 * count :, :LANES], spec[2 * count :, LANES:]
        conv = jnp.concatenate([sr * hr - si * hi, sr * hi + si * hr], axis=1)
        back = jnp.concatenate([gr * hr + gi * hi, gi * hr - gr * hi], axis=1)
        corr = jnp.concatenate([gr * sr + gi * si, gi * sr - gr * si], axis=1)
        p_h, p_l = split(jnp.concatenate([conv, back, corr], axis=0))
        v = dot(p_h, back_h) + dot(p_l, back_h) + dot(p_h, back_l)
        for number in range(3):
            vr = v[number * count : (number + 1) * count, :LANES]
            vi = v[number * count : (number + 1) * count, LANES:]
            lanes = slice(number * LANES, (number + 1) * LANES)
            real_h, real_l = split(vr * tr + vi * ti)
            if start == rows:
                u_h[rows : rows + 16, lanes] = jnp.where(first_row, real_h, u_h[rows : rows + 16, lanes])
                u_l[rows : rows + 16, lanes] = jnp.where(first_row, real_l, u_l[rows : rows + 16, lanes])
                continue
            imag_h, imag_l = split(vi * tr - vr * ti)
            u_h[start : start + count, lanes] = real_h
            u_l[start : start + count, lanes] = real_l
            u_h[rows + start : rows + start + count, lanes] = imag_h
            u_l[rows + start : rows + start + count, lanes] = imag_l

    y = jnp.zeros((half, 3 * LANES), jnp.float32)
    mine = pl.ds(pl.multiple_of(core * half, half), half)
    for number, columns in enumerate((first_back, second_back)):
        here = slice(number * rows, (number + 1) * rows)
        columns_h, columns_l = columns[0, mine, :], columns[1, mine, :]
        y += dot(columns_h, u_h[here, :]) + dot(columns_h, u_l[here, :]) + dot(columns_l, u_h[here, :])
    for number in range(3):
        out_ref[:, number * 8 : number * 8 + 8, :] = y[:, number * LANES : (number + 1) * LANES].reshape(chips, SUBLANES, LANES)


def collect_kernel(in_ref, out_ref):
    mine = in_ref[:, 16:, :].reshape(out_ref.shape[1:])
    for place in range(out_ref.shape[0]):
        out_ref[place] = mine


def add_kernel(in_ref, out_ref):
    total = in_ref[0]
    for place in range(1, in_ref.shape[0]):
        total += in_ref[place]
    for place in range(out_ref.shape[0]):
        out_ref[place] = total


def finish_kernel(in_ref, skip_ref, shares_ref, out_ref, back_ref, corr_ref, total_ref):
    channels = corr_ref.shape[0]
    total = shares_ref[0]
    for place in range(1, shares_ref.shape[0]):
        total += shares_ref[place]
    total_ref[...] = total
    for chunk in range(SUBLANES):
        lanes = slice(chunk * LANES, (chunk + 1) * LANES)
        corr_ref[:, lanes] = total_ref[pl.ds(chunk, channels, stride=SUBLANES), :]
        for number, result in enumerate((out_ref, back_ref)):
            conv = in_ref[pl.ds(number * 8 + chunk, channels, stride=24), :]
            result[:, lanes] = (conv + skip_ref[number, :, lanes]).astype(jnp.bfloat16)


def call(kernel, out_shape, operands, scratch=(), spaces=None):
    if spaces is None:
        spaces = [pltpu.VMEM] * len(operands)
    return pl.pallas_call(
        kernel,
        out_shape=out_shape,
        in_specs=[pl.BlockSpec(memory_space=space) for space in spaces],
        out_specs=jax.tree.map(lambda _: pl.BlockSpec(memory_space=pltpu.VMEM), out_shape),
        scratch_shapes=list(scratch),
        compiler_params=pltpu.CompilerParams(vmem_limit_bytes=VMEM_BYTES),
    )(*operands)


def on_device(signal, filter_taps, skip_gain, grad_out):
    channels, tokens = signal.shape
    chips = lax.axis_size("chip")
    ctx = 2 * chips
    assert channels == chips and tokens == SUBLANES * LANES
    length = tokens * ctx
    rows = length // LANES
    outer, *tables = make_tables(rows, ctx, 1.0 / math.sqrt(length))

    in_hbm = [
        pltpu.with_memory_space_constraint(x, pltpu.HBM)
        for x in (signal, grad_out, filter_taps, skip_gain, outer)
    ]
    packed, skip, outer = call(
        pack_kernel,
        (
            pltpu.VMEM((chips * 24, LANES), jnp.float32),
            pltpu.VMEM((2, channels, tokens), jnp.float32),
            pltpu.VMEM(outer.shape, outer.dtype),
        ),
        in_hbm,
        scratch=(
            pltpu.VMEM(signal.shape, signal.dtype),
            pltpu.VMEM(grad_out.shape, grad_out.dtype),
            pltpu.VMEM(filter_taps.shape, filter_taps.dtype),
            pltpu.SMEM(skip_gain.shape, skip_gain.dtype),
            pltpu.SemaphoreType.DMA((5,)),
        ),
        spaces=[pltpu.HBM] * 5,
    )
    spread = lax.all_to_all(packed.reshape(chips, 24, LANES), "chip", 0, 0, tiled=True)
    sequences = lax.all_gather(spread, "core", tiled=True)
    results = call(
        convolve_kernel,
        jax.ShapeDtypeStruct((chips, 24, LANES), jnp.float32),
        (sequences, outer, *tables),
        scratch=(
            pltpu.VMEM((2 * rows, 3 * LANES), jnp.float32),
            pltpu.VMEM((2 * rows, 3 * LANES), jnp.bfloat16),
            pltpu.VMEM((2 * rows, 3 * LANES), jnp.bfloat16),
        ),
    )
    returned = lax.all_to_all(results, "chip", 0, 0, tiled=True)
    shape = (channels * SUBLANES, LANES)
    first, second = lax.axis_size(TP_FIRST), lax.axis_size(TP_SECOND)
    everyone = call(collect_kernel, jax.ShapeDtypeStruct((first, *shape), jnp.float32), (returned,))
    shares = lax.all_to_all(everyone, TP_FIRST, 0, 0, tiled=True)
    everyone = call(add_kernel, jax.ShapeDtypeStruct((second, *shape), jnp.float32), (shares,))
    shares = lax.all_to_all(everyone, TP_SECOND, 0, 0, tiled=True)
    output, grad_signal, grad_filter = call(
        finish_kernel,
        (
            jax.ShapeDtypeStruct((channels, tokens), jnp.bfloat16),
            jax.ShapeDtypeStruct((channels, tokens), jnp.bfloat16),
            jax.ShapeDtypeStruct((channels, tokens), jnp.float32),
        ),
        (returned.reshape(chips * 24, LANES), skip, shares),
        scratch=(pltpu.VMEM(shape, jnp.float32),),
    )
    return (output, grad_signal, grad_filter)


def solution(mesh):
    ctx, tp = mesh.shape["ctx"], mesh.shape["tp"]
    parted = Mesh(mesh.devices.reshape(ctx // 2, 2, 2, tp // 4, 2), (*CTX, *TP))
    in_specs = (P(TP, CTX), P(None, CTX), P(TP), P(TP, CTX))
    out_specs = (P(TP, CTX), P(TP, CTX), P(None, CTX))
    return jax.shard_map(
        on_device, mesh=parted, in_specs=in_specs, out_specs=out_specs, check_vma=False
    )
```

```python
import math

import jax
import jax.numpy as jnp
import ml_dtypes
import numpy as np
from jax import lax
from jax.experimental import pallas as pl
from jax.experimental.pallas import tpu as pltpu
from jax.sharding import Mesh
from jax.sharding import PartitionSpec as P

LANES = 128
SUBLANES = 8
CTX = ("chip", "core")
TP = ("tp_far", "tp_even", "tp_next")
TP_FIRST = ("tp_far", "tp_next")
TP_SECOND = ("tp_even",)
VMEM_BYTES = 24 * 1024 * 1024


def split_table(table):
    high = table.astype(np.float32).astype(ml_dtypes.bfloat16)
    low = (table - high.astype(np.float64)).astype(ml_dtypes.bfloat16)
    return high, low


def make_tables(rows, blocks, scale):
    period = 2 * rows
    padded = period * LANES
    place = np.arange(rows)
    block = place // SUBLANES % (blocks // 2) * 2 + place // (rows // 2)
    a = block * SUBLANES + place % SUBLANES
    f1 = np.arange(rows)
    turn = 2.0 * np.pi * (np.outer(f1, a) % period) / period
    cosines = np.cos(turn)
    sines = -np.sin(turn)
    sines[0] = np.where(a % 2 == 0, 1.0, -1.0)
    outer = np.concatenate([cosines, sines], axis=0)
    weights = np.full((rows,), 2.0)
    weights[0] = 1.0
    outer_back = (outer * np.concatenate([weights, weights])[:, None]).T * (scale / padded)
    b = np.arange(LANES)
    kept = np.arange(rows + 1)
    angle = 2.0 * np.pi * (np.outer(kept, b) % padded) / padded
    twist = np.zeros((rows + 16, 2 * LANES))
    twist[: rows + 1, :LANES] = np.cos(angle)
    twist[: rows + 1, LANES:] = -np.sin(angle)
    inner = 2.0 * np.pi * (np.outer(b, b) % LANES) / LANES
    c, s = np.cos(inner), np.sin(inner)
    inner_there = np.block([[c, -s], [s, c]])
    inner_back = np.block([[c, s], [-s, c]])
    back_columns = np.concatenate(np.split(outer_back, 2 * rows // (2 * LANES), axis=1), axis=0)
    parts = [np.stack(split_table(part)) for part in (outer, inner_there, inner_back, *np.split(back_columns, 2))]
    return (*parts, twist.astype(np.float32))


def split(x):
    high = x.astype(jnp.bfloat16)
    low = (x - high.astype(jnp.float32)).astype(jnp.bfloat16)
    return high, low


def dot(x, y):
    return jnp.dot(x, y, preferred_element_type=jnp.float32)


def pack_kernel(
    signal_hbm, grad_hbm, filter_hbm, gain_hbm, table_hbm,
    out_ref, skip_ref, table_ref,
    signal_ref, grad_ref, filter_ref, gain_ref, sems,
):
    pairs = (
        (signal_hbm, signal_ref),
        (grad_hbm, grad_ref),
        (filter_hbm, filter_ref),
        (gain_hbm, gain_ref),
        (table_hbm, table_ref),
    )
    copies = [pltpu.make_async_copy(source, target, sems.at[k]) for k, (source, target) in enumerate(pairs)]
    for copy in copies:
        copy.start()
    channels = signal_ref.shape[0]
    arrays = []
    for number, ref in enumerate((signal_ref, grad_ref, filter_ref)):
        copies[number].wait()
        arrays.append(ref[...].astype(jnp.float32))
        for chunk in range(SUBLANES):
            lanes = slice(chunk * LANES, (chunk + 1) * LANES)
            out_ref[pl.ds(number * 8 + chunk, channels, stride=24), :] = arrays[number][:, lanes]
    copies[3].wait()
    row = lax.broadcasted_iota(jnp.int32, (channels, 1), 0)
    gains = jnp.zeros((channels, 1), jnp.float32)
    for channel in range(channels):
        gains = jnp.where(row == channel, gain_ref[channel], gains)
    skip_ref[0] = gains * arrays[0]
    skip_ref[1] = gains * arrays[1]
    for copy in copies[4:]:
        copy.wait()


def convolve_kernel(in_ref, outer, there, back, first_back, second_back, twist, out_ref, everyone_ref, a_ref, u_h, u_l):
    chips = out_ref.shape[0]
    half = chips * SUBLANES
    rows = 2 * half
    core = lax.axis_index("core")

    def sequence(number):
        return in_ref[:, number * 8 : number * 8 + 8, :].reshape(rows, LANES)

    both = jnp.concatenate([sequence(0), sequence(1)], axis=1).astype(jnp.bfloat16)
    taps_h, taps_l = split(sequence(2))
    outer_h, outer_l = outer[0], outer[1]
    a_ref[:, : 2 * LANES] = dot(outer_h, both) + dot(outer_l, both)
    turned = dot(outer_h, jnp.concatenate([taps_h, taps_l], axis=1))
    a_ref[:, 2 * LANES :] = turned[:, :LANES] + turned[:, LANES:] + dot(outer_l, taps_h)
    there_h, there_l = there[0], there[1]
    back_h, back_l = back[0], back[1]

    last = a_ref[rows : rows + 1, :]
    first_row = lax.broadcasted_iota(jnp.int32, (16, 1), 0) == 0

    for start, count in [(k, 64) for k in range(0, rows, 64)] + [(rows, 16)]:
        tr = twist[start : start + count, :LANES]
        ti = twist[start : start + count, LANES:]
        pieces = []
        for number in range(3):
            lanes = slice(number * LANES, (number + 1) * LANES)
            if start == rows:
                ar = jnp.where(first_row, last[:, lanes], 0.0)
                pieces.append(jnp.concatenate([ar * tr, ar * ti], axis=1))
                continue
            ar = a_ref[start : start + count, lanes]
            ai = a_ref[rows + start : rows + start + count, lanes]
            if start == 0:
                row = lax.broadcasted_iota(jnp.int32, (count, 1), 0)
                ai = jnp.where(row == 0, 0.0, ai)
            pieces.append(jnp.concatenate([ar * tr - ai * ti, ar * ti + ai * tr], axis=1))
        z_h, z_l = split(jnp.concatenate(pieces, axis=0))
        spec = dot(z_h, there_h) + dot(z_l, there_h) + dot(z_h, there_l)
        sr, si = spec[:count, :LANES], spec[:count, LANES:]
        gr, gi = spec[count : 2 * count, :LANES], spec[count : 2 * count, LANES:]
        hr, hi = spec[2 * count :, :LANES], spec[2 * count :, LANES:]
        conv = jnp.concatenate([sr * hr - si * hi, sr * hi + si * hr], axis=1)
        back = jnp.concatenate([gr * hr + gi * hi, gi * hr - gr * hi], axis=1)
        corr = jnp.concatenate([gr * sr + gi * si, gi * sr - gr * si], axis=1)
        p_h, p_l = split(jnp.concatenate([conv, back, corr], axis=0))
        v = dot(p_h, back_h) + dot(p_l, back_h) + dot(p_h, back_l)
        for number in range(3):
            vr = v[number * count : (number + 1) * count, :LANES]
            vi = v[number * count : (number + 1) * count, LANES:]
            lanes = slice(number * LANES, (number + 1) * LANES)
            real_h, real_l = split(vr * tr + vi * ti)
            if start == rows:
                u_h[rows : rows + 16, lanes] = jnp.where(first_row, real_h, u_h[rows : rows + 16, lanes])
                u_l[rows : rows + 16, lanes] = jnp.where(first_row, real_l, u_l[rows : rows + 16, lanes])
                continue
            imag_h, imag_l = split(vi * tr - vr * ti)
            u_h[start : start + count, lanes] = real_h
            u_l[start : start + count, lanes] = real_l
            u_h[rows + start : rows + start + count, lanes] = imag_h
            u_l[rows + start : rows + start + count, lanes] = imag_l

    y = jnp.zeros((half, 3 * LANES), jnp.float32)
    mine = pl.ds(pl.multiple_of(core * half, half), half)
    for number, columns in enumerate((first_back, second_back)):
        here = slice(number * rows, (number + 1) * rows)
        columns_h, columns_l = columns[0, mine, :], columns[1, mine, :]
        y += dot(columns_h, u_h[here, :]) + dot(columns_h, u_l[here, :]) + dot(columns_l, u_h[here, :])
    for number in range(2):
        out_ref[:, number * 8 : number * 8 + 8, :] = y[:, number * LANES : (number + 1) * LANES].reshape(chips, SUBLANES, LANES)
    for place in range(everyone_ref.shape[0]):
        everyone_ref[place] = y[:, 2 * LANES :]


def sum_of(in_ref):
    total = in_ref[0]
    for place in range(1, in_ref.shape[0]):
        total += in_ref[place]
    return total


def add_kernel(in_ref, out_ref):
    total = sum_of(in_ref)
    for place in range(out_ref.shape[0]):
        out_ref[place] = total


def join_kernel(in_ref, shares_ref, out_ref):
    out_ref[:, :16, :] = in_ref[...]
    out_ref[:, 16:, :] = sum_of(shares_ref).reshape(out_ref.shape[0], SUBLANES, LANES)


def finish_kernel(in_ref, skip_ref, out_ref, back_ref, corr_ref):
    channels = corr_ref.shape[0]
    for chunk in range(SUBLANES):
        lanes = slice(chunk * LANES, (chunk + 1) * LANES)
        corr_ref[:, lanes] = in_ref[pl.ds(16 + chunk, channels, stride=24), :]
        for number, result in enumerate((out_ref, back_ref)):
            conv = in_ref[pl.ds(number * 8 + chunk, channels, stride=24), :]
            result[:, lanes] = (conv + skip_ref[number, :, lanes]).astype(jnp.bfloat16)


def call(kernel, out_shape, operands, scratch=(), spaces=None):
    if spaces is None:
        spaces = [pltpu.VMEM] * len(operands)
    return pl.pallas_call(
        kernel,
        out_shape=out_shape,
        in_specs=[pl.BlockSpec(memory_space=space) for space in spaces],
        out_specs=jax.tree.map(lambda _: pl.BlockSpec(memory_space=pltpu.VMEM), out_shape),
        scratch_shapes=list(scratch),
        compiler_params=pltpu.CompilerParams(vmem_limit_bytes=VMEM_BYTES),
    )(*operands)


def on_device(signal, filter_taps, skip_gain, grad_out):
    channels, tokens = signal.shape
    chips = lax.axis_size("chip")
    ctx = 2 * chips
    assert channels == chips and tokens == SUBLANES * LANES
    length = tokens * ctx
    rows = length // LANES
    outer, *tables = make_tables(rows, ctx, 1.0 / math.sqrt(length))

    in_hbm = [
        pltpu.with_memory_space_constraint(x, pltpu.HBM)
        for x in (signal, grad_out, filter_taps, skip_gain, outer)
    ]
    packed, skip, outer = call(
        pack_kernel,
        (
            pltpu.VMEM((chips * 24, LANES), jnp.float32),
            pltpu.VMEM((2, channels, tokens), jnp.float32),
            pltpu.VMEM(outer.shape, outer.dtype),
        ),
        in_hbm,
        scratch=(
            pltpu.VMEM(signal.shape, signal.dtype),
            pltpu.VMEM(grad_out.shape, grad_out.dtype),
            pltpu.VMEM(filter_taps.shape, filter_taps.dtype),
            pltpu.SMEM(skip_gain.shape, skip_gain.dtype),
            pltpu.SemaphoreType.DMA((5,)),
        ),
        spaces=[pltpu.HBM] * 5,
    )
    spread = lax.all_to_all(packed.reshape(chips, 24, LANES), "chip", 0, 0, tiled=True)
    sequences = lax.all_gather(spread, "core", tiled=True)
    first, second = lax.axis_size(TP_FIRST), lax.axis_size(TP_SECOND)
    results, everyone = call(
        convolve_kernel,
        (
            pltpu.VMEM((chips, 16, LANES), jnp.float32),
            pltpu.VMEM((first, rows // 2, LANES), jnp.float32),
        ),
        (sequences, outer, *tables),
        scratch=(
            pltpu.VMEM((2 * rows, 3 * LANES), jnp.float32),
            pltpu.VMEM((2 * rows, 3 * LANES), jnp.bfloat16),
            pltpu.VMEM((2 * rows, 3 * LANES), jnp.bfloat16),
        ),
    )
    shares = lax.all_to_all(everyone, TP_FIRST, 0, 0, tiled=True)
    everyone = call(add_kernel, jax.ShapeDtypeStruct((second, rows // 2, LANES), jnp.float32), (shares,))
    shares = lax.all_to_all(everyone, TP_SECOND, 0, 0, tiled=True)
    joined = call(join_kernel, jax.ShapeDtypeStruct((chips, 24, LANES), jnp.float32), (results, shares))
    returned = lax.all_to_all(joined, "chip", 0, 0, tiled=True)
    output, grad_signal, grad_filter = call(
        finish_kernel,
        (
            jax.ShapeDtypeStruct((channels, tokens), jnp.bfloat16),
            jax.ShapeDtypeStruct((channels, tokens), jnp.bfloat16),
            jax.ShapeDtypeStruct((channels, tokens), jnp.float32),
        ),
        (returned.reshape(chips * 24, LANES), skip),
    )
    return (output, grad_signal, grad_filter)


def solution(mesh):
    ctx, tp = mesh.shape["ctx"], mesh.shape["tp"]
    parted = Mesh(mesh.devices.reshape(ctx // 2, 2, 2, tp // 4, 2), (*CTX, *TP))
    in_specs = (P(TP, CTX), P(None, CTX), P(TP), P(TP, CTX))
    out_specs = (P(TP, CTX), P(TP, CTX), P(None, CTX))
    return jax.shard_map(
        on_device, mesh=parted, in_specs=in_specs, out_specs=out_specs, check_vma=False
    )
```

```python
import math

import jax
import jax.numpy as jnp
import ml_dtypes
import numpy as np
from jax import lax
from jax.experimental import pallas as pl
from jax.experimental.pallas import tpu as pltpu
from jax.sharding import Mesh
from jax.sharding import PartitionSpec as P

LANES = 128
SUBLANES = 8
CTX = ("chip", "core")
TP = ("tp_far", "tp_even", "tp_next")
TP_FIRST = ("tp_even",)
TP_SECOND = ("tp_far", "tp_next")
VMEM_BYTES = 24 * 1024 * 1024


def split_table(table):
    high = table.astype(np.float32).astype(ml_dtypes.bfloat16)
    low = (table - high.astype(np.float64)).astype(ml_dtypes.bfloat16)
    return high, low


def make_tables(rows, blocks, scale):
    period = 2 * rows
    padded = period * LANES
    place = np.arange(rows)
    block = place // SUBLANES % (blocks // 2) * 2 + place // (rows // 2)
    a = block * SUBLANES + place % SUBLANES
    f1 = np.arange(rows)
    turn = 2.0 * np.pi * (np.outer(f1, a) % period) / period
    cosines = np.cos(turn)
    sines = -np.sin(turn)
    sines[0] = np.where(a % 2 == 0, 1.0, -1.0)
    outer = np.concatenate([cosines, sines], axis=0)
    weights = np.full((rows,), 2.0)
    weights[0] = 1.0
    outer_back = (outer * np.concatenate([weights, weights])[:, None]).T * (scale / padded)
    b = np.arange(LANES)
    kept = np.arange(rows + 1)
    angle = 2.0 * np.pi * (np.outer(kept, b) % padded) / padded
    twist = np.zeros((rows + 16, 2 * LANES))
    twist[: rows + 1, :LANES] = np.cos(angle)
    twist[: rows + 1, LANES:] = -np.sin(angle)
    inner = 2.0 * np.pi * (np.outer(b, b) % LANES) / LANES
    c, s = np.cos(inner), np.sin(inner)
    inner_there = np.block([[c, -s], [s, c]])
    inner_back = np.block([[c, s], [-s, c]])
    back_columns = np.concatenate(np.split(outer_back, 2 * rows // (2 * LANES), axis=1), axis=0)
    parts = [np.stack(split_table(part)) for part in (outer, inner_there, inner_back, *np.split(back_columns, 2))]
    return (*parts, twist.astype(np.float32))


def split(x):
    high = x.astype(jnp.bfloat16)
    low = (x - high.astype(jnp.float32)).astype(jnp.bfloat16)
    return high, low


def dot(x, y):
    return jnp.dot(x, y, preferred_element_type=jnp.float32)


def pack_kernel(
    signal_hbm, grad_hbm, filter_hbm, gain_hbm, table_hbm,
    out_ref, skip_ref, table_ref,
    signal_ref, grad_ref, filter_ref, gain_ref, sems,
):
    pairs = (
        (signal_hbm, signal_ref),
        (grad_hbm, grad_ref),
        (filter_hbm, filter_ref),
        (gain_hbm, gain_ref),
        (table_hbm, table_ref),
    )
    copies = [pltpu.make_async_copy(source, target, sems.at[k]) for k, (source, target) in enumerate(pairs)]
    for copy in copies:
        copy.start()
    channels = signal_ref.shape[0]
    arrays = []
    for number, ref in enumerate((signal_ref, grad_ref, filter_ref)):
        copies[number].wait()
        arrays.append(ref[...].astype(jnp.float32))
        for chunk in range(SUBLANES):
            lanes = slice(chunk * LANES, (chunk + 1) * LANES)
            out_ref[pl.ds(number * 8 + chunk, channels, stride=24), :] = arrays[number][:, lanes]
    copies[3].wait()
    row = lax.broadcasted_iota(jnp.int32, (channels, 1), 0)
    gains = jnp.zeros((channels, 1), jnp.float32)
    for channel in range(channels):
        gains = jnp.where(row == channel, gain_ref[channel], gains)
    skip_ref[0] = gains * arrays[0]
    skip_ref[1] = gains * arrays[1]
    for copy in copies[4:]:
        copy.wait()


def convolve_kernel(in_ref, outer, there, back, first_back, second_back, twist, out_ref, a_ref, u_h, u_l):
    chips = out_ref.shape[0]
    half = chips * SUBLANES
    rows = 2 * half
    core = lax.axis_index("core")

    def sequence(number):
        return in_ref[:, number * 8 : number * 8 + 8, :].reshape(rows, LANES)

    both = jnp.concatenate([sequence(0), sequence(1)], axis=1).astype(jnp.bfloat16)
    taps_h, taps_l = split(sequence(2))
    outer_h, outer_l = outer[0], outer[1]
    a_ref[:, : 2 * LANES] = dot(outer_h, both) + dot(outer_l, both)
    turned = dot(outer_h, jnp.concatenate([taps_h, taps_l], axis=1))
    a_ref[:, 2 * LANES :] = turned[:, :LANES] + turned[:, LANES:] + dot(outer_l, taps_h)
    there_h, there_l = there[0], there[1]
    back_h, back_l = back[0], back[1]

    last = a_ref[rows : rows + 1, :]
    first_row = lax.broadcasted_iota(jnp.int32, (16, 1), 0) == 0

    for start, count in [(k, 64) for k in range(0, rows, 64)] + [(rows, 16)]:
        tr = twist[start : start + count, :LANES]
        ti = twist[start : start + count, LANES:]
        pieces = []
        for number in range(3):
            lanes = slice(number * LANES, (number + 1) * LANES)
            if start == rows:
                ar = jnp.where(first_row, last[:, lanes], 0.0)
                pieces.append(jnp.concatenate([ar * tr, ar * ti], axis=1))
                continue
            ar = a_ref[start : start + count, lanes]
            ai = a_ref[rows + start : rows + start + count, lanes]
            if start == 0:
                row = lax.broadcasted_iota(jnp.int32, (count, 1), 0)
                ai = jnp.where(row == 0, 0.0, ai)
            pieces.append(jnp.concatenate([ar * tr - ai * ti, ar * ti + ai * tr], axis=1))
        z_h, z_l = split(jnp.concatenate(pieces, axis=0))
        spec = dot(z_h, there_h) + dot(z_l, there_h) + dot(z_h, there_l)
        sr, si = spec[:count, :LANES], spec[:count, LANES:]
        gr, gi = spec[count : 2 * count, :LANES], spec[count : 2 * count, LANES:]
        hr, hi = spec[2 * count :, :LANES], spec[2 * count :, LANES:]
        conv = jnp.concatenate([sr * hr - si * hi, sr * hi + si * hr], axis=1)
        back = jnp.concatenate([gr * hr + gi * hi, gi * hr - gr * hi], axis=1)
        corr = jnp.concatenate([gr * sr + gi * si, gi * sr - gr * si], axis=1)
        p_h, p_l = split(jnp.concatenate([conv, back, corr], axis=0))
        v = dot(p_h, back_h) + dot(p_l, back_h) + dot(p_h, back_l)
        for number in range(3):
            vr = v[number * count : (number + 1) * count, :LANES]
            vi = v[number * count : (number + 1) * count, LANES:]
            lanes = slice(number * LANES, (number + 1) * LANES)
            real_h, real_l = split(vr * tr + vi * ti)
            if start == rows:
                u_h[rows : rows + 16, lanes] = jnp.where(first_row, real_h, u_h[rows : rows + 16, lanes])
                u_l[rows : rows + 16, lanes] = jnp.where(first_row, real_l, u_l[rows : rows + 16, lanes])
                continue
            imag_h, imag_l = split(vi * tr - vr * ti)
            u_h[start : start + count, lanes] = real_h
            u_l[start : start + count, lanes] = real_l
            u_h[rows + start : rows + start + count, lanes] = imag_h
            u_l[rows + start : rows + start + count, lanes] = imag_l

    y = jnp.zeros((half, 3 * LANES), jnp.float32)
    mine = pl.ds(pl.multiple_of(core * half, half), half)
    for number, columns in enumerate((first_back, second_back)):
        here = slice(number * rows, (number + 1) * rows)
        columns_h, columns_l = columns[0, mine, :], columns[1, mine, :]
        y += dot(columns_h, u_h[here, :]) + dot(columns_h, u_l[here, :]) + dot(columns_l, u_h[here, :])
    for number in range(3):
        out_ref[:, number * 8 : number * 8 + 8, :] = y[:, number * LANES : (number + 1) * LANES].reshape(chips, SUBLANES, LANES)


def collect_kernel(in_ref, out_ref):
    mine = in_ref[:, 16:, :].reshape(out_ref.shape[1:])
    for place in range(out_ref.shape[0]):
        out_ref[place] = mine


def add_kernel(in_ref, out_ref):
    total = in_ref[0]
    for place in range(1, in_ref.shape[0]):
        total += in_ref[place]
    for place in range(out_ref.shape[0]):
        out_ref[place] = total


def finish_kernel(in_ref, skip_ref, shares_ref, out_ref, back_ref, corr_ref, total_ref):
    channels = corr_ref.shape[0]
    total = shares_ref[0]
    for place in range(1, shares_ref.shape[0]):
        total += shares_ref[place]
    total_ref[...] = total
    for chunk in range(SUBLANES):
        lanes = slice(chunk * LANES, (chunk + 1) * LANES)
        corr_ref[:, lanes] = total_ref[pl.ds(chunk, channels, stride=SUBLANES), :]
        for number, result in enumerate((out_ref, back_ref)):
            conv = in_ref[pl.ds(number * 8 + chunk, channels, stride=24), :]
            result[:, lanes] = (conv + skip_ref[number, :, lanes]).astype(jnp.bfloat16)


def call(kernel, out_shape, operands, scratch=(), spaces=None):
    if spaces is None:
        spaces = [pltpu.VMEM] * len(operands)
    return pl.pallas_call(
        kernel,
        out_shape=out_shape,
        in_specs=[pl.BlockSpec(memory_space=space) for space in spaces],
        out_specs=jax.tree.map(lambda _: pl.BlockSpec(memory_space=pltpu.VMEM), out_shape),
        scratch_shapes=list(scratch),
        compiler_params=pltpu.CompilerParams(vmem_limit_bytes=VMEM_BYTES),
    )(*operands)


def on_device(signal, filter_taps, skip_gain, grad_out):
    channels, tokens = signal.shape
    chips = lax.axis_size("chip")
    ctx = 2 * chips
    assert channels == chips and tokens == SUBLANES * LANES
    length = tokens * ctx
    rows = length // LANES
    outer, *tables = make_tables(rows, ctx, 1.0 / math.sqrt(length))

    in_hbm = [
        pltpu.with_memory_space_constraint(x, pltpu.HBM)
        for x in (signal, grad_out, filter_taps, skip_gain, outer)
    ]
    packed, skip, outer = call(
        pack_kernel,
        (
            pltpu.VMEM((chips * 24, LANES), jnp.float32),
            pltpu.VMEM((2, channels, tokens), jnp.float32),
            pltpu.VMEM(outer.shape, outer.dtype),
        ),
        in_hbm,
        scratch=(
            pltpu.VMEM(signal.shape, signal.dtype),
            pltpu.VMEM(grad_out.shape, grad_out.dtype),
            pltpu.VMEM(filter_taps.shape, filter_taps.dtype),
            pltpu.SMEM(skip_gain.shape, skip_gain.dtype),
            pltpu.SemaphoreType.DMA((5,)),
        ),
        spaces=[pltpu.HBM] * 5,
    )
    spread = lax.all_to_all(packed.reshape(chips, 24, LANES), "chip", 0, 0, tiled=True)
    sequences = lax.all_gather(spread, "core", tiled=True)
    results = call(
        convolve_kernel,
        jax.ShapeDtypeStruct((chips, 24, LANES), jnp.float32),
        (sequences, outer, *tables),
        scratch=(
            pltpu.VMEM((2 * rows, 3 * LANES), jnp.float32),
            pltpu.VMEM((2 * rows, 3 * LANES), jnp.bfloat16),
            pltpu.VMEM((2 * rows, 3 * LANES), jnp.bfloat16),
        ),
    )
    returned = lax.all_to_all(results, "chip", 0, 0, tiled=True)
    shape = (channels * SUBLANES, LANES)
    first, second = lax.axis_size(TP_FIRST), lax.axis_size(TP_SECOND)
    everyone = call(collect_kernel, jax.ShapeDtypeStruct((first, *shape), jnp.float32), (returned,))
    shares = lax.all_to_all(everyone, TP_FIRST, 0, 0, tiled=True)
    everyone = call(add_kernel, jax.ShapeDtypeStruct((second, *shape), jnp.float32), (shares,))
    shares = lax.all_to_all(everyone, TP_SECOND, 0, 0, tiled=True)
    output, grad_signal, grad_filter = call(
        finish_kernel,
        (
            jax.ShapeDtypeStruct((channels, tokens), jnp.bfloat16),
            jax.ShapeDtypeStruct((channels, tokens), jnp.bfloat16),
            jax.ShapeDtypeStruct((channels, tokens), jnp.float32),
        ),
        (returned.reshape(chips * 24, LANES), skip, shares),
        scratch=(pltpu.VMEM(shape, jnp.float32),),
    )
    return (output, grad_signal, grad_filter)


def solution(mesh):
    ctx, tp = mesh.shape["ctx"], mesh.shape["tp"]
    parted = Mesh(mesh.devices.reshape(ctx // 2, 2, 2, tp // 4, 2), (*CTX, *TP))
    in_specs = (P(TP, CTX), P(None, CTX), P(TP), P(TP, CTX))
    out_specs = (P(TP, CTX), P(TP, CTX), P(None, CTX))
    return jax.shard_map(
        on_device, mesh=parted, in_specs=in_specs, out_specs=out_specs, check_vma=False
    )
```

```python
import math

import jax
import jax.numpy as jnp
import ml_dtypes
import numpy as np
from jax import lax
from jax.experimental import pallas as pl
from jax.experimental.pallas import tpu as pltpu
from jax.sharding import Mesh
from jax.sharding import PartitionSpec as P

LANES = 128
SUBLANES = 8
CTX = ("chip", "core")
TP = ("tp_far", "tp_even", "tp_next")
TP_FIRST = ("tp_far", "tp_next")
TP_SECOND = ("tp_even",)
VMEM_BYTES = 24 * 1024 * 1024


def split_table(table):
    high = table.astype(np.float32).astype(ml_dtypes.bfloat16)
    low = (table - high.astype(np.float64)).astype(ml_dtypes.bfloat16)
    return high, low


def make_tables(rows, blocks, scale):
    period = 2 * rows
    padded = period * LANES
    place = np.arange(rows)
    block = place // SUBLANES % (blocks // 2) * 2 + place // (rows // 2)
    a = block * SUBLANES + place % SUBLANES
    f1 = np.arange(rows)
    turn = 2.0 * np.pi * (np.outer(f1, a) % period) / period
    cosines = np.cos(turn)
    sines = -np.sin(turn)
    sines[0] = np.where(a % 2 == 0, 1.0, -1.0)
    outer = np.concatenate([cosines, sines], axis=0)
    weights = np.full((rows,), 2.0)
    weights[0] = 1.0
    outer_back = (outer * np.concatenate([weights, weights])[:, None]).T * (scale / padded)
    b = np.arange(LANES)
    kept = np.arange(rows + 1)
    angle = 2.0 * np.pi * (np.outer(kept, b) % padded) / padded
    twist = np.zeros((rows + 16, 2 * LANES))
    twist[: rows + 1, :LANES] = np.cos(angle)
    twist[: rows + 1, LANES:] = -np.sin(angle)
    inner = 2.0 * np.pi * (np.outer(b, b) % LANES) / LANES
    c, s = np.cos(inner), np.sin(inner)
    inner_there = np.block([[c, -s], [s, c]])
    inner_back = np.block([[c, s], [-s, c]])
    back_columns = np.concatenate(np.split(outer_back, 2 * rows // (2 * LANES), axis=1), axis=0)
    parts = [np.stack(split_table(part)) for part in (outer, inner_there, inner_back, *np.split(back_columns, 2))]
    return (*parts, twist.astype(np.float32))


def split(x):
    high = x.astype(jnp.bfloat16)
    low = (x - high.astype(jnp.float32)).astype(jnp.bfloat16)
    return high, low


def dot(x, y):
    return jnp.dot(x, y, preferred_element_type=jnp.float32)


def pack_kernel(
    signal_hbm, grad_hbm, filter_hbm, gain_hbm, table_hbm,
    out_ref, skip_ref, table_ref,
    signal_ref, grad_ref, filter_ref, gain_ref, sems,
):
    pairs = (
        (signal_hbm, signal_ref),
        (grad_hbm, grad_ref),
        (filter_hbm, filter_ref),
        (gain_hbm, gain_ref),
        (table_hbm, table_ref),
    )
    copies = [pltpu.make_async_copy(source, target, sems.at[k]) for k, (source, target) in enumerate(pairs)]
    for copy in copies:
        copy.start()
    channels = signal_ref.shape[0]
    arrays = []
    for number, ref in enumerate((signal_ref, grad_ref, filter_ref)):
        copies[number].wait()
        arrays.append(ref[...].astype(jnp.float32))
        for chunk in range(SUBLANES):
            lanes = slice(chunk * LANES, (chunk + 1) * LANES)
            out_ref[pl.ds(number * 8 + chunk, channels, stride=24), :] = arrays[number][:, lanes]
    copies[3].wait()
    row = lax.broadcasted_iota(jnp.int32, (channels, 1), 0)
    gains = jnp.zeros((channels, 1), jnp.float32)
    for channel in range(channels):
        gains = jnp.where(row == channel, gain_ref[channel], gains)
    skip_ref[0] = gains * arrays[0]
    skip_ref[1] = gains * arrays[1]
    for copy in copies[4:]:
        copy.wait()


def convolve_kernel(in_ref, outer, there, back, first_back, second_back, twist, out_ref, everyone_ref, a_ref, u_h, u_l):
    chips = out_ref.shape[0]
    half = chips * SUBLANES
    rows = 2 * half
    core = lax.axis_index("core")

    def sequence(number):
        return in_ref[:, number * 8 : number * 8 + 8, :].reshape(rows, LANES)

    both = jnp.concatenate([sequence(0), sequence(1)], axis=1).astype(jnp.bfloat16)
    taps_h, taps_l = split(sequence(2))
    outer_h, outer_l = outer[0], outer[1]
    a_ref[:, : 2 * LANES] = dot(outer_h, both) + dot(outer_l, both)
    turned = dot(outer_h, jnp.concatenate([taps_h, taps_l], axis=1))
    a_ref[:, 2 * LANES :] = turned[:, :LANES] + turned[:, LANES:] + dot(outer_l, taps_h)
    there_h, there_l = there[0], there[1]
    back_h, back_l = back[0], back[1]

    last = a_ref[rows : rows + 1, :]
    first_row = lax.broadcasted_iota(jnp.int32, (16, 1), 0) == 0

    for start, count in [(k, 64) for k in range(0, rows, 64)] + [(rows, 16)]:
        tr = twist[start : start + count, :LANES]
        ti = twist[start : start + count, LANES:]
        pieces = []
        for number in range(3):
            lanes = slice(number * LANES, (number + 1) * LANES)
            if start == rows:
                ar = jnp.where(first_row, last[:, lanes], 0.0)
                pieces.append(jnp.concatenate([ar * tr, ar * ti], axis=1))
                continue
            ar = a_ref[start : start + count, lanes]
            ai = a_ref[rows + start : rows + start + count, lanes]
            if start == 0:
                row = lax.broadcasted_iota(jnp.int32, (count, 1), 0)
                ai = jnp.where(row == 0, 0.0, ai)
            pieces.append(jnp.concatenate([ar * tr - ai * ti, ar * ti + ai * tr], axis=1))
        z_h, z_l = split(jnp.concatenate(pieces, axis=0))
        spec = dot(z_h, there_h) + dot(z_l, there_h) + dot(z_h, there_l)
        sr, si = spec[:count, :LANES], spec[:count, LANES:]
        gr, gi = spec[count : 2 * count, :LANES], spec[count : 2 * count, LANES:]
        hr, hi = spec[2 * count :, :LANES], spec[2 * count :, LANES:]
        conv = jnp.concatenate([sr * hr - si * hi, sr * hi + si * hr], axis=1)
        back = jnp.concatenate([gr * hr + gi * hi, gi * hr - gr * hi], axis=1)
        corr = jnp.concatenate([gr * sr + gi * si, gi * sr - gr * si], axis=1)
        p_h, p_l = split(jnp.concatenate([conv, back, corr], axis=0))
        v = dot(p_h, back_h) + dot(p_l, back_h) + dot(p_h, back_l)
        for number in range(3):
            vr = v[number * count : (number + 1) * count, :LANES]
            vi = v[number * count : (number + 1) * count, LANES:]
            lanes = slice(number * LANES, (number + 1) * LANES)
            real_h, real_l = split(vr * tr + vi * ti)
            if start == rows:
                u_h[rows : rows + 16, lanes] = jnp.where(first_row, real_h, u_h[rows : rows + 16, lanes])
                u_l[rows : rows + 16, lanes] = jnp.where(first_row, real_l, u_l[rows : rows + 16, lanes])
                continue
            imag_h, imag_l = split(vi * tr - vr * ti)
            u_h[start : start + count, lanes] = real_h
            u_l[start : start + count, lanes] = real_l
            u_h[rows + start : rows + start + count, lanes] = imag_h
            u_l[rows + start : rows + start + count, lanes] = imag_l

    y = jnp.zeros((half, 3 * LANES), jnp.float32)
    mine = pl.ds(pl.multiple_of(core * half, half), half)
    for number, columns in enumerate((first_back, second_back)):
        here = slice(number * rows, (number + 1) * rows)
        columns_h, columns_l = columns[0, mine, :], columns[1, mine, :]
        y += dot(columns_h, u_h[here, :]) + dot(columns_h, u_l[here, :]) + dot(columns_l, u_h[here, :])
    for number in range(2):
        out_ref[:, number * 8 : number * 8 + 8, :] = y[:, number * LANES : (number + 1) * LANES].reshape(chips, SUBLANES, LANES)
    for place in range(everyone_ref.shape[0]):
        everyone_ref[place] = y[:, 2 * LANES :]


def sum_of(in_ref):
    total = in_ref[0]
    for place in range(1, in_ref.shape[0]):
        total += in_ref[place]
    return total


def collect_kernel(in_ref, out_ref):
    mine = in_ref[:, 16:, :].reshape(out_ref.shape[1:])
    for place in range(out_ref.shape[0]):
        out_ref[place] = mine


def join_kernel(in_ref, shares_ref, out_ref):
    out_ref[:, :16, :] = in_ref[...]
    out_ref[:, 16:, :] = sum_of(shares_ref).reshape(out_ref.shape[0], SUBLANES, LANES)


def finish_kernel(in_ref, skip_ref, shares_ref, out_ref, back_ref, corr_ref, total_ref):
    channels = corr_ref.shape[0]
    total = shares_ref[0]
    for place in range(1, shares_ref.shape[0]):
        total += shares_ref[place]
    total_ref[...] = total
    for chunk in range(SUBLANES):
        lanes = slice(chunk * LANES, (chunk + 1) * LANES)
        corr_ref[:, lanes] = total_ref[pl.ds(chunk, channels, stride=SUBLANES), :]
        for number, result in enumerate((out_ref, back_ref)):
            conv = in_ref[pl.ds(number * 8 + chunk, channels, stride=24), :]
            result[:, lanes] = (conv + skip_ref[number, :, lanes]).astype(jnp.bfloat16)


def call(kernel, out_shape, operands, scratch=(), spaces=None):
    if spaces is None:
        spaces = [pltpu.VMEM] * len(operands)
    return pl.pallas_call(
        kernel,
        out_shape=out_shape,
        in_specs=[pl.BlockSpec(memory_space=space) for space in spaces],
        out_specs=jax.tree.map(lambda _: pl.BlockSpec(memory_space=pltpu.VMEM), out_shape),
        scratch_shapes=list(scratch),
        compiler_params=pltpu.CompilerParams(vmem_limit_bytes=VMEM_BYTES),
    )(*operands)


def on_device(signal, filter_taps, skip_gain, grad_out):
    channels, tokens = signal.shape
    chips = lax.axis_size("chip")
    ctx = 2 * chips
    assert channels == chips and tokens == SUBLANES * LANES
    length = tokens * ctx
    rows = length // LANES
    outer, *tables = make_tables(rows, ctx, 1.0 / math.sqrt(length))

    in_hbm = [
        pltpu.with_memory_space_constraint(x, pltpu.HBM)
        for x in (signal, grad_out, filter_taps, skip_gain, outer)
    ]
    packed, skip, outer = call(
        pack_kernel,
        (
            pltpu.VMEM((chips * 24, LANES), jnp.float32),
            pltpu.VMEM((2, channels, tokens), jnp.float32),
            pltpu.VMEM(outer.shape, outer.dtype),
        ),
        in_hbm,
        scratch=(
            pltpu.VMEM(signal.shape, signal.dtype),
            pltpu.VMEM(grad_out.shape, grad_out.dtype),
            pltpu.VMEM(filter_taps.shape, filter_taps.dtype),
            pltpu.SMEM(skip_gain.shape, skip_gain.dtype),
            pltpu.SemaphoreType.DMA((5,)),
        ),
        spaces=[pltpu.HBM] * 5,
    )
    spread = lax.all_to_all(packed.reshape(chips, 24, LANES), "chip", 0, 0, tiled=True)
    sequences = lax.all_gather(spread, "core", tiled=True)
    first, second = lax.axis_size(TP_FIRST), lax.axis_size(TP_SECOND)
    results, everyone = call(
        convolve_kernel,
        (
            pltpu.VMEM((chips, 16, LANES), jnp.float32),
            pltpu.VMEM((first, rows // 2, LANES), jnp.float32),
        ),
        (sequences, outer, *tables),
        scratch=(
            pltpu.VMEM((2 * rows, 3 * LANES), jnp.float32),
            pltpu.VMEM((2 * rows, 3 * LANES), jnp.bfloat16),
            pltpu.VMEM((2 * rows, 3 * LANES), jnp.bfloat16),
        ),
    )
    shares = lax.all_to_all(everyone, TP_FIRST, 0, 0, tiled=True)
    joined = call(join_kernel, jax.ShapeDtypeStruct((chips, 24, LANES), jnp.float32), (results, shares))
    returned = lax.all_to_all(joined, "chip", 0, 0, tiled=True)
    shape = (channels * SUBLANES, LANES)
    everyone = call(collect_kernel, jax.ShapeDtypeStruct((second, *shape), jnp.float32), (returned,))
    shares = lax.all_to_all(everyone, TP_SECOND, 0, 0, tiled=True)
    output, grad_signal, grad_filter = call(
        finish_kernel,
        (
            jax.ShapeDtypeStruct((channels, tokens), jnp.bfloat16),
            jax.ShapeDtypeStruct((channels, tokens), jnp.bfloat16),
            jax.ShapeDtypeStruct((channels, tokens), jnp.float32),
        ),
        (returned.reshape(chips * 24, LANES), skip, shares),
        scratch=(pltpu.VMEM(shape, jnp.float32),),
    )
    return (output, grad_signal, grad_filter)


def solution(mesh):
    ctx, tp = mesh.shape["ctx"], mesh.shape["tp"]
    parted = Mesh(mesh.devices.reshape(ctx // 2, 2, 2, tp // 4, 2), (*CTX, *TP))
    in_specs = (P(TP, CTX), P(None, CTX), P(TP), P(TP, CTX))
    out_specs = (P(TP, CTX), P(TP, CTX), P(None, CTX))
    return jax.shard_map(
        on_device, mesh=parted, in_specs=in_specs, out_specs=out_specs, check_vma=False
    )
```

```python
import functools
import math

import jax
import jax.numpy as jnp
import ml_dtypes
import numpy as np
from jax import lax
from jax.experimental import pallas as pl
from jax.experimental.pallas import tpu as pltpu
from jax.sharding import Mesh
from jax.sharding import PartitionSpec as P

LANES = 128
SUBLANES = 8
CTX = ("chip", "core")
TP = ("tp_far", "tp_even", "tp_next")
TP_FIRST = ("tp_far", "tp_next")
TP_SECOND = ("tp_even",)
VMEM_BYTES = 24 * 1024 * 1024


def split_table(table):
    high = table.astype(np.float32).astype(ml_dtypes.bfloat16)
    low = (table - high.astype(np.float64)).astype(ml_dtypes.bfloat16)
    return high, low


def make_tables(rows, blocks):
    period = 2 * rows
    padded = period * LANES
    place = np.arange(rows)
    block = place // SUBLANES % (blocks // 2) * 2 + place // (rows // 2)
    a = block * SUBLANES + place % SUBLANES
    f1 = np.arange(rows)
    turn = 2.0 * np.pi * (np.outer(f1, a) % period) / period
    cosines = np.cos(turn)
    sines = -np.sin(turn)
    sines[0] = np.where(a % 2 == 0, 1.0, -1.0)
    outer = np.concatenate([cosines, sines], axis=0)
    b = np.arange(LANES)
    kept = np.arange(rows + 1)
    angle = 2.0 * np.pi * (np.outer(kept, b) % padded) / padded
    twist = np.zeros((rows + 16, 2 * LANES))
    twist[: rows + 1, :LANES] = np.cos(angle)
    twist[: rows + 1, LANES:] = -np.sin(angle)
    inner = 2.0 * np.pi * (np.outer(b, b) % LANES) / LANES
    c, s = np.cos(inner), np.sin(inner)
    inner_there = np.block([[c, -s], [s, c]])
    inner_back = inner_there.T
    return (
        *split_table(outer), np.stack(split_table(inner_there)), np.stack(split_table(inner_back)), twist.astype(np.float32)
    )


def split(x):
    high = x.astype(jnp.bfloat16)
    low = (x - high.astype(jnp.float32)).astype(jnp.bfloat16)
    return high, low


def dot(x, y, over=(1, 0)):
    return lax.dot_general(x, y, (((over[0],), (over[1],)), ((), ())), preferred_element_type=jnp.float32)


def pack_kernel(
    signal_hbm, grad_hbm, filter_hbm, gain_hbm, table_hbm,
    out_ref, skip_ref, table_ref,
    signal_ref, grad_ref, filter_ref, gain_ref, sems,
):
    pairs = (
        (signal_hbm, signal_ref),
        (grad_hbm, grad_ref),
        (filter_hbm, filter_ref),
        (gain_hbm, gain_ref),
        (table_hbm, table_ref),
    )
    copies = [pltpu.make_async_copy(source, target, sems.at[k]) for k, (source, target) in enumerate(pairs)]
    for copy in copies:
        copy.start()
    channels = signal_ref.shape[0]
    arrays = []
    for number, ref in enumerate((signal_ref, grad_ref, filter_ref)):
        copies[number].wait()
        arrays.append(ref[...].astype(jnp.float32))
        for chunk in range(SUBLANES):
            lanes = slice(chunk * LANES, (chunk + 1) * LANES)
            out_ref[pl.ds(number * 8 + chunk, channels, stride=24), :] = arrays[number][:, lanes]
    copies[3].wait()
    row = lax.broadcasted_iota(jnp.int32, (channels, 1), 0)
    gains = jnp.zeros((channels, 1), jnp.float32)
    for channel in range(channels):
        gains = jnp.where(row == channel, gain_ref[channel], gains)
    skip_ref[0] = gains * arrays[0]
    skip_ref[1] = gains * arrays[1]
    copies[4].wait()


def convolve_kernel(in_ref, outer_ref_h, outer_ref_l, there, back, twist, out_ref, a_ref, u_h, u_l, *, scale):
    chips = out_ref.shape[0]
    half = chips * SUBLANES
    rows = 2 * half
    core = lax.axis_index("core")

    def sequence(number):
        return in_ref[:, number * 8 : number * 8 + 8, :].reshape(rows, LANES)

    both = jnp.concatenate([sequence(0), sequence(1)], axis=1).astype(jnp.bfloat16)
    taps_h, taps_l = split(sequence(2))
    outer_h, outer_l = outer_ref_h[...], outer_ref_l[...]
    a_ref[:, : 2 * LANES] = dot(outer_h, both) + dot(outer_l, both)
    turned = dot(outer_h, jnp.concatenate([taps_h, taps_l], axis=1))
    a_ref[:, 2 * LANES :] = turned[:, :LANES] + turned[:, LANES:] + dot(outer_l, taps_h)
    there_h, there_l = there[0], there[1]
    back_h, back_l = back[0], back[1]

    last = a_ref[rows : rows + 1, :]
    first_row = lax.broadcasted_iota(jnp.int32, (16, 1), 0) == 0

    for start, count in [(k, 64) for k in range(0, rows, 64)] + [(rows, 16)]:
        tr = twist[start : start + count, :LANES]
        ti = twist[start : start + count, LANES:]
        pieces = []
        for number in range(3):
            lanes = slice(number * LANES, (number + 1) * LANES)
            if start == rows:
                ar = jnp.where(first_row, last[:, lanes], 0.0)
                pieces.append(jnp.concatenate([ar * tr, ar * ti], axis=1))
                continue
            ar = a_ref[start : start + count, lanes]
            ai = a_ref[rows + start : rows + start + count, lanes]
            if start == 0:
                row = lax.broadcasted_iota(jnp.int32, (count, 1), 0)
                ai = jnp.where(row == 0, 0.0, ai)
            pieces.append(jnp.concatenate([ar * tr - ai * ti, ar * ti + ai * tr], axis=1))
        z_h, z_l = split(jnp.concatenate(pieces, axis=0))
        spec = dot(z_h, there_h) + dot(z_l, there_h) + dot(z_h, there_l)
        sr, si = spec[:count, :LANES], spec[:count, LANES:]
        gr, gi = spec[count : 2 * count, :LANES], spec[count : 2 * count, LANES:]
        hr, hi = spec[2 * count :, :LANES], spec[2 * count :, LANES:]
        conv = jnp.concatenate([sr * hr - si * hi, sr * hi + si * hr], axis=1)
        back = jnp.concatenate([gr * hr + gi * hi, gi * hr - gr * hi], axis=1)
        corr = jnp.concatenate([gr * sr + gi * si, gi * sr - gr * si], axis=1)
        p_h, p_l = split(jnp.concatenate([conv, back, corr], axis=0))
        v = dot(p_h, back_h) + dot(p_l, back_h) + dot(p_h, back_l)
        if start in (0, rows):
            weight = jnp.where(lax.broadcasted_iota(jnp.int32, (count, 1), 0) == 0, 0.5, 1.0)
            tr, ti = tr * weight, ti * weight
        for number in range(3):
            vr = v[number * count : (number + 1) * count, :LANES]
            vi = v[number * count : (number + 1) * count, LANES:]
            lanes = slice(number * LANES, (number + 1) * LANES)
            real_h, real_l = split(vr * tr + vi * ti)
            if start == rows:
                u_h[rows : rows + 16, lanes] = jnp.where(first_row, real_h, u_h[rows : rows + 16, lanes])
                u_l[rows : rows + 16, lanes] = jnp.where(first_row, real_l, u_l[rows : rows + 16, lanes])
                continue
            imag_h, imag_l = split(vi * tr - vr * ti)
            u_h[start : start + count, lanes] = real_h
            u_l[start : start + count, lanes] = real_l
            u_h[rows + start : rows + start + count, lanes] = imag_h
            u_l[rows + start : rows + start + count, lanes] = imag_l

    mine = pl.ds(pl.multiple_of(core * half, half), half)
    columns_h, columns_l = outer_ref_h[:, mine], outer_ref_l[:, mine]
    y = dot(columns_h, u_h[...], (0, 0)) + dot(columns_h, u_l[...], (0, 0)) + dot(columns_l, u_h[...], (0, 0))
    y *= scale
    for number in range(3):
        out_ref[:, number * 8 : number * 8 + 8, :] = y[:, number * LANES : (number + 1) * LANES].reshape(chips, SUBLANES, LANES)


def collect_kernel(in_ref, out_ref):
    mine = in_ref[:, 16:, :].reshape(out_ref.shape[1:])
    for place in range(out_ref.shape[0]):
        out_ref[place] = mine


def add_kernel(in_ref, out_ref):
    total = in_ref[0]
    for place in range(1, in_ref.shape[0]):
        total += in_ref[place]
    for place in range(out_ref.shape[0]):
        out_ref[place] = total


def finish_kernel(in_ref, skip_ref, shares_ref, out_ref, back_ref, corr_ref, total_ref):
    channels = corr_ref.shape[0]
    total = shares_ref[0]
    for place in range(1, shares_ref.shape[0]):
        total += shares_ref[place]
    total_ref[...] = total
    for chunk in range(SUBLANES):
        lanes = slice(chunk * LANES, (chunk + 1) * LANES)
        corr_ref[:, lanes] = total_ref[pl.ds(chunk, channels, stride=SUBLANES), :]
        for number, result in enumerate((out_ref, back_ref)):
            conv = in_ref[pl.ds(number * 8 + chunk, channels, stride=24), :]
            result[:, lanes] = (conv + skip_ref[number, :, lanes]).astype(jnp.bfloat16)


def call(kernel, out_shape, operands, scratch=(), spaces=None):
    if spaces is None:
        spaces = [pltpu.VMEM] * len(operands)
    return pl.pallas_call(
        kernel,
        out_shape=out_shape,
        in_specs=[pl.BlockSpec(memory_space=space) for space in spaces],
        out_specs=jax.tree.map(lambda _: pl.BlockSpec(memory_space=pltpu.VMEM), out_shape),
        scratch_shapes=list(scratch),
        compiler_params=pltpu.CompilerParams(vmem_limit_bytes=VMEM_BYTES),
    )(*operands)


def on_device(signal, filter_taps, skip_gain, grad_out):
    channels, tokens = signal.shape
    chips = lax.axis_size("chip")
    ctx = 2 * chips
    assert channels == chips and tokens == SUBLANES * LANES
    length = tokens * ctx
    rows = length // LANES
    outer_h, outer_l, there, back, twist = make_tables(rows, ctx)

    in_hbm = [
        pltpu.with_memory_space_constraint(x, pltpu.HBM)
        for x in (signal, grad_out, filter_taps, skip_gain, there)
    ]
    packed, skip, there = call(
        pack_kernel,
        (
            pltpu.VMEM((chips * 24, LANES), jnp.float32),
            pltpu.VMEM((2, channels, tokens), jnp.float32),
            pltpu.VMEM(there.shape, there.dtype),
        ),
        in_hbm,
        scratch=(
            pltpu.VMEM(signal.shape, signal.dtype),
            pltpu.VMEM(grad_out.shape, grad_out.dtype),
            pltpu.VMEM(filter_taps.shape, filter_taps.dtype),
            pltpu.SMEM(skip_gain.shape, skip_gain.dtype),
            pltpu.SemaphoreType.DMA((5,)),
        ),
        spaces=[pltpu.HBM] * 5,
    )
    spread = lax.all_to_all(packed.reshape(chips, 24, LANES), "chip", 0, 0, tiled=True)
    sequences = lax.all_gather(spread, "core", tiled=True)
    results = call(
        functools.partial(convolve_kernel, scale=2.0 / (2 * length * math.sqrt(length))),
        jax.ShapeDtypeStruct((chips, 24, LANES), jnp.float32),
        (sequences, outer_h, outer_l, there, back, twist),
        scratch=(
            pltpu.VMEM((2 * rows, 3 * LANES), jnp.float32),
            pltpu.VMEM((2 * rows, 3 * LANES), jnp.bfloat16),
            pltpu.VMEM((2 * rows, 3 * LANES), jnp.bfloat16),
        ),
    )
    returned = lax.all_to_all(results, "chip", 0, 0, tiled=True)
    shape = (channels * SUBLANES, LANES)
    first, second = lax.axis_size(TP_FIRST), lax.axis_size(TP_SECOND)
    everyone = call(collect_kernel, jax.ShapeDtypeStruct((first, *shape), jnp.float32), (returned,))
    shares = lax.all_to_all(everyone, TP_FIRST, 0, 0, tiled=True)
    everyone = call(add_kernel, jax.ShapeDtypeStruct((second, *shape), jnp.float32), (shares,))
    shares = lax.all_to_all(everyone, TP_SECOND, 0, 0, tiled=True)
    output, grad_signal, grad_filter = call(
        finish_kernel,
        (
            jax.ShapeDtypeStruct((channels, tokens), jnp.bfloat16),
            jax.ShapeDtypeStruct((channels, tokens), jnp.bfloat16),
            jax.ShapeDtypeStruct((channels, tokens), jnp.float32),
        ),
        (returned.reshape(chips * 24, LANES), skip, shares),
        scratch=(pltpu.VMEM(shape, jnp.float32),),
    )
    return (output, grad_signal, grad_filter)


def solution(mesh):
    ctx, tp = mesh.shape["ctx"], mesh.shape["tp"]
    parted = Mesh(mesh.devices.reshape(ctx // 2, 2, 2, tp // 4, 2), (*CTX, *TP))
    in_specs = (P(TP, CTX), P(None, CTX), P(TP), P(TP, CTX))
    out_specs = (P(TP, CTX), P(TP, CTX), P(None, CTX))
    return jax.shard_map(
        on_device, mesh=parted, in_specs=in_specs, out_specs=out_specs, check_vma=False
    )
```

```python
import functools
import math

import jax
import jax.numpy as jnp
import ml_dtypes
import numpy as np
from jax import lax
from jax.experimental import pallas as pl
from jax.experimental.pallas import tpu as pltpu
from jax.sharding import Mesh
from jax.sharding import PartitionSpec as P

LANES = 128
SUBLANES = 8
CTX = ("chip", "core")
TP = ("tp_far", "tp_even", "tp_next")
TP_FIRST = ("tp_far", "tp_next")
TP_SECOND = ("tp_even",)
VMEM_BYTES = 24 * 1024 * 1024


def split_table(table):
    high = table.astype(np.float32).astype(ml_dtypes.bfloat16)
    low = (table - high.astype(np.float64)).astype(ml_dtypes.bfloat16)
    return high, low


def make_tables(rows, blocks):
    period = 2 * rows
    padded = period * LANES
    place = np.arange(rows)
    block = place // SUBLANES % (blocks // 2) * 2 + place // (rows // 2)
    a = block * SUBLANES + place % SUBLANES
    f1 = np.arange(rows)
    turn = 2.0 * np.pi * (np.outer(f1, a) % period) / period
    cosines = np.cos(turn)
    sines = -np.sin(turn)
    sines[0] = np.where(a % 2 == 0, 1.0, -1.0)
    outer = np.concatenate([cosines, sines], axis=0)
    b = np.arange(LANES)
    kept = np.arange(rows + 1)
    angle = 2.0 * np.pi * (np.outer(kept, b) % padded) / padded
    twist = np.zeros((rows + 16, 2 * LANES))
    twist[: rows + 1, :LANES] = np.cos(angle)
    twist[: rows + 1, LANES:] = -np.sin(angle)
    inner = 2.0 * np.pi * (np.outer(b, b) % LANES) / LANES
    c, s = np.cos(inner), np.sin(inner)
    inner_there = np.block([[c, -s], [s, c]])
    inner_back = inner_there.T
    return (
        *split_table(outer), np.stack(split_table(inner_there)), np.stack(split_table(inner_back)), twist.astype(np.float32)
    )


def split(x):
    high = x.astype(jnp.bfloat16)
    low = (x - high.astype(jnp.float32)).astype(jnp.bfloat16)
    return high, low


def dot(x, y, over=(1, 0)):
    return lax.dot_general(x, y, (((over[0],), (over[1],)), ((), ())), preferred_element_type=jnp.float32)


def pack_kernel(
    signal_hbm, grad_hbm, filter_hbm, gain_hbm, table_hbm,
    out_ref, skip_ref, table_ref,
    signal_ref, grad_ref, filter_ref, gain_ref, sems,
):
    pairs = (
        (signal_hbm, signal_ref),
        (grad_hbm, grad_ref),
        (filter_hbm, filter_ref),
        (gain_hbm, gain_ref),
        (table_hbm, table_ref),
    )
    copies = [pltpu.make_async_copy(source, target, sems.at[k]) for k, (source, target) in enumerate(pairs)]
    for copy in copies:
        copy.start()
    channels = signal_ref.shape[0]
    arrays = []
    for number, ref in enumerate((signal_ref, grad_ref, filter_ref)):
        copies[number].wait()
        arrays.append(ref[...].astype(jnp.float32))
        for chunk in range(SUBLANES):
            lanes = slice(chunk * LANES, (chunk + 1) * LANES)
            out_ref[pl.ds(number * 8 + chunk, channels, stride=24), :] = arrays[number][:, lanes]
    copies[3].wait()
    row = lax.broadcasted_iota(jnp.int32, (channels, 1), 0)
    gains = jnp.zeros((channels, 1), jnp.float32)
    for channel in range(channels):
        gains = jnp.where(row == channel, gain_ref[channel], gains)
    skip_ref[0] = gains * arrays[0]
    skip_ref[1] = gains * arrays[1]
    copies[4].wait()


def convolve_kernel(in_ref, outer_ref_h, outer_ref_l, there, back, twist, out_ref, everyone_ref, a_ref, u_h, u_l, *, scale):
    chips = out_ref.shape[0]
    half = chips * SUBLANES
    rows = 2 * half
    core = lax.axis_index("core")

    def sequence(number):
        return in_ref[:, number * 8 : number * 8 + 8, :].reshape(rows, LANES)

    both = jnp.concatenate([sequence(0), sequence(1)], axis=1).astype(jnp.bfloat16)
    taps_h, taps_l = split(sequence(2))
    outer_h, outer_l = outer_ref_h[...], outer_ref_l[...]
    a_ref[:, : 2 * LANES] = dot(outer_h, both) + dot(outer_l, both)
    turned = dot(outer_h, jnp.concatenate([taps_h, taps_l], axis=1))
    a_ref[:, 2 * LANES :] = turned[:, :LANES] + turned[:, LANES:] + dot(outer_l, taps_h)
    there_h, there_l = there[0], there[1]
    back_h, back_l = back[0], back[1]

    last = a_ref[rows : rows + 1, :]
    first_row = lax.broadcasted_iota(jnp.int32, (16, 1), 0) == 0

    for start, count in [(k, 64) for k in range(0, rows, 64)] + [(rows, 16)]:
        tr = twist[start : start + count, :LANES]
        ti = twist[start : start + count, LANES:]
        pieces = []
        for number in range(3):
            lanes = slice(number * LANES, (number + 1) * LANES)
            if start == rows:
                ar = jnp.where(first_row, last[:, lanes], 0.0)
                pieces.append(jnp.concatenate([ar * tr, ar * ti], axis=1))
                continue
            ar = a_ref[start : start + count, lanes]
            ai = a_ref[rows + start : rows + start + count, lanes]
            if start == 0:
                row = lax.broadcasted_iota(jnp.int32, (count, 1), 0)
                ai = jnp.where(row == 0, 0.0, ai)
            pieces.append(jnp.concatenate([ar * tr - ai * ti, ar * ti + ai * tr], axis=1))
        z_h, z_l = split(jnp.concatenate(pieces, axis=0))
        spec = dot(z_h, there_h) + dot(z_l, there_h) + dot(z_h, there_l)
        sr, si = spec[:count, :LANES], spec[:count, LANES:]
        gr, gi = spec[count : 2 * count, :LANES], spec[count : 2 * count, LANES:]
        hr, hi = spec[2 * count :, :LANES], spec[2 * count :, LANES:]
        conv = jnp.concatenate([sr * hr - si * hi, sr * hi + si * hr], axis=1)
        back = jnp.concatenate([gr * hr + gi * hi, gi * hr - gr * hi], axis=1)
        corr = jnp.concatenate([gr * sr + gi * si, gi * sr - gr * si], axis=1)
        p_h, p_l = split(jnp.concatenate([conv, back, corr], axis=0))
        v = dot(p_h, back_h) + dot(p_l, back_h) + dot(p_h, back_l)
        if start in (0, rows):
            weight = jnp.where(lax.broadcasted_iota(jnp.int32, (count, 1), 0) == 0, 0.5, 1.0)
            tr, ti = tr * weight, ti * weight
        for number in range(3):
            vr = v[number * count : (number + 1) * count, :LANES]
            vi = v[number * count : (number + 1) * count, LANES:]
            lanes = slice(number * LANES, (number + 1) * LANES)
            real_h, real_l = split(vr * tr + vi * ti)
            if start == rows:
                u_h[rows : rows + 16, lanes] = jnp.where(first_row, real_h, u_h[rows : rows + 16, lanes])
                u_l[rows : rows + 16, lanes] = jnp.where(first_row, real_l, u_l[rows : rows + 16, lanes])
                continue
            imag_h, imag_l = split(vi * tr - vr * ti)
            u_h[start : start + count, lanes] = real_h
            u_l[start : start + count, lanes] = real_l
            u_h[rows + start : rows + start + count, lanes] = imag_h
            u_l[rows + start : rows + start + count, lanes] = imag_l

    mine = pl.ds(pl.multiple_of(core * half, half), half)
    columns_h, columns_l = outer_ref_h[:, mine], outer_ref_l[:, mine]
    y = dot(columns_h, u_h[...], (0, 0)) + dot(columns_h, u_l[...], (0, 0)) + dot(columns_l, u_h[...], (0, 0))
    y *= scale
    for number in range(2):
        out_ref[:, number * 8 : number * 8 + 8, :] = y[:, number * LANES : (number + 1) * LANES].reshape(chips, SUBLANES, LANES)
    for place in range(everyone_ref.shape[0]):
        everyone_ref[place] = y[:, 2 * LANES :]


def sum_of(in_ref):
    total = in_ref[0]
    for place in range(1, in_ref.shape[0]):
        total += in_ref[place]
    return total


def collect_kernel(in_ref, out_ref):
    mine = in_ref[:, 16:, :].reshape(out_ref.shape[1:])
    for place in range(out_ref.shape[0]):
        out_ref[place] = mine


def join_kernel(in_ref, shares_ref, out_ref):
    out_ref[:, :16, :] = in_ref[...]
    out_ref[:, 16:, :] = sum_of(shares_ref).reshape(out_ref.shape[0], SUBLANES, LANES)


def finish_kernel(in_ref, skip_ref, shares_ref, out_ref, back_ref, corr_ref, total_ref):
    channels = corr_ref.shape[0]
    total = shares_ref[0]
    for place in range(1, shares_ref.shape[0]):
        total += shares_ref[place]
    total_ref[...] = total
    for chunk in range(SUBLANES):
        lanes = slice(chunk * LANES, (chunk + 1) * LANES)
        corr_ref[:, lanes] = total_ref[pl.ds(chunk, channels, stride=SUBLANES), :]
        for number, result in enumerate((out_ref, back_ref)):
            conv = in_ref[pl.ds(number * 8 + chunk, channels, stride=24), :]
            result[:, lanes] = (conv + skip_ref[number, :, lanes]).astype(jnp.bfloat16)


def call(kernel, out_shape, operands, scratch=(), spaces=None):
    if spaces is None:
        spaces = [pltpu.VMEM] * len(operands)
    return pl.pallas_call(
        kernel,
        out_shape=out_shape,
        in_specs=[pl.BlockSpec(memory_space=space) for space in spaces],
        out_specs=jax.tree.map(lambda _: pl.BlockSpec(memory_space=pltpu.VMEM), out_shape),
        scratch_shapes=list(scratch),
        compiler_params=pltpu.CompilerParams(vmem_limit_bytes=VMEM_BYTES),
    )(*operands)


def on_device(signal, filter_taps, skip_gain, grad_out):
    channels, tokens = signal.shape
    chips = lax.axis_size("chip")
    ctx = 2 * chips
    assert channels == chips and tokens == SUBLANES * LANES
    length = tokens * ctx
    rows = length // LANES
    outer_h, outer_l, there, back, twist = make_tables(rows, ctx)

    in_hbm = [
        pltpu.with_memory_space_constraint(x, pltpu.HBM)
        for x in (signal, grad_out, filter_taps, skip_gain, there)
    ]
    packed, skip, there = call(
        pack_kernel,
        (
            pltpu.VMEM((chips * 24, LANES), jnp.float32),
            pltpu.VMEM((2, channels, tokens), jnp.float32),
            pltpu.VMEM(there.shape, there.dtype),
        ),
        in_hbm,
        scratch=(
            pltpu.VMEM(signal.shape, signal.dtype),
            pltpu.VMEM(grad_out.shape, grad_out.dtype),
            pltpu.VMEM(filter_taps.shape, filter_taps.dtype),
            pltpu.SMEM(skip_gain.shape, skip_gain.dtype),
            pltpu.SemaphoreType.DMA((5,)),
        ),
        spaces=[pltpu.HBM] * 5,
    )
    spread = lax.all_to_all(packed.reshape(chips, 24, LANES), "chip", 0, 0, tiled=True)
    sequences = lax.all_gather(spread, "core", tiled=True)
    first, second = lax.axis_size(TP_FIRST), lax.axis_size(TP_SECOND)
    results, everyone = call(
        functools.partial(convolve_kernel, scale=2.0 / (2 * length * math.sqrt(length))),
        (
            pltpu.VMEM((chips, 16, LANES), jnp.float32),
            pltpu.VMEM((first, rows // 2, LANES), jnp.float32),
        ),
        (sequences, outer_h, outer_l, there, back, twist),
        scratch=(
            pltpu.VMEM((2 * rows, 3 * LANES), jnp.float32),
            pltpu.VMEM((2 * rows, 3 * LANES), jnp.bfloat16),
            pltpu.VMEM((2 * rows, 3 * LANES), jnp.bfloat16),
        ),
    )
    shares = lax.all_to_all(everyone, TP_FIRST, 0, 0, tiled=True)
    joined = call(join_kernel, jax.ShapeDtypeStruct((chips, 24, LANES), jnp.float32), (results, shares))
    returned = lax.all_to_all(joined, "chip", 0, 0, tiled=True)
    shape = (channels * SUBLANES, LANES)
    everyone = call(collect_kernel, jax.ShapeDtypeStruct((second, *shape), jnp.float32), (returned,))
    shares = lax.all_to_all(everyone, TP_SECOND, 0, 0, tiled=True)
    output, grad_signal, grad_filter = call(
        finish_kernel,
        (
            jax.ShapeDtypeStruct((channels, tokens), jnp.bfloat16),
            jax.ShapeDtypeStruct((channels, tokens), jnp.bfloat16),
            jax.ShapeDtypeStruct((channels, tokens), jnp.float32),
        ),
        (returned.reshape(chips * 24, LANES), skip, shares),
        scratch=(pltpu.VMEM(shape, jnp.float32),),
    )
    return (output, grad_signal, grad_filter)


def solution(mesh):
    ctx, tp = mesh.shape["ctx"], mesh.shape["tp"]
    parted = Mesh(mesh.devices.reshape(ctx // 2, 2, 2, tp // 4, 2), (*CTX, *TP))
    in_specs = (P(TP, CTX), P(None, CTX), P(TP), P(TP, CTX))
    out_specs = (P(TP, CTX), P(TP, CTX), P(None, CTX))
    return jax.shard_map(
        on_device, mesh=parted, in_specs=in_specs, out_specs=out_specs, check_vma=False
    )
```

```python
import functools
import math

import jax
import jax.numpy as jnp
import ml_dtypes
import numpy as np
from jax import lax
from jax.experimental import pallas as pl
from jax.experimental.pallas import tpu as pltpu
from jax.sharding import Mesh
from jax.sharding import PartitionSpec as P

LANES = 128
SUBLANES = 8
CTX = ("x_lo", "z", "core")
CHIPS = ("z", "x_lo")
TP = ("tp_far", "tp_even", "tp_next")
TP_FIRST = ("tp_far", "tp_next")
TP_SECOND = ("tp_even",)
VMEM_BYTES = 24 * 1024 * 1024


def split_table(table):
    high = table.astype(np.float32).astype(ml_dtypes.bfloat16)
    low = (table - high.astype(np.float64)).astype(ml_dtypes.bfloat16)
    return high, low


def make_tables(rows, blocks):
    period = 2 * rows
    padded = period * LANES
    place = np.arange(rows)
    member = place // SUBLANES % (blocks // 2)
    chip = member % 2 * (blocks // 4) + member // 2
    block = chip * 2 + place // (rows // 2)
    a = block * SUBLANES + place % SUBLANES
    f1 = np.arange(rows)
    turn = 2.0 * np.pi * (np.outer(f1, a) % period) / period
    cosines = np.cos(turn)
    sines = -np.sin(turn)
    sines[0] = np.where(a % 2 == 0, 1.0, -1.0)
    outer = np.concatenate([cosines, sines], axis=0)
    b = np.arange(LANES)
    kept = np.arange(rows + 1)
    angle = 2.0 * np.pi * (np.outer(kept, b) % padded) / padded
    twist = np.zeros((rows + 16, 2 * LANES))
    twist[: rows + 1, :LANES] = np.cos(angle)
    twist[: rows + 1, LANES:] = -np.sin(angle)
    inner = 2.0 * np.pi * (np.outer(b, b) % LANES) / LANES
    c, s = np.cos(inner), np.sin(inner)
    inner_there = np.block([[c, -s], [s, c]])
    inner_back = inner_there.T
    return (
        *split_table(outer), np.stack(split_table(inner_there)), np.stack(split_table(inner_back)), twist.astype(np.float32)
    )


def split(x):
    high = x.astype(jnp.bfloat16)
    low = (x - high.astype(jnp.float32)).astype(jnp.bfloat16)
    return high, low


def dot(x, y, over=(1, 0)):
    return lax.dot_general(x, y, (((over[0],), (over[1],)), ((), ())), preferred_element_type=jnp.float32)


def pack_kernel(
    signal_hbm, grad_hbm, filter_hbm, gain_hbm, table_hbm,
    out_ref, skip_ref, table_ref,
    signal_ref, grad_ref, filter_ref, gain_ref, sems,
):
    pairs = (
        (signal_hbm, signal_ref),
        (grad_hbm, grad_ref),
        (filter_hbm, filter_ref),
        (gain_hbm, gain_ref),
        (table_hbm, table_ref),
    )
    copies = [pltpu.make_async_copy(source, target, sems.at[k]) for k, (source, target) in enumerate(pairs)]
    for copy in copies:
        copy.start()
    channels = signal_ref.shape[0]
    arrays = []
    for number, ref in enumerate((signal_ref, grad_ref, filter_ref)):
        copies[number].wait()
        arrays.append(ref[...].astype(jnp.float32))
        for chunk in range(SUBLANES):
            lanes = slice(chunk * LANES, (chunk + 1) * LANES)
            out_ref[pl.ds(number * 8 + chunk, channels, stride=24), :] = arrays[number][:, lanes]
    copies[3].wait()
    row = lax.broadcasted_iota(jnp.int32, (channels, 1), 0)
    gains = jnp.zeros((channels, 1), jnp.float32)
    for channel in range(channels):
        gains = jnp.where(row == channel, gain_ref[channel], gains)
    skip_ref[0] = gains * arrays[0]
    skip_ref[1] = gains * arrays[1]
    copies[4].wait()


def convolve_kernel(in_ref, outer_ref_h, outer_ref_l, there, back, twist, out_ref, a_ref, u_h, u_l, *, scale):
    chips = out_ref.shape[0]
    half = chips * SUBLANES
    rows = 2 * half
    core = lax.axis_index("core")

    def sequence(number):
        return in_ref[:, number * 8 : number * 8 + 8, :].reshape(rows, LANES)

    both = jnp.concatenate([sequence(0), sequence(1)], axis=1).astype(jnp.bfloat16)
    taps_h, taps_l = split(sequence(2))
    outer_h, outer_l = outer_ref_h[...], outer_ref_l[...]
    a_ref[:, : 2 * LANES] = dot(outer_h, both) + dot(outer_l, both)
    turned = dot(outer_h, jnp.concatenate([taps_h, taps_l], axis=1))
    a_ref[:, 2 * LANES :] = turned[:, :LANES] + turned[:, LANES:] + dot(outer_l, taps_h)
    there_h, there_l = there[0], there[1]
    back_h, back_l = back[0], back[1]

    last = a_ref[rows : rows + 1, :]
    first_row = lax.broadcasted_iota(jnp.int32, (16, 1), 0) == 0

    for start, count in [(k, 64) for k in range(0, rows, 64)] + [(rows, 16)]:
        tr = twist[start : start + count, :LANES]
        ti = twist[start : start + count, LANES:]
        pieces = []
        for number in range(3):
            lanes = slice(number * LANES, (number + 1) * LANES)
            if start == rows:
                ar = jnp.where(first_row, last[:, lanes], 0.0)
                pieces.append(jnp.concatenate([ar * tr, ar * ti], axis=1))
                continue
            ar = a_ref[start : start + count, lanes]
            ai = a_ref[rows + start : rows + start + count, lanes]
            if start == 0:
                row = lax.broadcasted_iota(jnp.int32, (count, 1), 0)
                ai = jnp.where(row == 0, 0.0, ai)
            pieces.append(jnp.concatenate([ar * tr - ai * ti, ar * ti + ai * tr], axis=1))
        z_h, z_l = split(jnp.concatenate(pieces, axis=0))
        spec = dot(z_h, there_h) + dot(z_l, there_h) + dot(z_h, there_l)
        sr, si = spec[:count, :LANES], spec[:count, LANES:]
        gr, gi = spec[count : 2 * count, :LANES], spec[count : 2 * count, LANES:]
        hr, hi = spec[2 * count :, :LANES], spec[2 * count :, LANES:]
        conv = jnp.concatenate([sr * hr - si * hi, sr * hi + si * hr], axis=1)
        back = jnp.concatenate([gr * hr + gi * hi, gi * hr - gr * hi], axis=1)
        corr = jnp.concatenate([gr * sr + gi * si, gi * sr - gr * si], axis=1)
        p_h, p_l = split(jnp.concatenate([conv, back, corr], axis=0))
        v = dot(p_h, back_h) + dot(p_l, back_h) + dot(p_h, back_l)
        if start in (0, rows):
            weight = jnp.where(lax.broadcasted_iota(jnp.int32, (count, 1), 0) == 0, 0.5, 1.0)
            tr, ti = tr * weight, ti * weight
        for number in range(3):
            vr = v[number * count : (number + 1) * count, :LANES]
            vi = v[number * count : (number + 1) * count, LANES:]
            lanes = slice(number * LANES, (number + 1) * LANES)
            real_h, real_l = split(vr * tr + vi * ti)
            if start == rows:
                u_h[rows : rows + 16, lanes] = jnp.where(first_row, real_h, u_h[rows : rows + 16, lanes])
                u_l[rows : rows + 16, lanes] = jnp.where(first_row, real_l, u_l[rows : rows + 16, lanes])
                continue
            imag_h, imag_l = split(vi * tr - vr * ti)
            u_h[start : start + count, lanes] = real_h
            u_l[start : start + count, lanes] = real_l
            u_h[rows + start : rows + start + count, lanes] = imag_h
            u_l[rows + start : rows + start + count, lanes] = imag_l

    mine = pl.ds(pl.multiple_of(core * half, half), half)
    columns_h, columns_l = outer_ref_h[:, mine], outer_ref_l[:, mine]
    y = dot(columns_h, u_h[...], (0, 0)) + dot(columns_h, u_l[...], (0, 0)) + dot(columns_l, u_h[...], (0, 0))
    y *= scale
    for number in range(3):
        out_ref[:, number * 8 : number * 8 + 8, :] = y[:, number * LANES : (number + 1) * LANES].reshape(chips, SUBLANES, LANES)


def collect_kernel(in_ref, out_ref):
    mine = in_ref[:, 16:, :].reshape(out_ref.shape[1:])
    for place in range(out_ref.shape[0]):
        out_ref[place] = mine


def add_kernel(in_ref, out_ref):
    total = in_ref[0]
    for place in range(1, in_ref.shape[0]):
        total += in_ref[place]
    for place in range(out_ref.shape[0]):
        out_ref[place] = total


def finish_kernel(in_ref, skip_ref, shares_ref, out_ref, back_ref, corr_ref, total_ref):
    channels = corr_ref.shape[0]
    total = shares_ref[0]
    for place in range(1, shares_ref.shape[0]):
        total += shares_ref[place]
    total_ref[...] = total
    for chunk in range(SUBLANES):
        lanes = slice(chunk * LANES, (chunk + 1) * LANES)
        corr_ref[:, lanes] = total_ref[pl.ds(chunk, channels, stride=SUBLANES), :]
        for number, result in enumerate((out_ref, back_ref)):
            conv = in_ref[pl.ds(number * 8 + chunk, channels, stride=24), :]
            result[:, lanes] = (conv + skip_ref[number, :, lanes]).astype(jnp.bfloat16)


def call(kernel, out_shape, operands, scratch=(), spaces=None):
    if spaces is None:
        spaces = [pltpu.VMEM] * len(operands)
    return pl.pallas_call(
        kernel,
        out_shape=out_shape,
        in_specs=[pl.BlockSpec(memory_space=space) for space in spaces],
        out_specs=jax.tree.map(lambda _: pl.BlockSpec(memory_space=pltpu.VMEM), out_shape),
        scratch_shapes=list(scratch),
        compiler_params=pltpu.CompilerParams(vmem_limit_bytes=VMEM_BYTES),
    )(*operands)


def on_device(signal, filter_taps, skip_gain, grad_out):
    channels, tokens = signal.shape
    chips = lax.axis_size(CHIPS)
    ctx = 2 * chips
    assert channels == chips and tokens == SUBLANES * LANES
    length = tokens * ctx
    rows = length // LANES
    outer_h, outer_l, there, back, twist = make_tables(rows, ctx)

    in_hbm = [
        pltpu.with_memory_space_constraint(x, pltpu.HBM)
        for x in (signal, grad_out, filter_taps, skip_gain, there)
    ]
    packed, skip, there = call(
        pack_kernel,
        (
            pltpu.VMEM((chips * 24, LANES), jnp.float32),
            pltpu.VMEM((2, channels, tokens), jnp.float32),
            pltpu.VMEM(there.shape, there.dtype),
        ),
        in_hbm,
        scratch=(
            pltpu.VMEM(signal.shape, signal.dtype),
            pltpu.VMEM(grad_out.shape, grad_out.dtype),
            pltpu.VMEM(filter_taps.shape, filter_taps.dtype),
            pltpu.SMEM(skip_gain.shape, skip_gain.dtype),
            pltpu.SemaphoreType.DMA((5,)),
        ),
        spaces=[pltpu.HBM] * 5,
    )
    spread = lax.all_to_all(packed.reshape(chips, 24, LANES), CHIPS, 0, 0, tiled=True)
    sequences = lax.all_gather(spread, "core", tiled=True)
    results = call(
        functools.partial(convolve_kernel, scale=2.0 / (2 * length * math.sqrt(length))),
        jax.ShapeDtypeStruct((chips, 24, LANES), jnp.float32),
        (sequences, outer_h, outer_l, there, back, twist),
        scratch=(
            pltpu.VMEM((2 * rows, 3 * LANES), jnp.float32),
            pltpu.VMEM((2 * rows, 3 * LANES), jnp.bfloat16),
            pltpu.VMEM((2 * rows, 3 * LANES), jnp.bfloat16),
        ),
    )
    returned = lax.all_to_all(results, CHIPS, 0, 0, tiled=True)
    shape = (channels * SUBLANES, LANES)
    first, second = lax.axis_size(TP_FIRST), lax.axis_size(TP_SECOND)
    everyone = call(collect_kernel, jax.ShapeDtypeStruct((first, *shape), jnp.float32), (returned,))
    shares = lax.all_to_all(everyone, TP_FIRST, 0, 0, tiled=True)
    everyone = call(add_kernel, jax.ShapeDtypeStruct((second, *shape), jnp.float32), (shares,))
    shares = lax.all_to_all(everyone, TP_SECOND, 0, 0, tiled=True)
    output, grad_signal, grad_filter = call(
        finish_kernel,
        (
            jax.ShapeDtypeStruct((channels, tokens), jnp.bfloat16),
            jax.ShapeDtypeStruct((channels, tokens), jnp.bfloat16),
            jax.ShapeDtypeStruct((channels, tokens), jnp.float32),
        ),
        (returned.reshape(chips * 24, LANES), skip, shares),
        scratch=(pltpu.VMEM(shape, jnp.float32),),
    )
    return (output, grad_signal, grad_filter)


def solution(mesh):
    ctx, tp = mesh.shape["ctx"], mesh.shape["tp"]
    parted = Mesh(mesh.devices.reshape(2, ctx // 4, 2, 2, tp // 4, 2), (*CTX, *TP))
    in_specs = (P(TP, CTX), P(None, CTX), P(TP), P(TP, CTX))
    out_specs = (P(TP, CTX), P(TP, CTX), P(None, CTX))
    return jax.shard_map(
        on_device, mesh=parted, in_specs=in_specs, out_specs=out_specs, check_vma=False
    )
```

```python
import functools
import math

import jax
import jax.numpy as jnp
import ml_dtypes
import numpy as np
from jax import lax
from jax.experimental import pallas as pl
from jax.experimental.pallas import tpu as pltpu
from jax.sharding import Mesh
from jax.sharding import PartitionSpec as P

LANES = 128
SUBLANES = 8
CTX = ("chip", "core")
TP = ("tp_far", "tp_even", "tp_next")
TP_FIRST = ("tp_next", "tp_far")
TP_SECOND = ("tp_even",)
VMEM_BYTES = 24 * 1024 * 1024


def split_table(table):
    high = table.astype(np.float32).astype(ml_dtypes.bfloat16)
    low = (table - high.astype(np.float64)).astype(ml_dtypes.bfloat16)
    return high, low


def make_tables(rows, blocks):
    period = 2 * rows
    padded = period * LANES
    place = np.arange(rows)
    block = place // SUBLANES % (blocks // 2) * 2 + place // (rows // 2)
    a = block * SUBLANES + place % SUBLANES
    f1 = np.arange(rows)
    turn = 2.0 * np.pi * (np.outer(f1, a) % period) / period
    cosines = np.cos(turn)
    sines = -np.sin(turn)
    sines[0] = np.where(a % 2 == 0, 1.0, -1.0)
    outer = np.concatenate([cosines, sines], axis=0)
    b = np.arange(LANES)
    kept = np.arange(rows + 1)
    angle = 2.0 * np.pi * (np.outer(kept, b) % padded) / padded
    twist = np.zeros((rows + 16, 2 * LANES))
    twist[: rows + 1, :LANES] = np.cos(angle)
    twist[: rows + 1, LANES:] = -np.sin(angle)
    inner = 2.0 * np.pi * (np.outer(b, b) % LANES) / LANES
    c, s = np.cos(inner), np.sin(inner)
    inner_there = np.block([[c, -s], [s, c]])
    inner_back = inner_there.T
    return (
        *split_table(outer), np.stack(split_table(inner_there)), np.stack(split_table(inner_back)), twist.astype(np.float32)
    )


def split(x):
    high = x.astype(jnp.bfloat16)
    low = (x - high.astype(jnp.float32)).astype(jnp.bfloat16)
    return high, low


def dot(x, y, over=(1, 0)):
    return lax.dot_general(x, y, (((over[0],), (over[1],)), ((), ())), preferred_element_type=jnp.float32)


def pack_kernel(
    signal_hbm, grad_hbm, filter_hbm, gain_hbm, table_hbm,
    out_ref, skip_ref, table_ref,
    signal_ref, grad_ref, filter_ref, gain_ref, sems,
):
    pairs = (
        (signal_hbm, signal_ref),
        (grad_hbm, grad_ref),
        (filter_hbm, filter_ref),
        (gain_hbm, gain_ref),
        (table_hbm, table_ref),
    )
    copies = [pltpu.make_async_copy(source, target, sems.at[k]) for k, (source, target) in enumerate(pairs)]
    for copy in copies:
        copy.start()
    channels = signal_ref.shape[0]
    arrays = []
    for number, ref in enumerate((signal_ref, grad_ref, filter_ref)):
        copies[number].wait()
        arrays.append(ref[...].astype(jnp.float32))
        for chunk in range(SUBLANES):
            lanes = slice(chunk * LANES, (chunk + 1) * LANES)
            out_ref[pl.ds(number * 8 + chunk, channels, stride=24), :] = arrays[number][:, lanes]
    copies[3].wait()
    row = lax.broadcasted_iota(jnp.int32, (channels, 1), 0)
    gains = jnp.zeros((channels, 1), jnp.float32)
    for channel in range(channels):
        gains = jnp.where(row == channel, gain_ref[channel], gains)
    skip_ref[0] = gains * arrays[0]
    skip_ref[1] = gains * arrays[1]
    copies[4].wait()


def convolve_kernel(in_ref, outer_ref_h, outer_ref_l, there, back, twist, out_ref, a_ref, u_h, u_l, *, scale):
    chips = out_ref.shape[0]
    half = chips * SUBLANES
    rows = 2 * half
    core = lax.axis_index("core")

    def sequence(number):
        return in_ref[:, number * 8 : number * 8 + 8, :].reshape(rows, LANES)

    both = jnp.concatenate([sequence(0), sequence(1)], axis=1).astype(jnp.bfloat16)
    taps_h, taps_l = split(sequence(2))
    outer_h, outer_l = outer_ref_h[...], outer_ref_l[...]
    a_ref[:, : 2 * LANES] = dot(outer_h, both) + dot(outer_l, both)
    turned = dot(outer_h, jnp.concatenate([taps_h, taps_l], axis=1))
    a_ref[:, 2 * LANES :] = turned[:, :LANES] + turned[:, LANES:] + dot(outer_l, taps_h)
    there_h, there_l = there[0], there[1]
    back_h, back_l = back[0], back[1]

    last = a_ref[rows : rows + 1, :]
    first_row = lax.broadcasted_iota(jnp.int32, (16, 1), 0) == 0

    for start, count in [(k, 64) for k in range(0, rows, 64)] + [(rows, 16)]:
        tr = twist[start : start + count, :LANES]
        ti = twist[start : start + count, LANES:]
        pieces = []
        for number in range(3):
            lanes = slice(number * LANES, (number + 1) * LANES)
            if start == rows:
                ar = jnp.where(first_row, last[:, lanes], 0.0)
                pieces.append(jnp.concatenate([ar * tr, ar * ti], axis=1))
                continue
            ar = a_ref[start : start + count, lanes]
            ai = a_ref[rows + start : rows + start + count, lanes]
            if start == 0:
                row = lax.broadcasted_iota(jnp.int32, (count, 1), 0)
                ai = jnp.where(row == 0, 0.0, ai)
            pieces.append(jnp.concatenate([ar * tr - ai * ti, ar * ti + ai * tr], axis=1))
        z_h, z_l = split(jnp.concatenate(pieces, axis=0))
        spec = dot(z_h, there_h) + dot(z_l, there_h) + dot(z_h, there_l)
        sr, si = spec[:count, :LANES], spec[:count, LANES:]
        gr, gi = spec[count : 2 * count, :LANES], spec[count : 2 * count, LANES:]
        hr, hi = spec[2 * count :, :LANES], spec[2 * count :, LANES:]
        conv = jnp.concatenate([sr * hr - si * hi, sr * hi + si * hr], axis=1)
        back = jnp.concatenate([gr * hr + gi * hi, gi * hr - gr * hi], axis=1)
        corr = jnp.concatenate([gr * sr + gi * si, gi * sr - gr * si], axis=1)
        p_h, p_l = split(jnp.concatenate([conv, back, corr], axis=0))
        v = dot(p_h, back_h) + dot(p_l, back_h) + dot(p_h, back_l)
        if start in (0, rows):
            weight = jnp.where(lax.broadcasted_iota(jnp.int32, (count, 1), 0) == 0, 0.5, 1.0)
            tr, ti = tr * weight, ti * weight
        for number in range(3):
            vr = v[number * count : (number + 1) * count, :LANES]
            vi = v[number * count : (number + 1) * count, LANES:]
            lanes = slice(number * LANES, (number + 1) * LANES)
            real_h, real_l = split(vr * tr + vi * ti)
            if start == rows:
                u_h[rows : rows + 16, lanes] = jnp.where(first_row, real_h, u_h[rows : rows + 16, lanes])
                u_l[rows : rows + 16, lanes] = jnp.where(first_row, real_l, u_l[rows : rows + 16, lanes])
                continue
            imag_h, imag_l = split(vi * tr - vr * ti)
            u_h[start : start + count, lanes] = real_h
            u_l[start : start + count, lanes] = real_l
            u_h[rows + start : rows + start + count, lanes] = imag_h
            u_l[rows + start : rows + start + count, lanes] = imag_l

    mine = pl.ds(pl.multiple_of(core * half, half), half)
    columns_h, columns_l = outer_ref_h[:, mine], outer_ref_l[:, mine]
    y = dot(columns_h, u_h[...], (0, 0)) + dot(columns_h, u_l[...], (0, 0)) + dot(columns_l, u_h[...], (0, 0))
    y *= scale
    for number in range(3):
        out_ref[:, number * 8 : number * 8 + 8, :] = y[:, number * LANES : (number + 1) * LANES].reshape(chips, SUBLANES, LANES)


def collect_kernel(in_ref, out_ref):
    mine = in_ref[:, 16:, :].reshape(out_ref.shape[1:])
    for place in range(out_ref.shape[0]):
        out_ref[place] = mine


def add_kernel(in_ref, out_ref):
    total = in_ref[0]
    for place in range(1, in_ref.shape[0]):
        total += in_ref[place]
    for place in range(out_ref.shape[0]):
        out_ref[place] = total


def finish_kernel(in_ref, skip_ref, shares_ref, out_ref, back_ref, corr_ref, total_ref):
    channels = corr_ref.shape[0]
    total = shares_ref[0]
    for place in range(1, shares_ref.shape[0]):
        total += shares_ref[place]
    total_ref[...] = total
    for chunk in range(SUBLANES):
        lanes = slice(chunk * LANES, (chunk + 1) * LANES)
        corr_ref[:, lanes] = total_ref[pl.ds(chunk, channels, stride=SUBLANES), :]
        for number, result in enumerate((out_ref, back_ref)):
            conv = in_ref[pl.ds(number * 8 + chunk, channels, stride=24), :]
            result[:, lanes] = (conv + skip_ref[number, :, lanes]).astype(jnp.bfloat16)


def call(kernel, out_shape, operands, scratch=(), spaces=None):
    if spaces is None:
        spaces = [pltpu.VMEM] * len(operands)
    return pl.pallas_call(
        kernel,
        out_shape=out_shape,
        in_specs=[pl.BlockSpec(memory_space=space) for space in spaces],
        out_specs=jax.tree.map(lambda _: pl.BlockSpec(memory_space=pltpu.VMEM), out_shape),
        scratch_shapes=list(scratch),
        compiler_params=pltpu.CompilerParams(vmem_limit_bytes=VMEM_BYTES),
    )(*operands)


def on_device(signal, filter_taps, skip_gain, grad_out):
    channels, tokens = signal.shape
    chips = lax.axis_size("chip")
    ctx = 2 * chips
    assert channels == chips and tokens == SUBLANES * LANES
    length = tokens * ctx
    rows = length // LANES
    outer_h, outer_l, there, back, twist = make_tables(rows, ctx)

    in_hbm = [
        pltpu.with_memory_space_constraint(x, pltpu.HBM)
        for x in (signal, grad_out, filter_taps, skip_gain, there)
    ]
    packed, skip, there = call(
        pack_kernel,
        (
            pltpu.VMEM((chips * 24, LANES), jnp.float32),
            pltpu.VMEM((2, channels, tokens), jnp.float32),
            pltpu.VMEM(there.shape, there.dtype),
        ),
        in_hbm,
        scratch=(
            pltpu.VMEM(signal.shape, signal.dtype),
            pltpu.VMEM(grad_out.shape, grad_out.dtype),
            pltpu.VMEM(filter_taps.shape, filter_taps.dtype),
            pltpu.SMEM(skip_gain.shape, skip_gain.dtype),
            pltpu.SemaphoreType.DMA((5,)),
        ),
        spaces=[pltpu.HBM] * 5,
    )
    spread = lax.all_to_all(packed.reshape(chips, 24, LANES), "chip", 0, 0, tiled=True)
    sequences = lax.all_gather(spread, "core", tiled=True)
    results = call(
        functools.partial(convolve_kernel, scale=2.0 / (2 * length * math.sqrt(length))),
        jax.ShapeDtypeStruct((chips, 24, LANES), jnp.float32),
        (sequences, outer_h, outer_l, there, back, twist),
        scratch=(
            pltpu.VMEM((2 * rows, 3 * LANES), jnp.float32),
            pltpu.VMEM((2 * rows, 3 * LANES), jnp.bfloat16),
            pltpu.VMEM((2 * rows, 3 * LANES), jnp.bfloat16),
        ),
    )
    returned = lax.all_to_all(results, "chip", 0, 0, tiled=True)
    shape = (channels * SUBLANES, LANES)
    first, second = lax.axis_size(TP_FIRST), lax.axis_size(TP_SECOND)
    everyone = call(collect_kernel, jax.ShapeDtypeStruct((first, *shape), jnp.float32), (returned,))
    shares = lax.all_to_all(everyone, TP_FIRST, 0, 0, tiled=True)
    everyone = call(add_kernel, jax.ShapeDtypeStruct((second, *shape), jnp.float32), (shares,))
    shares = lax.all_to_all(everyone, TP_SECOND, 0, 0, tiled=True)
    output, grad_signal, grad_filter = call(
        finish_kernel,
        (
            jax.ShapeDtypeStruct((channels, tokens), jnp.bfloat16),
            jax.ShapeDtypeStruct((channels, tokens), jnp.bfloat16),
            jax.ShapeDtypeStruct((channels, tokens), jnp.float32),
        ),
        (returned.reshape(chips * 24, LANES), skip, shares),
        scratch=(pltpu.VMEM(shape, jnp.float32),),
    )
    return (output, grad_signal, grad_filter)


def solution(mesh):
    ctx, tp = mesh.shape["ctx"], mesh.shape["tp"]
    parted = Mesh(mesh.devices.reshape(ctx // 2, 2, 2, tp // 4, 2), (*CTX, *TP))
    in_specs = (P(TP, CTX), P(None, CTX), P(TP), P(TP, CTX))
    out_specs = (P(TP, CTX), P(TP, CTX), P(None, CTX))
    return jax.shard_map(
        on_device, mesh=parted, in_specs=in_specs, out_specs=out_specs, check_vma=False
    )
```

```python
import functools
import math

import jax
import jax.numpy as jnp
import ml_dtypes
import numpy as np
from jax import lax
from jax.experimental import pallas as pl
from jax.experimental.pallas import tpu as pltpu
from jax.sharding import Mesh
from jax.sharding import PartitionSpec as P

LANES = 128
SUBLANES = 8
CTX = ("chip", "core")
TP = ("tp_far", "tp_half", "tp_two", "tp_next")
TP_FIRST = ("tp_next", "tp_far")
TP_SECOND = ("tp_two", "tp_half")
VMEM_BYTES = 24 * 1024 * 1024


def split_table(table):
    high = table.astype(np.float32).astype(ml_dtypes.bfloat16)
    low = (table - high.astype(np.float64)).astype(ml_dtypes.bfloat16)
    return high, low


def make_tables(rows, blocks):
    period = 2 * rows
    padded = period * LANES
    place = np.arange(rows)
    block = place // SUBLANES % (blocks // 2) * 2 + place // (rows // 2)
    a = block * SUBLANES + place % SUBLANES
    f1 = np.arange(rows)
    turn = 2.0 * np.pi * (np.outer(f1, a) % period) / period
    cosines = np.cos(turn)
    sines = -np.sin(turn)
    sines[0] = np.where(a % 2 == 0, 1.0, -1.0)
    outer = np.concatenate([cosines, sines], axis=0)
    b = np.arange(LANES)
    kept = np.arange(rows + 1)
    angle = 2.0 * np.pi * (np.outer(kept, b) % padded) / padded
    twist = np.zeros((rows + 16, 2 * LANES))
    twist[: rows + 1, :LANES] = np.cos(angle)
    twist[: rows + 1, LANES:] = -np.sin(angle)
    inner = 2.0 * np.pi * (np.outer(b, b) % LANES) / LANES
    c, s = np.cos(inner), np.sin(inner)
    inner_there = np.block([[c, -s], [s, c]])
    inner_back = inner_there.T
    return (
        *split_table(outer), np.stack(split_table(inner_there)), np.stack(split_table(inner_back)), twist.astype(np.float32)
    )


def split(x):
    high = x.astype(jnp.bfloat16)
    low = (x - high.astype(jnp.float32)).astype(jnp.bfloat16)
    return high, low


def dot(x, y, over=(1, 0)):
    return lax.dot_general(x, y, (((over[0],), (over[1],)), ((), ())), preferred_element_type=jnp.float32)


def pack_kernel(
    signal_hbm, grad_hbm, filter_hbm, gain_hbm, table_hbm,
    out_ref, skip_ref, table_ref,
    signal_ref, grad_ref, filter_ref, gain_ref, sems,
):
    pairs = (
        (signal_hbm, signal_ref),
        (grad_hbm, grad_ref),
        (filter_hbm, filter_ref),
        (gain_hbm, gain_ref),
        (table_hbm, table_ref),
    )
    copies = [pltpu.make_async_copy(source, target, sems.at[k]) for k, (source, target) in enumerate(pairs)]
    for copy in copies:
        copy.start()
    channels = signal_ref.shape[0]
    arrays = []
    for number, ref in enumerate((signal_ref, grad_ref, filter_ref)):
        copies[number].wait()
        arrays.append(ref[...].astype(jnp.float32))
        for chunk in range(SUBLANES):
            lanes = slice(chunk * LANES, (chunk + 1) * LANES)
            out_ref[pl.ds(number * 8 + chunk, channels, stride=24), :] = arrays[number][:, lanes]
    copies[3].wait()
    row = lax.broadcasted_iota(jnp.int32, (channels, 1), 0)
    gains = jnp.zeros((channels, 1), jnp.float32)
    for channel in range(channels):
        gains = jnp.where(row == channel, gain_ref[channel], gains)
    skip_ref[0] = gains * arrays[0]
    skip_ref[1] = gains * arrays[1]
    copies[4].wait()


def convolve_kernel(in_ref, outer_ref_h, outer_ref_l, there, back, twist, out_ref, a_ref, u_h, u_l, *, scale):
    chips = out_ref.shape[0]
    half = chips * SUBLANES
    rows = 2 * half
    core = lax.axis_index("core")

    def sequence(number):
        return in_ref[:, number * 8 : number * 8 + 8, :].reshape(rows, LANES)

    both = jnp.concatenate([sequence(0), sequence(1)], axis=1).astype(jnp.bfloat16)
    taps_h, taps_l = split(sequence(2))
    outer_h, outer_l = outer_ref_h[...], outer_ref_l[...]
    a_ref[:, : 2 * LANES] = dot(outer_h, both) + dot(outer_l, both)
    turned = dot(outer_h, jnp.concatenate([taps_h, taps_l], axis=1))
    a_ref[:, 2 * LANES :] = turned[:, :LANES] + turned[:, LANES:] + dot(outer_l, taps_h)
    there_h, there_l = there[0], there[1]
    back_h, back_l = back[0], back[1]

    last = a_ref[rows : rows + 1, :]
    first_row = lax.broadcasted_iota(jnp.int32, (16, 1), 0) == 0

    for start, count in [(k, 64) for k in range(0, rows, 64)] + [(rows, 16)]:
        tr = twist[start : start + count, :LANES]
        ti = twist[start : start + count, LANES:]
        pieces = []
        for number in range(3):
            lanes = slice(number * LANES, (number + 1) * LANES)
            if start == rows:
                ar = jnp.where(first_row, last[:, lanes], 0.0)
                pieces.append(jnp.concatenate([ar * tr, ar * ti], axis=1))
                continue
            ar = a_ref[start : start + count, lanes]
            ai = a_ref[rows + start : rows + start + count, lanes]
            if start == 0:
                row = lax.broadcasted_iota(jnp.int32, (count, 1), 0)
                ai = jnp.where(row == 0, 0.0, ai)
            pieces.append(jnp.concatenate([ar * tr - ai * ti, ar * ti + ai * tr], axis=1))
        z_h, z_l = split(jnp.concatenate(pieces, axis=0))
        spec = dot(z_h, there_h) + dot(z_l, there_h) + dot(z_h, there_l)
        sr, si = spec[:count, :LANES], spec[:count, LANES:]
        gr, gi = spec[count : 2 * count, :LANES], spec[count : 2 * count, LANES:]
        hr, hi = spec[2 * count :, :LANES], spec[2 * count :, LANES:]
        conv = jnp.concatenate([sr * hr - si * hi, sr * hi + si * hr], axis=1)
        back = jnp.concatenate([gr * hr + gi * hi, gi * hr - gr * hi], axis=1)
        corr = jnp.concatenate([gr * sr + gi * si, gi * sr - gr * si], axis=1)
        p_h, p_l = split(jnp.concatenate([conv, back, corr], axis=0))
        v = dot(p_h, back_h) + dot(p_l, back_h) + dot(p_h, back_l)
        if start in (0, rows):
            weight = jnp.where(lax.broadcasted_iota(jnp.int32, (count, 1), 0) == 0, 0.5, 1.0)
            tr, ti = tr * weight, ti * weight
        for number in range(3):
            vr = v[number * count : (number + 1) * count, :LANES]
            vi = v[number * count : (number + 1) * count, LANES:]
            lanes = slice(number * LANES, (number + 1) * LANES)
            real_h, real_l = split(vr * tr + vi * ti)
            if start == rows:
                u_h[rows : rows + 16, lanes] = jnp.where(first_row, real_h, u_h[rows : rows + 16, lanes])
                u_l[rows : rows + 16, lanes] = jnp.where(first_row, real_l, u_l[rows : rows + 16, lanes])
                continue
            imag_h, imag_l = split(vi * tr - vr * ti)
            u_h[start : start + count, lanes] = real_h
            u_l[start : start + count, lanes] = real_l
            u_h[rows + start : rows + start + count, lanes] = imag_h
            u_l[rows + start : rows + start + count, lanes] = imag_l

    mine = pl.ds(pl.multiple_of(core * half, half), half)
    columns_h, columns_l = outer_ref_h[:, mine], outer_ref_l[:, mine]
    y = dot(columns_h, u_h[...], (0, 0)) + dot(columns_h, u_l[...], (0, 0)) + dot(columns_l, u_h[...], (0, 0))
    y *= scale
    for number in range(3):
        out_ref[:, number * 8 : number * 8 + 8, :] = y[:, number * LANES : (number + 1) * LANES].reshape(chips, SUBLANES, LANES)


def collect_kernel(in_ref, out_ref):
    mine = in_ref[:, 16:, :].reshape(out_ref.shape[1:])
    for place in range(out_ref.shape[0]):
        out_ref[place] = mine


def add_kernel(in_ref, out_ref):
    total = in_ref[0]
    for place in range(1, in_ref.shape[0]):
        total += in_ref[place]
    for place in range(out_ref.shape[0]):
        out_ref[place] = total


def finish_kernel(in_ref, skip_ref, shares_ref, out_ref, back_ref, corr_ref, total_ref):
    channels = corr_ref.shape[0]
    total = shares_ref[0]
    for place in range(1, shares_ref.shape[0]):
        total += shares_ref[place]
    total_ref[...] = total
    for chunk in range(SUBLANES):
        lanes = slice(chunk * LANES, (chunk + 1) * LANES)
        corr_ref[:, lanes] = total_ref[pl.ds(chunk, channels, stride=SUBLANES), :]
        for number, result in enumerate((out_ref, back_ref)):
            conv = in_ref[pl.ds(number * 8 + chunk, channels, stride=24), :]
            result[:, lanes] = (conv + skip_ref[number, :, lanes]).astype(jnp.bfloat16)


def call(kernel, out_shape, operands, scratch=(), spaces=None):
    if spaces is None:
        spaces = [pltpu.VMEM] * len(operands)
    return pl.pallas_call(
        kernel,
        out_shape=out_shape,
        in_specs=[pl.BlockSpec(memory_space=space) for space in spaces],
        out_specs=jax.tree.map(lambda _: pl.BlockSpec(memory_space=pltpu.VMEM), out_shape),
        scratch_shapes=list(scratch),
        compiler_params=pltpu.CompilerParams(vmem_limit_bytes=VMEM_BYTES),
    )(*operands)


def on_device(signal, filter_taps, skip_gain, grad_out):
    channels, tokens = signal.shape
    chips = lax.axis_size("chip")
    ctx = 2 * chips
    assert channels == chips and tokens == SUBLANES * LANES
    length = tokens * ctx
    rows = length // LANES
    outer_h, outer_l, there, back, twist = make_tables(rows, ctx)

    in_hbm = [
        pltpu.with_memory_space_constraint(x, pltpu.HBM)
        for x in (signal, grad_out, filter_taps, skip_gain, there)
    ]
    packed, skip, there = call(
        pack_kernel,
        (
            pltpu.VMEM((chips * 24, LANES), jnp.float32),
            pltpu.VMEM((2, channels, tokens), jnp.float32),
            pltpu.VMEM(there.shape, there.dtype),
        ),
        in_hbm,
        scratch=(
            pltpu.VMEM(signal.shape, signal.dtype),
            pltpu.VMEM(grad_out.shape, grad_out.dtype),
            pltpu.VMEM(filter_taps.shape, filter_taps.dtype),
            pltpu.SMEM(skip_gain.shape, skip_gain.dtype),
            pltpu.SemaphoreType.DMA((5,)),
        ),
        spaces=[pltpu.HBM] * 5,
    )
    spread = lax.all_to_all(packed.reshape(chips, 24, LANES), "chip", 0, 0, tiled=True)
    sequences = lax.all_gather(spread, "core", tiled=True)
    results = call(
        functools.partial(convolve_kernel, scale=2.0 / (2 * length * math.sqrt(length))),
        jax.ShapeDtypeStruct((chips, 24, LANES), jnp.float32),
        (sequences, outer_h, outer_l, there, back, twist),
        scratch=(
            pltpu.VMEM((2 * rows, 3 * LANES), jnp.float32),
            pltpu.VMEM((2 * rows, 3 * LANES), jnp.bfloat16),
            pltpu.VMEM((2 * rows, 3 * LANES), jnp.bfloat16),
        ),
    )
    returned = lax.all_to_all(results, "chip", 0, 0, tiled=True)
    shape = (channels * SUBLANES, LANES)
    first, second = lax.axis_size(TP_FIRST), lax.axis_size(TP_SECOND)
    everyone = call(collect_kernel, jax.ShapeDtypeStruct((first, *shape), jnp.float32), (returned,))
    shares = lax.all_to_all(everyone, TP_FIRST, 0, 0, tiled=True)
    everyone = call(add_kernel, jax.ShapeDtypeStruct((second, *shape), jnp.float32), (shares,))
    shares = lax.all_to_all(everyone, TP_SECOND, 0, 0, tiled=True)
    output, grad_signal, grad_filter = call(
        finish_kernel,
        (
            jax.ShapeDtypeStruct((channels, tokens), jnp.bfloat16),
            jax.ShapeDtypeStruct((channels, tokens), jnp.bfloat16),
            jax.ShapeDtypeStruct((channels, tokens), jnp.float32),
        ),
        (returned.reshape(chips * 24, LANES), skip, shares),
        scratch=(pltpu.VMEM(shape, jnp.float32),),
    )
    return (output, grad_signal, grad_filter)


def solution(mesh):
    ctx, tp = mesh.shape["ctx"], mesh.shape["tp"]
    parted = Mesh(mesh.devices.reshape(ctx // 2, 2, 2, tp // 8, 2, 2), (*CTX, *TP))
    in_specs = (P(TP, CTX), P(None, CTX), P(TP), P(TP, CTX))
    out_specs = (P(TP, CTX), P(TP, CTX), P(None, CTX))
    return jax.shard_map(
        on_device, mesh=parted, in_specs=in_specs, out_specs=out_specs, check_vma=False
    )
```
